128 devices in a mesh: gx: 8 (over z_lo, x), gy: 16 (over y, z_hi, core).
Axes of the slice: x: 4, y: 4, z: 4 (z_hi: 2, z_lo: 2; z = z_hi * 2 + z_lo), core: 2. Of those that a mesh axis runs over, the one named last changes fastest.
Arguments:
- state: float32 [3, 64, 128, 2048], P(None, None, 'gx', 'gy'), may hold values from -6 to 6
- parent: float32 [3, 64, 48, 544], P(None, None, 'gx', 'gy'), may hold values from -6 to 6
- stiffness: float32 [64], replicated, may hold values from 0.5 to 1.5
- offsets: int32 [4], replicated, may hold values from -1 to 29, as said below
Outputs:
- advanced: float32 [3, 64, 128, 2048], P(None, None, 'gx', 'gy')
The draws below stay inside these ranges and needn't reach their ends.
Inputs may be any that keep to these rules, and one draw needn't show every extreme that they name: offsets = (ox, oy, sx, sy): ox from 2 to 13, oy equal to 29, sx and sy each -1 or 1 with sy = -sx.
All inputs are finite; a program needn't handle non-finite values.
Results may differ from the reference program's by a relative error of at most 0.00016.
Values sent between devices are 32-bit elements; how exact they have to be, the bound alone decides.
A program may use at most 128 MiB of HBM per device.

```python
import math
import jax
import jax.numpy as jnp
from jax import lax

NZ = 64
SUBSTEPS = 4
NX = 128
NY = 2048
PX = 48
PY = 544


def draw_offsets(key, part):
    key = jax.random.fold_in(key, 7)
    first, second = jax.random.split(key, 2)
    limit_x = PX - NX // 4 - 3
    limit_y = PY - NY // 4 - 3
    anchor_x = jax.random.randint(first, (), 2, limit_x + 1)
    anchor_y = jnp.full((), limit_y, jnp.int32)
    move_x = 2 * jax.random.randint(second, (), 0, 2) - 1
    move_y = -move_x
    return jnp.stack([anchor_x, anchor_y, move_x, move_y]).astype(jnp.int32)


def levels(own_key, extent, shards, low, largest):
    def one(dim, parts):
        steps = jax.random.uniform(jax.random.fold_in(jax.random.fold_in(own_key, 6), dim), (parts,), jnp.float32, low / len(shards), largest / len(shards))
        return jnp.repeat(jnp.exp(steps), extent[dim] // parts).reshape((-1,) + (1,) * (len(extent) - dim - 1))

    loudness = one(*shards[0])
    for cut in shards[1:]:
        loudness = loudness * one(*cut)
    return loudness


def bell_draw(key, shape, spread, reach, cuts=(), held_as=jnp.bfloat16):
    entries = jax.random.normal(key, shape, jnp.float32) * spread
    if len(cuts) > 0:
        entries = levels(key, shape, cuts, -0.22, 0.18) * entries
    return jnp.clip(entries, min=-reach, max=reach).astype(held_as)


def setup_inputs(seed: int = 0) -> dict:
    keys = jax.random.split(jax.random.key(seed), 5)
    state = bell_draw(keys[0], (3, NZ, NX, NY), 1.0, 6.0, ((2, 8), (3, 16)), jnp.float32)
    parent = bell_draw(keys[1], (3, NZ, PX, PY), 1.0, 6.0, ((2, 8), (3, 16)), jnp.float32)
    stiffness = jnp.clip(jnp.exp(jax.random.uniform(keys[2], (NZ,), jnp.float32, math.log(0.5), math.log(1.5))), 0.5, 1.5)
    offsets = draw_offsets(jax.random.fold_in(keys[4], 71), 0)
    return {"state": state, "parent": parent, "stiffness": stiffness, "offsets": offsets}


courant = 0.5


def weights(index, anchor, count):
    base = 2 * index - 3
    lower = anchor + jnp.floor_divide(base, 8)
    frac = jnp.mod(base, 8).astype(jnp.float32) / 8.0
    cells = jnp.arange(count, dtype=jnp.int32)
    below = (cells[None, :] == lower[:, None]).astype(jnp.float32)
    above = (cells[None, :] == lower[:, None] + 1).astype(jnp.float32)
    return below * (1.0 - frac)[:, None] + above * frac[:, None]


def reference(state, parent, stiffness, offsets):
    ox = offsets[0]
    oy = offsets[1]
    sx = offsets[2]
    sy = offsets[3]
    padded = jnp.pad(state, ((0, 0), (0, 0), (4, 4), (4, 4)))
    zero = jnp.zeros((), jnp.int32)
    moved = lax.dynamic_slice(padded, (zero, zero, (4 + 4 * sx).astype(jnp.int32), (4 + 4 * sy).astype(jnp.int32)), state.shape)
    rows = jnp.arange(NX, dtype=jnp.int32)
    cols = jnp.arange(NY, dtype=jnp.int32)
    inside_rows = (rows + 4 * sx >= 0) & (rows + 4 * sx < NX)
    inside_cols = (cols + 4 * sy >= 0) & (cols + 4 * sy < NY)
    inside = inside_rows[:, None] & inside_cols[None, :]
    weight_x = weights(rows, ox + sx, PX)
    weight_y = weights(cols, oy + sy, PY)
    coarse = jnp.einsum("ir,czrs->czis", weight_x, parent, precision=lax.Precision.HIGHEST)
    fine = jnp.einsum("czis,js->czij", coarse, weight_y, precision=lax.Precision.HIGHEST)
    fields = jnp.where(inside, moved, fine)
    pressure = fields[0]
    wind_x = fields[1]
    wind_y = fields[2]
    speed = stiffness[:, None, None]
    for step in range(SUBSTEPS):
        padp = jnp.pad(pressure, ((0, 0), (1, 1), (1, 1)))
        wind_x = wind_x - courant * (padp[:, 2:, 1:-1] - padp[:, :-2, 1:-1])
        wind_y = wind_y - courant * (padp[:, 1:-1, 2:] - padp[:, 1:-1, :-2])
        padu = jnp.pad(wind_x, ((0, 0), (1, 1), (1, 1)))
        padv = jnp.pad(wind_y, ((0, 0), (1, 1), (1, 1)))
        pressure = pressure - courant * speed * ((padu[:, 2:, 1:-1] - padu[:, :-2, 1:-1]) + (padv[:, 1:-1, 2:] - padv[:, 1:-1, :-2]))
    return jnp.stack([pressure, wind_x, wind_y])
```

```python
import functools

import jax
import jax.numpy as jnp
from jax import lax
from jax.experimental import pallas as pl
from jax.experimental.pallas import tpu as pltpu
from jax.sharding import PartitionSpec as P

MESH = pl.DeviceIdType.MESH
F32 = jnp.float32
GX, GY = 8, 16
NZ, BX, BY = 64, 16, 128
CHUNKS = 2
ZC = NZ // CHUNKS
TILES = ZC // 8
PROWS, PCOLS = 6, 34
SLOTS = ((0.375, 0.625, 0.0), (0.125, 0.875, 0.0), (0.0, 0.875, 0.125), (0.0, 0.625, 0.375))


def roll(x, shift):
    shift = shift % 128
    return x if shift == 0 else pltpu.roll(x, shift, 1)


def iota(shape, dim):
    return lax.broadcasted_iota(jnp.int32, shape, dim)


def dot(a, b):
    return jnp.dot(a, b, precision=lax.Precision.HIGHEST, preferred_element_type=F32)


def bilinear(cell, lower, frac):
    return jnp.where(cell == lower, 1.0 - frac, 0.0) + jnp.where(cell == lower + 1, frac, 0.0)


class Copies:
    def __init__(self, send, recv):
        self.send, self.recv, self.count, self.started = send, recv, 0, []

    def slot(self):
        self.count += 1
        return self.count - 1

    def make(self, slot, src, dst, device, recv_slot=None):
        return pltpu.make_async_remote_copy(
            src_ref=src,
            dst_ref=dst,
            send_sem=self.send.at[slot],
            recv_sem=self.recv.at[slot if recv_slot is None else recv_slot],
            device_id=device,
            device_id_type=MESH,
        )

    def start(self, cond, slot, src, dst, device, recv_slot=None):
        @pl.when(cond)
        def _():
            self.make(slot, src, dst, device, recv_slot).start()

        self.started.append((cond, slot, src, dst, device, recv_slot))

    def arrive(self, cond, slot, ref, device):
        @pl.when(cond)
        def _():
            self.make(slot, ref, ref, device).wait_recv()

    def finish(self):
        for cond, slot, src, dst, device, recv_slot in self.started:

            @pl.when(cond)
            def _():
                self.make(slot, src, dst, device, recv_slot).wait_send()


def kernel(
    s,
    off_ref,
    stiff_ref,
    st_hbm,
    par_hbm,
    out_hbm,
    st,
    pin,
    pp3,
    sp,
    own,
    hx,
    yp,
    lp,
    cp,
    cr,
    qm,
    qe,
    pb,
    ub,
    vb,
    ok,
    lr,
    h0,
    outv,
    rsp,
    rsr,
    rsum,
    rnb,
    wr,
    fr,
    hfr,
    csm,
    csr,
    wc,
    in_sem,
    par_sem,
    out_sem,
    send_sem,
    recv_sem,
):
    gx, gy = lax.axis_index("gx"), lax.axis_index("gy")
    here = lambda dx, dy: {"gx": gx + dx, "gy": gy + dy}
    inside = lambda dx, dy: (gx + dx >= 0) & (gx + dx < GX) & (gy + dy >= 0) & (gy + dy < GY)
    ex = GX - 1 if s > 0 else 0
    ey = 0 if s > 0 else GY - 1
    at_x, at_y = gx == ex, gy == ey
    last = 13 if s > 0 else 14
    copies = Copies(send_sem, recv_sem)

    def lo(d):
        return (2 * d) // 3

    def feeds(src, dst):
        return (src >= lo(dst)) & (src <= lo(dst) + 3) & (dst >= 0) & (dst < GX) & (src >= 0) & (src < GX)

    partners = [(dx, dy, inside(dx, dy)) for dx, dy in ((-1, 0), (1, 0), (0, -1), (0, 1), (-1, 1), (1, -1))]
    partners.append((2 * s, 0, gx == ex - 2 * s))
    partners.append((-2 * s, 0, at_x))
    for d in (-3, -2, 2, 3):
        partners.append((d, 0, at_y & (feeds(gx, gx + d) | feeds(gx + d, gx))))
    barrier = pltpu.get_barrier_semaphore()
    for dx, dy, cond in partners:

        @pl.when(cond)
        def _():
            pl.semaphore_signal(barrier, inc=1, device_id=here(dx, dy), device_id_type=MESH)

    def chunk_rows(f, c):
        return pl.ds(f * NZ * BX + c * ZC * BX, ZC * BX)

    def load(c, f):
        return pltpu.make_async_copy(st_hbm.at[chunk_rows(f, c)], st.at[chunk_rows(f, c)], in_sem.at[c, f])

    par_copy = pltpu.make_async_copy(par_hbm, pin, par_sem)
    par_copy.start()
    for c in range(CHUNKS):
        for f in range(3):
            load(c, f).start()

    lane = iota((8, 128), 1)
    group, e = lane >> 3, lane & 7
    lane_c = iota((ZC, 128), 1)
    group_c, e_c = lane_c >> 3, lane_c & 7

    sub = iota((8, 128), 0)
    for t in range(NZ // 8):
        value = jnp.zeros((8, 128), F32)
        for q in range(8):
            value = jnp.where(sub == q, stiff_ref[8 * t + q], value)
        sp[pl.ds(8 * t, 8), :] = 0.5 * value

    for c in range(CHUNKS):
        for f in range(3):
            load(c, f).wait()
            pack = jnp.zeros((ZC, 128), F32)
            for x in range(BX):
                row = st[pl.ds(f * NZ * BX + c * ZC * BX + x, ZC, stride=BX), :]
                own[c, f, x] = row
                pack = jnp.where(group_c == x, roll(row, 8 * x + (8 if s > 0 else 0)), pack)
            yp[c, f] = pack
            for q in range(TILES // 2):
                first, second = pack[16 * q : 16 * q + 8], pack[16 * q + 8 : 16 * q + 16]
                turn = 0 if s > 0 else 48
                cp[c, f, q] = jnp.where(lane < 64, roll(first, turn), roll(second, turn + 64))

    par_copy.wait()
    use_rows = (gx >= 5) if s > 0 else (gx <= 2)

    @pl.when(use_rows | at_y)
    def _():
        def body(k, carry):
            pp3[pl.ds(16 * k, 16)] = jnp.zeros((16, 8, 128), F32)
            pp3[pl.ds(16 * k, 16), 0:PROWS, 0:PCOLS] = pin[pl.ds(16 * k, 16)]
            return carry

        lax.fori_loop(0, 3 * NZ // 16, body, 0)

    pp = pp3.reshape(3 * NZ * 8, 128)

    def parent_row(f, row, z, count):
        return pp[pl.ds((f * NZ + z) * 8 + row, count, stride=8), :]

    ox = off_ref[0]

    @pl.when(use_rows)
    def _():
        low = ox + 31 if s > 0 else ox - 2
        for k in range(3):
            for z in range(0, NZ, 16):
                total = jnp.zeros((16, 128), F32)
                for f in range(3):
                    part = jnp.zeros((16, 128), F32)
                    for row in range(PROWS):
                        weight = jnp.where(PROWS * gx + row == low + k, 1.0, 0.0)
                        part = part + weight * parent_row(f, row, z, 16)
                    total = total + roll(part, PCOLS * f)
                rsp[k, pl.ds(z, 16)] = total

    kk = iota((128, 128), 0)
    nn = iota((128, 128), 1)

    @pl.when(at_x)
    def _():
        base = 28 if s > 0 else 30
        other = jnp.where(gy <= last, gy + 1, gy - 1)

        def weights(block, f, j):
            lower = base + 32 * gy + ((2 * j - 3) >> 3)
            frac = ((2 * j - 3) & 7).astype(F32) * 0.125
            valid = (kk >= PCOLS * f) & (kk < PCOLS * f + PCOLS)
            return jnp.where(valid, bilinear(PCOLS * block + kk - PCOLS * f, lower, frac), 0.0)

        ne = nn & 7
        is_v = ne >= 4
        je = jnp.where(ne == 0, -2, jnp.where((ne == 1) | (ne == 4), -1, jnp.where(ne == 3, 129, 128)))
        fe = jnp.where(is_v, 2, 0)
        for b, block in enumerate((gy, other)):
            for f in range(3):
                wr[b, f] = weights(block, f, nn)
            wr[b, 3] = weights(block, fe, je)

    @pl.when(at_y)
    def _():
        first_col = 27 if s > 0 else 30
        for h in range(2):
            total = jnp.zeros((32, 128), F32)
            lane_h = iota((32, 128), 1)
            for row in range(PROWS):
                for f in range(3):
                    at = 9 * row + 3 * f + 64 * h
                    part = roll(parent_row(f, row, 32 * h, 32), at - first_col)
                    total = jnp.where((lane_h >= at) & (lane_h < at + 3), part, total)
            csm[pl.ds(0, 32), :] = total if h == 0 else csm[pl.ds(0, 32), :] + total

        krow = (kk * 57) >> 9
        krem = kk - 9 * krow
        kf = (krem >= 3).astype(jnp.int32) + (krem >= 6).astype(jnp.int32)
        ks = krem - 3 * kf
        ne = nn & 7
        col = (ne - 4) if s > 0 else ne
        wy = bilinear(ks, (2 * col + 5) >> 3, ((2 * col + 5) & 7).astype(F32) * 0.125)
        wy = jnp.where((col >= 0) & (col < 4) & (kk < 54), wy, 0.0)
        g = nn >> 3
        rows = (g, jnp.where(g < 2, g - 2, jnp.where(g < 4, g + 14, 0)))
        for k in range(4):
            for m in range(2):
                i = rows[m]
                lower = ox + s + 4 * gx + ((2 * i - 3) >> 3)
                wx = bilinear(PROWS * (lo(gx) + k) + krow, lower, ((2 * i - 3) & 7).astype(F32) * 0.125)
                for f in range(3):
                    wc[k, f, m] = jnp.where(kf == f, wx * wy, 0.0)

    for r in range(1, 4):
        for c in range(CHUNKS):

            @pl.when(gx == 0)
            def _():
                pb[r, c, 0:2] = jnp.zeros((2, ZC, 128), F32)
                ub[r, c, 0:1] = jnp.zeros((1, ZC, 128), F32)

            @pl.when(gx == GX - 1)
            def _():
                pb[r, c, 18:20] = jnp.zeros((2, ZC, 128), F32)
                ub[r, c, 17:18] = jnp.zeros((1, ZC, 128), F32)

            @pl.when(gy == 0)
            def _():
                lr[r, c, 0] = jnp.zeros((ZC, 128), F32)

            @pl.when(gy == GY - 1)
            def _():
                lr[r, c, 1] = jnp.zeros((ZC, 128), F32)

    pl.semaphore_wait(barrier, sum(cond.astype(jnp.int32) for _, _, cond in partners))

    cs_recv = [copies.slot() for _ in range(4)]
    for d in (-3, -2, -1, 1, 2, 3):
        slot = gx - lo(gx + d)
        copies.start(
            at_y & feeds(gx, gx + d), copies.slot(), csm, csr.at[slot], here(d, 0), recv_slot=cs_recv[0] + slot
        )
    rs_slots = [copies.slot(), copies.slot()]
    for k, far in enumerate((2, 1)):
        copies.start(gx == ex - far * s, rs_slots[k], rsp, rsr.at[k], here(far * s, 0))
    y_slots, c_slots, x_slots = [], [], []
    counts = (6, 5, 4)
    for c in range(CHUNKS):
        y_slots.append(copies.slot())
        copies.start(inside(0, s), y_slots[c], yp.at[c], lp.at[c], here(0, s))
        c_slots.append(copies.slot())
        copies.start(inside(-s, s), c_slots[c], cp.at[c], cr.at[c], here(-s, s))
        x_slots.append([copies.slot() for _ in range(3)])
        for f in range(3):
            n = counts[f]
            copies.start(
                inside(-s, 0),
                x_slots[c][f],
                own.at[c, f, pl.ds(0 if s > 0 else BX - n, n)],
                hx.at[c, f, pl.ds(0, n)],
                here(-s, 0),
            )

    nb_slots = [copies.slot(), copies.slot()]

    @pl.when(at_x)
    def _():
        for k, far in enumerate((2, 1)):
            copies.make(rs_slots[k], rsp, rsr.at[k], here(-far * s, 0)).wait_recv()
        for k in range(3):
            rsum[k] = rsp[k] + rsr[0, k] + rsr[1, k]

    copies.start(at_x & (gy >= 1) & (gy - 1 <= last), nb_slots[0], rsum, rnb, here(0, -1))
    copies.start(at_x & (gy + 1 > last) & (gy + 1 < GY), nb_slots[1], rsum, rnb, here(0, 1))

    @pl.when(at_y)
    def _():
        for k in range(4):
            src = lo(gx) + k

            @pl.when(src == gx)
            def _():
                csr[k] = csm[...]

            @pl.when(src != gx)
            def _():
                copies.make(cs_recv[k], csm, csr.at[k], here(src - gx, 0)).wait_recv()

        for f in range(3):
            for m, dest in enumerate((qm, qe)):
                for h in range(2):
                    total = jnp.zeros((32, 128), F32)
                    for k in range(4):
                        total = total + dot(roll(csr[k], 64 * h), wc[k, f, m])
                    for z in range(0, 32, min(ZC, 32)):
                        c, at = divmod(32 * h + z, ZC)
                        dest[c, f, pl.ds(at, min(ZC, 32))] = total[z : z + min(ZC, 32)]

    @pl.when(at_x)
    def _():
        @pl.when(gy <= last)
        def _():
            copies.make(nb_slots[0], rsum, rnb, here(0, 1)).wait_recv()

        @pl.when(gy > last)
        def _():
            copies.make(nb_slots[1], rsum, rnb, here(0, -1)).wait_recv()

        for c in range(CHUNKS):
            zr = pl.ds(c * ZC, ZC)
            for f in range(4):
                slots = [dot(rsum[k, zr], wr[0, f]) + dot(rnb[k, zr], wr[1, f]) for k in range(3)]
                strips = [sum(w * x for w, x in zip(SLOTS[r], slots) if w) for r in range(4)]
                if f < 3:
                    for r in range(4):
                        fr[c, f, r] = strips[r]
                else:
                    total = jnp.zeros((ZC, 128), F32)
                    for r in range(4):
                        total = jnp.where(group_c == (12 if s > 0 else 0) + r, strips[r], total)
                    hfr[c] = total

    left_e = (e == 0) | (e == 1) | (e == 4)
    right_e = (e == 2) | (e == 3) | (e == 5)
    beyond = ((gy == 0) & left_e) | ((gy == GY - 1) & right_e)
    edge = lane < 4 if s > 0 else lane >= 124

    def source(c, f, i):
        old = i + 4 * s
        if 0 <= old < BX:
            return own.at[c, f, old]
        return hx.at[c, f, old - BX if s > 0 else old + counts[f]]

    def assemble(c):
        copies.arrive(inside(0, -s), y_slots[c], lp.at[c], here(0, -s))
        copies.arrive(inside(s, -s), c_slots[c], cr.at[c], here(s, -s))
        for f in range(3):
            copies.arrive(inside(s, 0), x_slots[c][f], hx.at[c, f, pl.ds(0, counts[f])], here(s, 0))

        @pl.when(jnp.logical_not(at_y))
        def _():
            def body(q, carry):
                for f in range(3):
                    corner = cr[c, f, q]
                    for w in range(2):
                        zr = pl.ds(pl.multiple_of(16 * q + 8 * w, 8), 8)
                        side = lp[c, f, zr]
                        if s > 0:
                            qm[c, f, zr] = jnp.where(lane < 96, roll(side, -32), roll(corner, 96 - 64 * w))
                            qe[c, f, zr] = jnp.where(lane < 16, roll(side, -16), roll(corner, -16 - 64 * w))
                        else:
                            qm[c, f, zr] = jnp.where(lane < 32, roll(corner, -16 - 64 * w), roll(side, 32))
                            qe[c, f, zr] = jnp.where(lane < 16, roll(corner, -64 * w), roll(side, -80))
                return carry

            lax.fori_loop(0, TILES // 2, body, 0)

        def rows(t, carry):
            zr = pl.ds(pl.multiple_of(8 * t, 8), 8)
            for f, (dest, first, count) in enumerate(((pb, -2, 20), (ub, -1, 18), (vb, 0, 16))):
                main, extra = qm[c, f, zr], qe[c, f, zr]
                for n in range(count):
                    i = first + n
                    if 0 <= i < BX:
                        side = roll(main, -(8 * i + 4))
                    else:
                        side = roll(extra, -(8 * (i + 2 if i < 0 else i - 14) + 4))
                    dest[0, c, n, zr] = jnp.where(edge, side, roll(source(c, f, i)[zr], 4 * s))
            return carry

        lax.fori_loop(0, TILES, rows, 0)
        strip = 12 if s > 0 else 0

        @pl.when(at_x)
        def _():
            for r in range(4):
                pb[0, c, 2 + strip + r] = fr[c, 0, r]
                ub[0, c, 1 + strip + r] = fr[c, 1, r]
                vb[0, c, strip + r] = fr[c, 2, r]

        @pl.when(gx == 0)
        def _():
            pb[0, c, 0:2] = jnp.zeros((2, ZC, 128), F32)

        @pl.when(gx == GX - 1)
        def _():
            pb[0, c, 18:20] = jnp.zeros((2, ZC, 128), F32)

        ap, av = (-122, -119) if s > 0 else (-2, 1)

        def columns(t, carry):
            zr = pl.ds(pl.multiple_of(8 * t, 8), 8)
            mine = jnp.zeros((8, 128), F32)
            halo = jnp.zeros((8, 128), F32)
            for x in range(BX):
                mine = jnp.where(group == x, roll(pb[0, c, x + 2, zr], 8 * x + 2), mine)
                both = jnp.where(
                    e < 4, roll(source(c, 0, x)[zr], 8 * x + ap), roll(source(c, 2, x)[zr], 8 * x + av)
                )
                halo = jnp.where(group == x, both, halo)
            moved = jnp.where(e < 4, roll(qm[c, 0, zr], -2), roll(qm[c, 2, zr], 1))
            halo = jnp.where(left_e if s > 0 else right_e, moved, halo)
            ok[0, c, zr] = mine
            h0[c, zr] = halo
            return carry

        lax.fori_loop(0, TILES, columns, 0)

        @pl.when(at_x)
        def _():
            strip_rows = (group_c >= strip) & (group_c < strip + 4)
            h0[c] = jnp.where(strip_rows, hfr[c], h0[c])

    def substep(r, c):
        def body(t, carry):
            zr = pl.ds(pl.multiple_of(8 * t, 8), 8)
            halo = h0[c, zr] if r == 0 else jnp.where(left_e, lr[r, c, 0, zr], lr[r, c, 1, zr])
            halo = jnp.where(beyond, 0.0, halo)
            mine = ok[r, c, zr]
            slope = jnp.where(e == 4, roll(mine, 2) - roll(halo, 4), roll(halo, 2) - roll(mine, 4))
            wind = jnp.where(beyond, 0.0, halo - 0.5 * slope)
            side = jnp.where(
                e == 0, roll(halo, -2), jnp.where(e == 1, halo, jnp.where(e == 2, roll(wind, -3), roll(wind, -1)))
            )
            speed = sp[pl.ds(pl.multiple_of(c * ZC + 8 * t, 8), 8), :]
            p = [pb[r, c, n, zr] for n in range(20)]
            u = []
            for n in range(18):
                new = ub[r, c, n, zr] - 0.5 * (p[n + 2] - p[n])
                if n == 0:
                    new = jnp.where(gx == 0, 0.0, new)
                if n == 17:
                    new = jnp.where(gx == GX - 1, 0.0, new)
                u.append(new)
            pack = jnp.zeros((8, 128), F32)
            for x in range(BX):
                here_p = p[x + 2]
                side_p = roll(side, -(8 * x + 1))
                before = jnp.where(lane == 0, side_p, roll(here_p, 1))
                after = jnp.where(lane == 127, side_p, roll(here_p, -1))
                v = vb[r, c, x, zr] - 0.5 * (after - before)
                side_v = roll(side, -(8 * x + 3))
                before = jnp.where(lane == 0, side_v, roll(v, 1))
                after = jnp.where(lane == 127, side_v, roll(v, -1))
                new_p = here_p - speed * ((u[x + 2] - u[x]) + (after - before))
                if r < 3:
                    pb[r + 1, c, x + 2, zr] = new_p
                    ub[r + 1, c, x + 1, zr] = u[x + 1]
                    vb[r + 1, c, x, zr] = v
                    both = jnp.where(e < 4, roll(new_p, 8 * x + 2), roll(v, 8 * x + 5))
                    pack = jnp.where(group == x, both, pack)
                else:
                    for f, value in enumerate((new_p, u[x + 1], v)):
                        at = f * NZ * BX + (c * ZC + 8 * t) * BX + x
                        outv[pl.ds(at, 8, stride=BX), :] = value
            if r < 3:
                ok[r + 1, c, zr] = pack
            return carry

        lax.fori_loop(0, TILES, body, 0)

    slots = {}

    def send(r, c):
        slots[r, c] = [copies.slot() for _ in range(6)]
        k = slots[r, c]
        copies.start(inside(-1, 0), k[0], pb.at[r, c, pl.ds(2, 2)], pb.at[r, c, pl.ds(18, 2)], here(-1, 0))
        copies.start(inside(1, 0), k[1], pb.at[r, c, pl.ds(16, 2)], pb.at[r, c, pl.ds(0, 2)], here(1, 0))
        copies.start(inside(-1, 0), k[2], ub.at[r, c, pl.ds(1, 1)], ub.at[r, c, pl.ds(17, 1)], here(-1, 0))
        copies.start(inside(1, 0), k[3], ub.at[r, c, pl.ds(16, 1)], ub.at[r, c, pl.ds(0, 1)], here(1, 0))
        copies.start(inside(0, -1), k[4], ok.at[r, c], lr.at[r, c, 1], here(0, -1))
        copies.start(inside(0, 1), k[5], ok.at[r, c], lr.at[r, c, 0], here(0, 1))

    def receive(r, c):
        k = slots[r, c]
        copies.arrive(inside(1, 0), k[0], pb.at[r, c, pl.ds(18, 2)], here(1, 0))
        copies.arrive(inside(-1, 0), k[1], pb.at[r, c, pl.ds(0, 2)], here(-1, 0))
        copies.arrive(inside(1, 0), k[2], ub.at[r, c, pl.ds(17, 1)], here(1, 0))
        copies.arrive(inside(-1, 0), k[3], ub.at[r, c, pl.ds(0, 1)], here(-1, 0))
        copies.arrive(inside(0, 1), k[4], lr.at[r, c, 1], here(0, 1))
        copies.arrive(inside(0, -1), k[5], lr.at[r, c, 0], here(0, -1))

    def store(c, f):
        return pltpu.make_async_copy(outv.at[chunk_rows(f, c)], out_hbm.at[chunk_rows(f, c)], out_sem.at[c, f])

    for r in range(4):
        for c in range(CHUNKS):
            if r == 0:
                assemble(c)
            else:
                receive(r, c)
            substep(r, c)
            if r < 3:
                send(r + 1, c)
            else:
                for f in range(3):
                    store(c, f).start()
    copies.finish()
    for c in range(CHUNKS):
        for f in range(3):
            store(c, f).wait()


def move(s, state, parent, stiffness, offsets):
    vmem = lambda *shape: pltpu.VMEM(shape, F32)
    sems = 4 + 6 + 2 + CHUNKS * 5 + 2 + 3 * CHUNKS * 6
    scratch = [
        vmem(3 * NZ * BX, 128),
        vmem(3 * NZ, PROWS, PCOLS),
        vmem(3 * NZ, 8, 128),
        vmem(NZ, 128),
        vmem(CHUNKS, 3, BX, ZC, 128),
        vmem(CHUNKS, 3, 6, ZC, 128),
        vmem(CHUNKS, 3, ZC, 128),
        vmem(CHUNKS, 3, ZC, 128),
        vmem(CHUNKS, 3, TILES // 2, 8, 128),
        vmem(CHUNKS, 3, TILES // 2, 8, 128),
        vmem(CHUNKS, 3, ZC, 128),
        vmem(CHUNKS, 3, ZC, 128),
        vmem(4, CHUNKS, 20, ZC, 128),
        vmem(4, CHUNKS, 18, ZC, 128),
        vmem(4, CHUNKS, 16, ZC, 128),
        vmem(4, CHUNKS, ZC, 128),
        vmem(4, CHUNKS, 2, ZC, 128),
        vmem(CHUNKS, ZC, 128),
        vmem(3 * NZ * BX, 128),
        vmem(3, NZ, 128),
        vmem(2, 3, NZ, 128),
        vmem(3, NZ, 128),
        vmem(3, NZ, 128),
        vmem(2, 4, 128, 128),
        vmem(CHUNKS, 3, 4, ZC, 128),
        vmem(CHUNKS, ZC, 128),
        vmem(32, 128),
        vmem(4, 32, 128),
        vmem(4, 3, 2, 128, 128),
        pltpu.SemaphoreType.DMA((CHUNKS, 3)),
        pltpu.SemaphoreType.DMA,
        pltpu.SemaphoreType.DMA((CHUNKS, 3)),
        pltpu.SemaphoreType.DMA((sems,)),
        pltpu.SemaphoreType.DMA((sems,)),
    ]
    smem = pl.BlockSpec(memory_space=pltpu.SMEM)
    hbm = pl.BlockSpec(memory_space=pl.ANY)
    return pl.pallas_call(
        functools.partial(kernel, s),
        out_shape=jax.ShapeDtypeStruct((3 * NZ * BX, BY), F32),
        in_specs=[smem, smem, hbm, hbm],
        out_specs=hbm,
        scratch_shapes=scratch,
        compiler_params=pltpu.CompilerParams(
            collective_id=0 if s > 0 else 1, has_side_effects=True, vmem_limit_bytes=48 * 2**20
        ),
    )(offsets, stiffness, state, parent)


def per_device(state, parent, stiffness, offsets):
    flat = state.reshape(3 * NZ * BX, BY)
    cells = parent.reshape(3 * NZ, PROWS, PCOLS)
    out = lax.cond(
        offsets[2] > 0, functools.partial(move, 1), functools.partial(move, -1), flat, cells, stiffness, offsets
    )
    return out.reshape(3, NZ, BX, BY)


def solution(mesh):
    return jax.shard_map(
        per_device,
        mesh=mesh,
        in_specs=(P(None, None, "gx", "gy"), P(None, None, "gx", "gy"), P(), P()),
        out_specs=P(None, None, "gx", "gy"),
        check_vma=False,
    )
```

```python
import functools

import jax
import jax.numpy as jnp
from jax import lax
from jax.experimental import pallas as pl
from jax.experimental.pallas import tpu as pltpu
from jax.sharding import PartitionSpec as P

MESH = pl.DeviceIdType.MESH
F32 = jnp.float32
GX, GY = 8, 16
NZ, BX, BY = 64, 16, 128
CHUNKS = 4
ZC = NZ // CHUNKS
TILES = ZC // 8
PROWS, PCOLS = 6, 34
SLOTS = ((0.375, 0.625, 0.0), (0.125, 0.875, 0.0), (0.0, 0.875, 0.125), (0.0, 0.625, 0.375))


def roll(x, shift):
    shift = shift % 128
    return x if shift == 0 else pltpu.roll(x, shift, 1)


def iota(shape, dim):
    return lax.broadcasted_iota(jnp.int32, shape, dim)


def split_dot(a, b):
    high = a.astype(jnp.bfloat16)
    low = (a - high.astype(F32)).astype(jnp.bfloat16)
    both = jnp.dot(jnp.concatenate([high, low], axis=0), b, preferred_element_type=F32)
    return both[: a.shape[0]] + both[a.shape[0] :]


def bilinear(cell, lower, frac):
    return jnp.where(cell == lower, 1.0 - frac, 0.0) + jnp.where(cell == lower + 1, frac, 0.0)


def kernel(
    s,
    off_hbm,
    stiff_hbm,
    st_hbm,
    par_hbm,
    out_hbm,
    st,
    pin,
    sp,
    own,
    hx,
    yp,
    lp,
    cp,
    cr,
    qm,
    qe,
    pb,
    ub,
    vb,
    ok,
    lr,
    bm,
    be,
    wv,
    sd,
    sx,
    outv,
    tb,
    rsp,
    rsr,
    rsum,
    rnb,
    wr,
    fr,
    hfr,
    csm,
    csr,
    wc,
    off_ref,
    stiff_ref,
    in_sem,
    par_sem,
    smem_sem,
    out_sem,
    send_sem,
    recv_sem,
):
    gx, gy = lax.axis_index("gx"), lax.axis_index("gy")
    here = lambda dx, dy: {"gx": gx + dx, "gy": gy + dy}
    inside = lambda dx, dy: (gx + dx >= 0) & (gx + dx < GX) & (gy + dy >= 0) & (gy + dy < GY)
    ex = GX - 1 if s > 0 else 0
    ey = 0 if s > 0 else GY - 1
    at_x, at_y = gx == ex, gy == ey
    last = 13 if s > 0 else 14

    def lo(d):
        return (2 * d) // 3

    def feeds(src, dst):
        return (src >= lo(dst)) & (src <= lo(dst) + 3) & (dst >= 0) & (dst < GX) & (src >= 0) & (src < GX)

    partners = [(dx, dy, inside(dx, dy)) for dx, dy in ((-1, 0), (1, 0), (0, -1), (0, 1), (-1, 1), (1, -1))]
    partners.append((2 * s, 0, gx == ex - 2 * s))
    partners.append((-2 * s, 0, at_x))
    for d in (-3, -2, 2, 3):
        partners.append((d, 0, at_y & (feeds(gx, gx + d) | feeds(gx + d, gx))))
    barrier = pltpu.get_barrier_semaphore()
    for dx, dy, cond in partners:

        @pl.when(cond)
        def _():
            pl.semaphore_signal(barrier, inc=1, device_id=here(dx, dy), device_id_type=MESH)

    def remote(slot, src, dst, device, recv_slot=None):
        return pltpu.make_async_remote_copy(
            src_ref=src,
            dst_ref=dst,
            send_sem=send_sem.at[slot],
            recv_sem=recv_sem.at[slot if recv_slot is None else recv_slot],
            device_id=device,
            device_id_type=MESH,
        )

    def start(messages):
        for cond, *copy in messages:

            @pl.when(cond)
            def _():
                remote(*copy).start()

    def sent(messages):
        for cond, *copy in messages:

            @pl.when(cond)
            def _():
                remote(*copy).wait_send()

    def arrive(cond, slot, ref, device):
        @pl.when(cond)
        def _():
            remote(slot, ref, ref, device).wait_recv()

    CS_RECV, CS_SEND, RS, NB, FIRST = 0, 4, 10, 12, 14
    ROUND = FIRST + 5 * CHUNKS
    counts = (6, 5, 4)

    def column_messages():
        return [
            (
                at_y & feeds(gx, gx + d),
                CS_SEND + k,
                csm,
                csr.at[gx - lo(gx + d)],
                here(d, 0),
                CS_RECV + gx - lo(gx + d),
            )
            for k, d in enumerate((-3, -2, -1, 1, 2, 3))
        ]

    def row_messages():
        return [(gx == ex - far * s, RS + k, rsp, rsr.at[k], here(far * s, 0)) for k, far in enumerate((2, 1))]

    def strip_messages():
        return [
            (at_x & (gy >= 1) & (gy - 1 <= last), NB, rsum, rnb, here(0, -1)),
            (at_x & (gy + 1 > last) & (gy + 1 < GY), NB + 1, rsum, rnb, here(0, 1)),
        ]

    def first_rows(f):
        return pl.ds(0 if s > 0 else BX - counts[f], counts[f])

    def first_x(c):
        return [
            (
                inside(-s, 0),
                FIRST + 5 * c + f,
                own.at[c, f, first_rows(f)],
                hx.at[c, f, pl.ds(0, counts[f])],
                here(-s, 0),
            )
            for f in range(3)
        ]

    def first_y(c):
        return [
            (inside(0, s), FIRST + 5 * c + 3, yp.at[c], lp.at[c], here(0, s)),
            (inside(-s, s), FIRST + 5 * c + 4, cp.at[c], cr.at[c], here(-s, s)),
        ]

    def p_rows(r, c, first):
        return pb.at[r, c, pl.ds(first + 4, 2)]

    near, far_side = (0, BX) if s > 0 else (BX - 2, -2)

    def near_messages(c):
        return [(inside(-s, 0), round_slot(1, c), p_rows(1, c, near), p_rows(1, c, far_side), here(-s, 0))]

    def round_slot(r, c):
        return ROUND + ((r - 1) * CHUNKS + c) * 4

    def round_messages(r, c):
        k = round_slot(r, c)
        return [
            (inside(-1, 0), k, p_rows(r, c, 0), p_rows(r, c, BX), here(-1, 0)),
            (inside(1, 0), k + 1, p_rows(r, c, BX - 2), p_rows(r, c, -2), here(1, 0)),
            (inside(0, -1), k + 2, ok.at[r, c], lr.at[r, c, 1], here(0, -1)),
            (inside(0, 1), k + 3, ok.at[r, c], lr.at[r, c, 0], here(0, 1)),
        ]

    def receive(r, c):
        k = round_slot(r, c)
        arrive(inside(1, 0), k, p_rows(r, c, BX), here(1, 0))
        arrive(inside(-1, 0), k + 1, p_rows(r, c, -2), here(-1, 0))
        arrive(inside(0, 1), k + 2, lr.at[r, c, 1], here(0, 1))
        arrive(inside(0, -1), k + 3, lr.at[r, c, 0], here(0, -1))

    def chunk_rows(f, c):
        return pl.ds(f * NZ * BX + c * ZC * BX, ZC * BX)

    def load(c, f):
        return pltpu.make_async_copy(st_hbm.at[chunk_rows(f, c)], st.at[chunk_rows(f, c)], in_sem.at[c, f])

    def store(c, f):
        return pltpu.make_async_copy(outv.at[chunk_rows(f, c)], out_hbm.at[chunk_rows(f, c)], out_sem.at[c, f])

    def state_row(c, f, x):
        return st[pl.ds(f * NZ * BX + c * ZC * BX + x, ZC, stride=BX), :]

    for c in range(CHUNKS):
        for f in range(3):
            load(c, f).start()
    par_copy = pltpu.make_async_copy(par_hbm, pin, par_sem)
    par_copy.start()
    scalars = [
        pltpu.make_async_copy(off_hbm, off_ref, smem_sem.at[0]),
        pltpu.make_async_copy(stiff_hbm, stiff_ref, smem_sem.at[1]),
    ]
    for copy in scalars:
        copy.start()

    lane = iota((8, 128), 1)
    group, e = lane >> 3, lane & 7
    lane_c = iota((ZC, 128), 1)
    group_c, e_c = lane_c >> 3, lane_c & 7

    sent_rows = [range(n) if s > 0 else range(BX - n, BX) for n in counts]
    for c in range(CHUNKS):
        for f in range(3):
            load(c, f).wait()
            for x in sent_rows[f]:
                own[c, f, x] = state_row(c, f, x)
    pl.semaphore_wait(barrier, sum(cond.astype(jnp.int32) for _, _, cond in partners))
    for c in range(CHUNKS):
        start(first_x(c))

    def pack(c, carry):
        for f in range(3):
            packed = jnp.zeros((ZC, 128), F32)
            for x in range(BX):
                if x in sent_rows[f]:
                    row = own[c, f, x]
                else:
                    row = state_row(c, f, x)
                    own[c, f, x] = row
                packed = jnp.where(group_c == x, roll(row, 8 * x + (8 if s > 0 else 0)), packed)
            yp[c, f] = packed
            for q in range(TILES // 2):
                one, two = packed[16 * q : 16 * q + 8], packed[16 * q + 8 : 16 * q + 16]
                turn = 0 if s > 0 else 48
                cp[c, f, q] = jnp.where(lane < 64, roll(one, turn), roll(two, turn + 64))
        start(first_y(c))
        return carry

    lax.fori_loop(0, CHUNKS, pack, 0)

    par_copy.wait()
    for copy in scalars:
        copy.wait()
    use_rows = (gx >= 5) if s > 0 else (gx <= 2)
    ox = off_ref[0]

    @pl.when(use_rows)
    def _():
        low = ox + 31 if s > 0 else ox - 2
        for k in range(3):
            tb[k] = jnp.zeros((128, 128), F32)
            weight = [jnp.where(PROWS * gx + row == low + k, 1.0, 0.0) for row in range(PROWS)]
            for f in range(3):
                tb[k, PCOLS * f : PCOLS * f + PCOLS, 0:NZ] = sum(
                    weight[row] * pin[PROWS * f + row] for row in range(PROWS)
                )
        for k in range(3):
            rsp[k] = jnp.transpose(tb[k])[0:NZ]

    start(row_messages())

    @pl.when(at_y)
    def _():
        first_col = 27 if s > 0 else 30
        tb[3] = jnp.zeros((128, 128), F32)
        for row in range(PROWS):
            for f in range(3):
                at = 9 * row + 3 * f
                tb[3, at : at + 3, 0:NZ] = pin[PROWS * f + row, first_col : first_col + 3]
        turned = jnp.transpose(tb[3])
        csm[...] = turned[0:32] + roll(turned[32:64], 64)

    start(column_messages())

    sub = iota((8, 128), 0)
    for t in range(NZ // 8):
        value = jnp.zeros((8, 128), F32)
        for q in range(8):
            value = jnp.where(sub == q, stiff_ref[8 * t + q], value)
        sp[pl.ds(8 * t, 8), :] = 0.5 * value

    def ends(c, carry):
        for r in range(1, 4):

            @pl.when(gx == 0)
            def _():
                pb[r, c, 2:4] = jnp.zeros((2, ZC, 128), F32)

            @pl.when(gx == GX - 1)
            def _():
                pb[r, c, 20:22] = jnp.zeros((2, ZC, 128), F32)

            @pl.when(gy == 0)
            def _():
                lr[r, c, 0] = jnp.zeros((ZC, 128), F32)

            @pl.when(gy == GY - 1)
            def _():
                lr[r, c, 1] = jnp.zeros((ZC, 128), F32)

        return carry

    lax.fori_loop(0, CHUNKS, ends, 0)

    kk = iota((128, 128), 0)
    nn = iota((128, 128), 1)

    @pl.when(at_y)
    def _():
        krow = (kk * 57) >> 9
        krem = kk - 9 * krow
        kf = (krem >= 3).astype(jnp.int32) + (krem >= 6).astype(jnp.int32)
        ks = krem - 3 * kf
        ne = nn & 7
        col = (ne - 4) if s > 0 else ne
        wy = bilinear(ks, (2 * col + 5) >> 3, ((2 * col + 5) & 7).astype(F32) * 0.125)
        wy = jnp.where((col >= 0) & (col < 4) & (kk < 54), wy, 0.0)
        g = nn >> 3
        rows = (g, jnp.where(g < 2, g - 2, jnp.where(g < 4, g + 14, jnp.where(g < 6, g - 8 if s > 0 else g + 14, 0))))
        for k in range(4):
            for m in range(2):
                i = rows[m]
                lower = ox + s + 4 * gx + ((2 * i - 3) >> 3)
                wx = bilinear(PROWS * (lo(gx) + k) + krow, lower, ((2 * i - 3) & 7).astype(F32) * 0.125)
                for f in range(3):
                    wc[f, m, 128 * k : 128 * k + 128] = jnp.where(kf == f, wx * wy, 0.0).astype(jnp.bfloat16)

        for k in range(4):
            src = lo(gx) + k

            @pl.when(src == gx)
            def _():
                csr[k] = csm[...]

            @pl.when(src != gx)
            def _():
                remote(CS_RECV + k, csm, csr.at[k], here(src - gx, 0)).wait_recv()

        parts = [jnp.concatenate([csr[k], roll(csr[k], 64)], axis=0) for k in range(4)]
        column = jnp.concatenate(parts, axis=1)
        for f in range(3):
            for m, dest in enumerate((qm, qe)):
                total = split_dot(column, wc[f, m])
                for c in range(CHUNKS):
                    dest[c, f] = total[c * ZC : (c + 1) * ZC]

    @pl.when(at_x)
    def _():
        for k, far in enumerate((2, 1)):
            remote(RS + k, rsp, rsr.at[k], here(-far * s, 0)).wait_recv()
        for k in range(3):
            rsum[k] = rsp[k] + rsr[0, k] + rsr[1, k]

    start(strip_messages())

    @pl.when(at_x)
    def _():
        base = 28 if s > 0 else 30
        other = jnp.where(gy <= last, gy + 1, gy - 1)

        def weights(block, f, j):
            lower = base + 32 * gy + ((2 * j - 3) >> 3)
            frac = ((2 * j - 3) & 7).astype(F32) * 0.125
            valid = (kk >= PCOLS * f) & (kk < PCOLS * f + PCOLS)
            return jnp.where(valid, bilinear(PCOLS * block + kk - PCOLS * f, lower, frac), 0.0)

        ne = nn & 7
        for b, block in enumerate((gy, other)):
            kr = slice(128 * b, 128 * b + 128)
            for f in range(3):
                wr[f, kr] = weights(block, f, nn).astype(jnp.bfloat16)
                wr[3 + f, kr] = weights(block, f, ne - 4).astype(jnp.bfloat16)
                wr[6 + f, kr] = weights(block, f, ne + 124).astype(jnp.bfloat16)

    edge = lane_c < 4 if s > 0 else lane_c >= 124
    strip = 12 if s > 0 else 0
    ends_x = ((gx == 0) & (lane_c < 16)) | ((gx == GX - 1) & (lane_c >= 16) & (lane_c < 32))
    ends_l, ends_r = (gy == 0) & (e_c < 4), (gy == GY - 1) & (e_c >= 4)
    ends_y = ((gy == 0) & ((e_c < 2) | (e_c == 4))) | ((gy == GY - 1) & ((e_c == 2) | (e_c == 3) | (e_c == 5)))
    spans = ((pb, 4, -4, 22), (ub, 3, -3, 20), (vb, 2, -2, 18)) if s > 0 else ((pb, 4, -2, 22), (ub, 3, -1, 20), (vb, 2, 0, 18))

    def held(i):
        return 0 <= i + 4 * s < BX

    def source(c, f, i):
        old = i + 4 * s
        if held(i):
            return own[c, f, old]
        return hx[c, f, old - BX if s > 0 else old + counts[f]]

    def extra_group(i):
        return {-4: 4, -3: 5, -2: 0, -1: 1, 16: 2, 17: 3, 18: 4, 19: 5}[i]

    def assemble(c, mine):
        for f, (dest, base, first, count) in enumerate(spans):
            main, extra = qm[c, f], qe[c, f]
            for i in range(first, first + count):
                if held(i) != mine:
                    continue
                if 0 <= i < BX:
                    side = roll(main, -(8 * i + 4))
                else:
                    side = roll(extra, -(8 * extra_group(i) + 4))
                dest[0, c, i + base] = jnp.where(edge, side, roll(source(c, f, i), 4 * s))

    def late_columns(c):
        for f, last_row in enumerate(((18, -2), (17, -1), (16, 0))):
            main, extra = bm[c, f], be[c, f]
            for i in range(12, last_row[0]) if s > 0 else range(last_row[1], 4):
                row = source(c, f, i)
                if 0 <= i < BX:
                    main = jnp.where(group_c == i, roll(row, 8 * i + (8 if s > 0 else 0)), main)
                else:
                    g = extra_group(i)
                    extra = jnp.where(group_c == g, roll(row, 8 * g + (8 if s > 0 else 0)), extra)
            bm[c, f] = main
            be[c, f] = extra

    def windows(c):
        q = [(qm[c, f], jnp.where(ends_x, 0.0, qe[c, f])) for f in range(3)]
        b = [(bm[c, f], jnp.where(ends_x, 0.0, be[c, f])) for f in range(3)]
        return (q, b) if s > 0 else (b, q)

    def new_v(p, v, ends):
        return jnp.where(ends, 0.0, v - 0.5 * (roll(p, -1) - roll(p, 1)))

    def put_sides(dest, c, pl_, pr_, vl_, vr_):
        dest[c] = jnp.where(
            e_c == 0, roll(pr_, -4), jnp.where(e_c == 1, roll(pl_, -2), jnp.where(e_c == 2, roll(vr_, -2), vl_))
        )

    def up(main, extra):
        return jnp.where(lane_c < 8, roll(extra, -8), roll(main, 8))

    def down(main, extra):
        return jnp.where(lane_c >= 120, roll(extra, 104), roll(main, -8))

    def window_step(fields, ends, speed):
        (p, px), (u, ux), (v, _) = fields
        u1 = u - 0.5 * (down(p, px) - up(p, px))
        slope = jnp.where(lane_c < 16, roll(p, 8) - roll(px, 8), roll(px, -8) - roll(p, 24))
        u1x = jnp.where(ends_x, 0.0, ux - 0.5 * slope)
        v1 = new_v(p, v, ends)
        p1 = p - speed * ((down(u1, u1x) - up(u1, u1x)) + (roll(v1, -1) - roll(v1, 1)))
        return jnp.where(ends, 0.0, p1), v1

    def step(r, c, first, count):
        final = isinstance(r, int) and r == 3
        packs = not final and not (isinstance(r, int) and r == 0)

        def tile(t):
            zr = pl.ds(8 * t, 8)
            side, extra = sd[c, zr], sx[c, zr]
            speed = sp[pl.ds(pl.multiple_of(c * ZC + 8 * t, 8), 8), :]
            p = {n: pb[r, c, n + 4, zr] for n in range(first - 2, first + count + 2)}
            u = {}
            for n in range(first - 1, first + count + 1):
                new = ub[r, c, n + 3, zr] - 0.5 * (p[n + 1] - p[n - 1])
                if n == -1:
                    new = jnp.where(gx == 0, 0.0, new)
                if n == BX:
                    new = jnp.where(gx == GX - 1, 0.0, new)
                u[n] = new
                mine = first <= n < first + count or (n == -1 and first == 0) or (n == BX and first + count == BX)
                if not final and mine and -1 <= n <= BX:
                    ub[r + 1, c, n + 3, zr] = new
            pack = jnp.zeros((8, 128), F32)
            for x in range(first, first + count):
                near_side, g = (side, x) if 0 <= x < BX else (extra, extra_group(x))
                side_p = roll(near_side, -(8 * g + 1))
                before = jnp.where(lane == 0, side_p, roll(p[x], 1))
                after = jnp.where(lane == 127, side_p, roll(p[x], -1))
                v = vb[r, c, x + 2, zr] - 0.5 * (after - before)
                side_v = roll(near_side, -(8 * g + 3))
                before = jnp.where(lane == 0, side_v, roll(v, 1))
                after = jnp.where(lane == 127, side_v, roll(v, -1))
                new_p = p[x] - speed * ((u[x + 1] - u[x - 1]) + (after - before))
                if x < 0:
                    new_p = jnp.where(gx == 0, 0.0, new_p)
                if x >= BX:
                    new_p = jnp.where(gx == GX - 1, 0.0, new_p)
                if final:
                    for f, value in enumerate((new_p, u[x], v)):
                        outv[pl.ds(f * NZ * BX + (c * ZC + 8 * t) * BX + x, 8, stride=BX), :] = value
                else:
                    pb[r + 1, c, x + 4, zr] = new_p
                    if 0 <= x < BX:
                        vb[r + 1, c, x + 2, zr] = v
                    if packs:
                        pack = jnp.where(group == x, roll(new_p, 8 * x + 2), pack)
            if packs:
                ok[r + 1, c, zr] = pack

        for t in range(TILES):
            tile(t)

    early, late = ((-2, 12), (10, 6)) if s > 0 else ((6, 12), (0, 6))

    def begin(c, carry):
        arrive(inside(0, -s), FIRST + 5 * c + 3, lp.at[c], here(0, -s))
        arrive(inside(s, -s), FIRST + 5 * c + 4, cr.at[c], here(s, -s))

        @pl.when(jnp.logical_not(at_y))
        def _():
            for f in range(3):
                for t in range(TILES):
                    zr, w = pl.ds(8 * t, 8), t % 2
                    corner, side = cr[c, f, t // 2], lp[c, f, zr]
                    if s > 0:
                        qm[c, f, zr] = jnp.where(lane < 96, roll(side, -32), roll(corner, 96 - 64 * w))
                        qe[c, f, zr] = jnp.where(
                            lane < 16, roll(side, -16), jnp.where(lane < 32, roll(corner, -16 - 64 * w), roll(side, 32))
                        )
                    else:
                        qm[c, f, zr] = jnp.where(lane < 32, roll(corner, -16 - 64 * w), roll(side, 32))
                        qe[c, f, zr] = jnp.where(lane < 16, roll(corner, -64 * w), roll(side, -80))

        for f in range(3):
            mine = yp[c, f]
            bm[c, f] = roll(mine, -32 * s)
            be[c, f] = roll(mine, -16 if s > 0 else -80)
        assemble(c, True)

        @pl.when(gx == GX - 1 - ex)
        def _():
            pb[0, c, pl.ds(0 if s > 0 else 20, 4)] = jnp.zeros((4, ZC, 128), F32)

        lw, rw = windows(c)
        for dest, k in ((sd, 0), (sx, 1)):
            (pl_, vl_), (pr_, vr_) = [(w[0][k], w[2][k]) for w in (lw, rw)]
            pl_, pr_ = jnp.where(ends_l, 0.0, pl_), jnp.where(ends_r, 0.0, pr_)
            put_sides(dest, c, pl_, pr_, new_v(pl_, vl_, ends_l), new_v(pr_, vr_, ends_r))
        step(0, c, *early)
        start(near_messages(c))
        return carry

    lax.fori_loop(0, CHUNKS, begin, 0)

    @pl.when(at_x)
    def _():
        @pl.when(gy <= last)
        def _():
            remote(NB, rsum, rnb, here(0, 1)).wait_recv()

        @pl.when(gy > last)
        def _():
            remote(NB + 1, rsum, rnb, here(0, -1)).wait_recv()

        group_z = iota((NZ, 128), 1) >> 3
        rows = jnp.concatenate([jnp.concatenate([rsum[k], rnb[k]], axis=1) for k in range(3)], axis=0)
        for n in range(9):
            total = split_dot(rows, wr[n])
            slots = [total[NZ * k : NZ * k + NZ] for k in range(3)]
            strips = [sum(w * x for w, x in zip(SLOTS[r], slots) if w) for r in range(4)]
            if n < 3:
                for r in range(4):
                    for c in range(CHUNKS):
                        fr[c, n, r] = strips[r][c * ZC : (c + 1) * ZC]
            else:
                total = jnp.zeros((NZ, 128), F32)
                for r in range(4):
                    total = jnp.where(group_z == strip + r, strips[r], total)
                for c in range(CHUNKS):
                    hfr[c, n - 3] = total[c * ZC : (c + 1) * ZC]

    def complete(c, carry):
        for f in range(3):
            arrive(inside(s, 0), FIRST + 5 * c + f, hx.at[c, f, pl.ds(0, counts[f])], here(s, 0))
        assemble(c, False)
        late_columns(c)

        @pl.when(at_x)
        def _():
            for r in range(4):
                for f, (dest, base, _, _) in enumerate(spans):
                    dest[0, c, base + strip + r] = fr[c, f, r]
            pb[0, c, pl.ds(20 if s > 0 else 2, 2)] = jnp.zeros((2, ZC, 128), F32)
            strip_rows = (group_c >= strip) & (group_c < strip + 4)
            for f in range(3):
                for dest, region in ((qm, 0 if s > 0 else 1), (bm, 1 if s > 0 else 0)):
                    dest[c, f] = jnp.where(strip_rows, hfr[c, 3 * region + f], dest[c, f])

        lw, rw = windows(c)
        speed = window_speed(c)
        lw = [(jnp.where(ends_l, 0.0, m), jnp.where(ends_l, 0.0, x)) for m, x in lw]
        rw = [(jnp.where(ends_r, 0.0, m), jnp.where(ends_r, 0.0, x)) for m, x in rw]
        pl1, vl1 = window_step(lw, ends_l, speed)
        pr1, vr1 = window_step(rw, ends_r, speed)
        put_sides(sd, c, lw[0][0], rw[0][0], vl1, vr1)
        step(0, c, *late)
        arrive(inside(s, 0), round_slot(1, c), p_rows(1, c, far_side), here(s, 0))
        vl2, vr2 = new_v(pl1, vl1, ends_l), new_v(pr1, vr1, ends_r)
        put_sides(sd, c, pl1, pr1, vl2, vr2)
        wv[c] = jnp.where(e_c < 5, roll(vl2, 1), roll(vr2, 1))
        step(1, c, 0, BX)
        start(round_messages(2, c))
        return carry

    def window_speed(c):
        return sp[pl.ds(pl.multiple_of(c * ZC, ZC), ZC), :]

    lax.fori_loop(0, CHUNKS, complete, 0)

    def gather(r, c):
        receive(r, c)
        mine = ok[r, c]
        halo = jnp.where(e_c < 2, lr[r, c, 0], jnp.where(e_c < 4, lr[r, c, 1], wv[c]))
        halo = jnp.where(ends_y, 0.0, halo)
        slope = jnp.where(e_c == 4, roll(mine, 2) - roll(halo, 4), roll(halo, 2) - roll(mine, 4))
        wind = jnp.where(ends_y, 0.0, halo - 0.5 * slope)
        wv[c] = wind
        sd[c] = jnp.where(
            e_c == 0,
            roll(halo, -2),
            jnp.where(e_c == 1, halo, jnp.where(e_c == 2, roll(wind, -3), roll(wind, -1))),
        )

    def middle(c, carry):
        gather(2, c)
        step(2, c, 0, BX)
        start(round_messages(3, c))
        return carry

    lax.fori_loop(0, CHUNKS, middle, 0)

    def finish(c, carry):
        gather(3, c)
        step(3, c, 0, BX)
        for f in range(3):
            store(c, f).start()
        return carry

    lax.fori_loop(0, CHUNKS, finish, 0)

    sent(column_messages())
    sent(row_messages())
    sent(strip_messages())

    def settle(c, carry):
        sent(first_x(c))
        sent(first_y(c))
        sent(near_messages(c))
        for r in range(2, 4):
            sent(round_messages(r, c))
        for f in range(3):
            store(c, f).wait()
        return carry

    lax.fori_loop(0, CHUNKS, settle, 0)


def move(s, state, parent, stiffness, offsets):
    vmem = lambda *shape: pltpu.VMEM(shape, F32)
    sems = 14 + CHUNKS * 5 + 3 * CHUNKS * 4
    scratch = [
        vmem(3 * NZ * BX, 128),
        vmem(3 * PROWS, PCOLS, NZ),
        vmem(NZ, 128),
        vmem(CHUNKS, 3, BX, ZC, 128),
        vmem(CHUNKS, 3, 6, ZC, 128),
        vmem(CHUNKS, 3, ZC, 128),
        vmem(CHUNKS, 3, ZC, 128),
        vmem(CHUNKS, 3, TILES // 2, 8, 128),
        vmem(CHUNKS, 3, TILES // 2, 8, 128),
        vmem(CHUNKS, 3, ZC, 128),
        vmem(CHUNKS, 3, ZC, 128),
        vmem(4, CHUNKS, 24, ZC, 128),
        vmem(4, CHUNKS, 22, ZC, 128),
        vmem(4, CHUNKS, 20, ZC, 128),
        vmem(4, CHUNKS, ZC, 128),
        vmem(4, CHUNKS, 2, ZC, 128),
        vmem(CHUNKS, 3, ZC, 128),
        vmem(CHUNKS, 3, ZC, 128),
        vmem(CHUNKS, ZC, 128),
        vmem(CHUNKS, ZC, 128),
        vmem(CHUNKS, ZC, 128),
        vmem(3 * NZ * BX, 128),
        vmem(4, 128, 128),
        vmem(3, NZ, 128),
        vmem(2, 3, NZ, 128),
        vmem(3, NZ, 128),
        vmem(3, NZ, 128),
        pltpu.VMEM((9, 256, 128), jnp.bfloat16),
        vmem(CHUNKS, 3, 4, ZC, 128),
        vmem(CHUNKS, 6, ZC, 128),
        vmem(32, 128),
        vmem(4, 32, 128),
        pltpu.VMEM((3, 2, 512, 128), jnp.bfloat16),
        pltpu.SMEM((4,), jnp.int32),
        pltpu.SMEM((NZ,), F32),
        pltpu.SemaphoreType.DMA((CHUNKS, 3)),
        pltpu.SemaphoreType.DMA,
        pltpu.SemaphoreType.DMA((2,)),
        pltpu.SemaphoreType.DMA((CHUNKS, 3)),
        pltpu.SemaphoreType.DMA((sems,)),
        pltpu.SemaphoreType.DMA((sems,)),
    ]
    hbm = pl.BlockSpec(memory_space=pltpu.HBM)
    return pl.pallas_call(
        functools.partial(kernel, s),
        out_shape=jax.ShapeDtypeStruct((3 * NZ * BX, BY), F32),
        in_specs=[hbm, hbm, hbm, hbm],
        out_specs=hbm,
        scratch_shapes=scratch,
        compiler_params=pltpu.CompilerParams(
            collective_id=0 if s > 0 else 1, has_side_effects=True, vmem_limit_bytes=48 * 2**20
        ),
    )(offsets, stiffness, state, parent)


def per_device(state, parent, stiffness, offsets):
    flat = state.reshape(3 * NZ * BX, BY)
    cells = parent.transpose(0, 2, 3, 1).reshape(3 * PROWS, PCOLS, NZ)
    out = lax.cond(
        offsets[2] > 0, functools.partial(move, 1), functools.partial(move, -1), flat, cells, stiffness, offsets
    )
    return out.reshape(3, NZ, BX, BY)


def solution(mesh):
    return jax.shard_map(
        per_device,
        mesh=mesh,
        in_specs=(P(None, None, "gx", "gy"), P(None, None, "gx", "gy"), P(), P()),
        out_specs=P(None, None, "gx", "gy"),
        check_vma=False,
    )
```

```python
import functools

import jax
import jax.numpy as jnp
from jax import lax
from jax.experimental import pallas as pl
from jax.experimental.pallas import tpu as pltpu
from jax.sharding import PartitionSpec as P

MESH = pl.DeviceIdType.MESH
F32 = jnp.float32
GX, GY = 8, 16
NZ, BX, BY = 64, 16, 128
CHUNKS = 4
AHEAD = 2
ZC = NZ // CHUNKS
TILES = ZC // 8
PROWS, PCOLS = 6, 34
SLOTS = ((0.375, 0.625, 0.0), (0.125, 0.875, 0.0), (0.0, 0.875, 0.125), (0.0, 0.625, 0.375))


def roll(x, shift):
    shift = shift % 128
    return x if shift == 0 else pltpu.roll(x, shift, 1)


def iota(shape, dim):
    return lax.broadcasted_iota(jnp.int32, shape, dim)


def split_dot(a, b):
    high = a.astype(jnp.bfloat16)
    low = (a - high.astype(F32)).astype(jnp.bfloat16)
    both = jnp.dot(jnp.concatenate([high, low], axis=0), b, preferred_element_type=F32)
    return both[: a.shape[0]] + both[a.shape[0] :]


def bilinear(cell, lower, frac):
    return jnp.where(cell == lower, 1.0 - frac, 0.0) + jnp.where(cell == lower + 1, frac, 0.0)


def kernel(
    s,
    off_hbm,
    stiff_hbm,
    st_hbm,
    par_hbm,
    out_hbm,
    st,
    pin,
    sp,
    own,
    hx,
    yp,
    lp,
    cp,
    cr,
    qm,
    qe,
    pb,
    ub,
    vb,
    ok,
    lr,
    bm,
    be,
    wv,
    sd,
    sx,
    outv,
    tb,
    rsp,
    rsr,
    rsum,
    rnb,
    wr,
    fr,
    hfr,
    csm,
    csr,
    wc,
    off_ref,
    stiff_ref,
    in_sem,
    par_sem,
    smem_sem,
    out_sem,
    send_sem,
    recv_sem,
):
    gx, gy = lax.axis_index("gx"), lax.axis_index("gy")
    here = lambda dx, dy: {"gx": gx + dx, "gy": gy + dy}
    inside = lambda dx, dy: (gx + dx >= 0) & (gx + dx < GX) & (gy + dy >= 0) & (gy + dy < GY)
    ex = GX - 1 if s > 0 else 0
    ey = 0 if s > 0 else GY - 1
    at_x, at_y = gx == ex, gy == ey
    last = 13 if s > 0 else 14

    def lo(d):
        return (2 * d) // 3

    def feeds(src, dst):
        return (src >= lo(dst)) & (src <= lo(dst) + 3) & (dst >= 0) & (dst < GX) & (src >= 0) & (src < GX)

    partners = [(dx, dy, inside(dx, dy)) for dx, dy in ((-1, 0), (1, 0), (0, -1), (0, 1), (-1, 1), (1, -1))]
    partners.append((2 * s, 0, gx == ex - 2 * s))
    partners.append((-2 * s, 0, at_x))
    for d in (-3, -2, 2, 3):
        partners.append((d, 0, at_y & (feeds(gx, gx + d) | feeds(gx + d, gx))))
    barrier = pltpu.get_barrier_semaphore()
    for dx, dy, cond in partners:

        @pl.when(cond)
        def _():
            pl.semaphore_signal(barrier, inc=1, device_id=here(dx, dy), device_id_type=MESH)

    def remote(slot, src, dst, device, recv_slot=None):
        return pltpu.make_async_remote_copy(
            src_ref=src,
            dst_ref=dst,
            send_sem=send_sem.at[slot],
            recv_sem=recv_sem.at[slot if recv_slot is None else recv_slot],
            device_id=device,
            device_id_type=MESH,
        )

    def start(messages):
        for cond, *copy in messages:

            @pl.when(cond)
            def _():
                remote(*copy).start()

    def sent(messages):
        for cond, *copy in messages:

            @pl.when(cond)
            def _():
                remote(*copy).wait_send()

    def arrive(cond, slot, ref, device):
        @pl.when(cond)
        def _():
            remote(slot, ref, ref, device).wait_recv()

    CS_RECV, CS_SEND, RS, NB, FIRST = 0, 4, 10, 12, 14
    ROUND = FIRST + 5 * CHUNKS
    counts = (6, 5, 4)

    def column_messages():
        return [
            (
                at_y & feeds(gx, gx + d),
                CS_SEND + k,
                csm,
                csr.at[gx - lo(gx + d)],
                here(d, 0),
                CS_RECV + gx - lo(gx + d),
            )
            for k, d in enumerate((-3, -2, -1, 1, 2, 3))
        ]

    def row_messages():
        return [(gx == ex - far * s, RS + k, rsp, rsr.at[k], here(far * s, 0)) for k, far in enumerate((2, 1))]

    def strip_messages():
        return [
            (at_x & (gy >= 1) & (gy - 1 <= last), NB, rsum, rnb, here(0, -1)),
            (at_x & (gy + 1 > last) & (gy + 1 < GY), NB + 1, rsum, rnb, here(0, 1)),
        ]

    def first_rows(f):
        return pl.ds(0 if s > 0 else BX - counts[f], counts[f])

    def first_x(c):
        return [
            (
                inside(-s, 0),
                FIRST + 5 * c + f,
                own.at[c, f, first_rows(f)],
                hx.at[c, f, pl.ds(0, counts[f])],
                here(-s, 0),
            )
            for f in range(3)
        ]

    def first_y(c):
        return [
            (inside(0, s), FIRST + 5 * c + 3, yp.at[c], lp.at[c], here(0, s)),
            (inside(-s, s), FIRST + 5 * c + 4, cp.at[c], cr.at[c], here(-s, s)),
        ]

    def p_rows(r, c, first):
        return pb.at[r, c, pl.ds(first + 4, 2)]

    near, far_side = (0, BX) if s > 0 else (BX - 2, -2)

    def near_messages(c):
        return [(inside(-s, 0), round_slot(1, c), p_rows(1, c, near), p_rows(1, c, far_side), here(-s, 0))]

    def round_slot(r, c):
        return ROUND + ((r - 1) * CHUNKS + c) * 4

    def round_messages(r, c):
        k = round_slot(r, c)
        return [
            (inside(-1, 0), k, p_rows(r, c, 0), p_rows(r, c, BX), here(-1, 0)),
            (inside(1, 0), k + 1, p_rows(r, c, BX - 2), p_rows(r, c, -2), here(1, 0)),
            (inside(0, -1), k + 2, ok.at[r, c], lr.at[r, c, 1], here(0, -1)),
            (inside(0, 1), k + 3, ok.at[r, c], lr.at[r, c, 0], here(0, 1)),
        ]

    def receive(r, c):
        k = round_slot(r, c)
        arrive(inside(1, 0), k, p_rows(r, c, BX), here(1, 0))
        arrive(inside(-1, 0), k + 1, p_rows(r, c, -2), here(-1, 0))
        arrive(inside(0, 1), k + 2, lr.at[r, c, 1], here(0, 1))
        arrive(inside(0, -1), k + 3, lr.at[r, c, 0], here(0, -1))

    def chunk_rows(f, c):
        return pl.ds(f * NZ * BX + c * ZC * BX, ZC * BX)

    def load(c, f):
        return pltpu.make_async_copy(st_hbm.at[chunk_rows(f, c)], st.at[chunk_rows(f, c)], in_sem.at[c, f])

    def store(c, f):
        return pltpu.make_async_copy(outv.at[chunk_rows(f, c)], out_hbm.at[chunk_rows(f, c)], out_sem.at[c, f])

    def state_row(c, f, x):
        return st[pl.ds(f * NZ * BX + c * ZC * BX + x, ZC, stride=BX), :]

    for c in range(CHUNKS):
        for f in range(3):
            load(c, f).start()
    par_copy = pltpu.make_async_copy(par_hbm, pin, par_sem)
    par_copy.start()
    scalars = [
        pltpu.make_async_copy(off_hbm, off_ref, smem_sem.at[0]),
        pltpu.make_async_copy(stiff_hbm, stiff_ref, smem_sem.at[1]),
    ]
    for copy in scalars:
        copy.start()

    lane = iota((8, 128), 1)
    group, e = lane >> 3, lane & 7
    lane_c = iota((ZC, 128), 1)
    group_c, e_c = lane_c >> 3, lane_c & 7

    par_copy.wait()
    for copy in scalars:
        copy.wait()
    use_rows = (gx >= 5) if s > 0 else (gx <= 2)
    ox = off_ref[0]

    @pl.when(use_rows)
    def _():
        low = ox + 31 if s > 0 else ox - 2
        for k in range(3):
            tb[k] = jnp.zeros((128, 128), F32)
            weight = [jnp.where(PROWS * gx + row == low + k, 1.0, 0.0) for row in range(PROWS)]
            for f in range(3):
                tb[k, PCOLS * f : PCOLS * f + PCOLS, 0:NZ] = sum(
                    weight[row] * pin[PROWS * f + row] for row in range(PROWS)
                )
        for k in range(3):
            rsp[k] = jnp.transpose(tb[k])[0:NZ]

    sent_rows = [range(n) if s > 0 else range(BX - n, BX) for n in counts]
    for c in range(CHUNKS):
        for f in range(3):
            load(c, f).wait()
            for x in sent_rows[f]:
                own[c, f, x] = state_row(c, f, x)
        if c == 0:
            pl.semaphore_wait(barrier, sum(cond.astype(jnp.int32) for _, _, cond in partners))
            start(row_messages())
        if c < AHEAD:
            start(first_x(c))

    def pack(c, carry):
        for f in range(3):
            packed = jnp.zeros((ZC, 128), F32)
            for x in range(BX):
                if x in sent_rows[f]:
                    row = own[c, f, x]
                else:
                    row = state_row(c, f, x)
                    own[c, f, x] = row
                packed = jnp.where(group_c == x, roll(row, 8 * x + (8 if s > 0 else 0)), packed)
            yp[c, f] = packed
            for q in range(TILES // 2):
                one, two = packed[16 * q : 16 * q + 8], packed[16 * q + 8 : 16 * q + 16]
                turn = 0 if s > 0 else 48
                cp[c, f, q] = jnp.where(lane < 64, roll(one, turn), roll(two, turn + 64))
        start(first_y(c))
        return carry

    lax.fori_loop(0, CHUNKS, pack, 0)

    @pl.when(at_y)
    def _():
        first_col = 27 if s > 0 else 30
        tb[3] = jnp.zeros((128, 128), F32)
        for row in range(PROWS):
            for f in range(3):
                at = 9 * row + 3 * f
                tb[3, at : at + 3, 0:NZ] = pin[PROWS * f + row, first_col : first_col + 3]
        turned = jnp.transpose(tb[3])
        csm[...] = turned[0:32] + roll(turned[32:64], 64)

    start(column_messages())

    sub = iota((8, 128), 0)
    for t in range(NZ // 8):
        value = jnp.zeros((8, 128), F32)
        for q in range(8):
            value = jnp.where(sub == q, stiff_ref[8 * t + q], value)
        sp[pl.ds(8 * t, 8), :] = 0.5 * value

    def ends(c, carry):
        for r in range(1, 4):

            @pl.when(gx == 0)
            def _():
                pb[r, c, 2:4] = jnp.zeros((2, ZC, 128), F32)

            @pl.when(gx == GX - 1)
            def _():
                pb[r, c, 20:22] = jnp.zeros((2, ZC, 128), F32)

            @pl.when(gy == 0)
            def _():
                lr[r, c, 0] = jnp.zeros((ZC, 128), F32)

            @pl.when(gy == GY - 1)
            def _():
                lr[r, c, 1] = jnp.zeros((ZC, 128), F32)

        return carry

    lax.fori_loop(0, CHUNKS, ends, 0)

    kk = iota((128, 128), 0)
    nn = iota((128, 128), 1)

    @pl.when(at_y)
    def _():
        krow = (kk * 57) >> 9
        krem = kk - 9 * krow
        kf = (krem >= 3).astype(jnp.int32) + (krem >= 6).astype(jnp.int32)
        ks = krem - 3 * kf
        ne = nn & 7
        col = (ne - 4) if s > 0 else ne
        wy = bilinear(ks, (2 * col + 5) >> 3, ((2 * col + 5) & 7).astype(F32) * 0.125)
        wy = jnp.where((col >= 0) & (col < 4) & (kk < 54), wy, 0.0)
        g = nn >> 3
        rows = (g, jnp.where(g < 2, g - 2, jnp.where(g < 4, g + 14, jnp.where(g < 6, g - 8 if s > 0 else g + 14, 0))))
        for k in range(4):
            for m in range(2):
                i = rows[m]
                lower = ox + s + 4 * gx + ((2 * i - 3) >> 3)
                wx = bilinear(PROWS * (lo(gx) + k) + krow, lower, ((2 * i - 3) & 7).astype(F32) * 0.125)
                for f in range(3):
                    wc[f, m, 128 * k : 128 * k + 128] = jnp.where(kf == f, wx * wy, 0.0).astype(jnp.bfloat16)

        for k in range(4):
            src = lo(gx) + k

            @pl.when(src == gx)
            def _():
                csr[k] = csm[...]

            @pl.when(src != gx)
            def _():
                remote(CS_RECV + k, csm, csr.at[k], here(src - gx, 0)).wait_recv()

        parts = [jnp.concatenate([csr[k], roll(csr[k], 64)], axis=0) for k in range(4)]
        column = jnp.concatenate(parts, axis=1)
        for f in range(3):
            for m, dest in enumerate((qm, qe)):
                total = split_dot(column, wc[f, m])
                for c in range(CHUNKS):
                    dest[c, f] = total[c * ZC : (c + 1) * ZC]

    edge = lane_c < 4 if s > 0 else lane_c >= 124
    strip = 12 if s > 0 else 0
    ends_x = ((gx == 0) & (lane_c < 16)) | ((gx == GX - 1) & (lane_c >= 16) & (lane_c < 32))
    ends_l, ends_r = (gy == 0) & (e_c < 4), (gy == GY - 1) & (e_c >= 4)
    ends_y = ((gy == 0) & ((e_c < 2) | (e_c == 4))) | ((gy == GY - 1) & ((e_c == 2) | (e_c == 3) | (e_c == 5)))
    spans = ((pb, 4, -4, 22), (ub, 3, -3, 20), (vb, 2, -2, 18)) if s > 0 else ((pb, 4, -2, 22), (ub, 3, -1, 20), (vb, 2, 0, 18))

    def held(i):
        return 0 <= i + 4 * s < BX

    def source(c, f, i):
        old = i + 4 * s
        if held(i):
            return own[c, f, old]
        return hx[c, f, old - BX if s > 0 else old + counts[f]]

    def extra_group(i):
        return {-4: 4, -3: 5, -2: 0, -1: 1, 16: 2, 17: 3, 18: 4, 19: 5}[i]

    def assemble(c, mine):
        for f, (dest, base, first, count) in enumerate(spans):
            main, extra = qm[c, f], qe[c, f]
            for i in range(first, first + count):
                if held(i) != mine:
                    continue
                if 0 <= i < BX:
                    side = roll(main, -(8 * i + 4))
                else:
                    side = roll(extra, -(8 * extra_group(i) + 4))
                dest[0, c, i + base] = jnp.where(edge, side, roll(source(c, f, i), 4 * s))

    def late_columns(c):
        for f, last_row in enumerate(((18, -2), (17, -1), (16, 0))):
            main, extra = bm[c, f], be[c, f]
            for i in range(12, last_row[0]) if s > 0 else range(last_row[1], 4):
                row = source(c, f, i)
                if 0 <= i < BX:
                    main = jnp.where(group_c == i, roll(row, 8 * i + (8 if s > 0 else 0)), main)
                else:
                    g = extra_group(i)
                    extra = jnp.where(group_c == g, roll(row, 8 * g + (8 if s > 0 else 0)), extra)
            bm[c, f] = main
            be[c, f] = extra

    def windows(c):
        q = [(qm[c, f], jnp.where(ends_x, 0.0, qe[c, f])) for f in range(3)]
        b = [(bm[c, f], jnp.where(ends_x, 0.0, be[c, f])) for f in range(3)]
        return (q, b) if s > 0 else (b, q)

    def new_v(p, v, ends):
        return jnp.where(ends, 0.0, v - 0.5 * (roll(p, -1) - roll(p, 1)))

    def put_sides(dest, c, pl_, pr_, vl_, vr_):
        dest[c] = jnp.where(
            e_c == 0, roll(pr_, -4), jnp.where(e_c == 1, roll(pl_, -2), jnp.where(e_c == 2, roll(vr_, -2), vl_))
        )

    def up(main, extra):
        return jnp.where(lane_c < 8, roll(extra, -8), roll(main, 8))

    def down(main, extra):
        return jnp.where(lane_c >= 120, roll(extra, 104), roll(main, -8))

    def window_step(fields, ends, speed):
        (p, px), (u, ux), (v, _) = fields
        u1 = u - 0.5 * (down(p, px) - up(p, px))
        slope = jnp.where(lane_c < 16, roll(p, 8) - roll(px, 8), roll(px, -8) - roll(p, 24))
        u1x = jnp.where(ends_x, 0.0, ux - 0.5 * slope)
        v1 = new_v(p, v, ends)
        p1 = p - speed * ((down(u1, u1x) - up(u1, u1x)) + (roll(v1, -1) - roll(v1, 1)))
        return jnp.where(ends, 0.0, p1), v1

    def step(r, c, first, count):
        final = isinstance(r, int) and r == 3
        packs = not final and not (isinstance(r, int) and r == 0)

        def tile(t):
            zr = pl.ds(8 * t, 8)
            side, extra = sd[c, zr], sx[c, zr]
            speed = sp[pl.ds(pl.multiple_of(c * ZC + 8 * t, 8), 8), :]
            p = {n: pb[r, c, n + 4, zr] for n in range(first - 2, first + count + 2)}
            u = {}
            for n in range(first - 1, first + count + 1):
                new = ub[r, c, n + 3, zr] - 0.5 * (p[n + 1] - p[n - 1])
                if n == -1:
                    new = jnp.where(gx == 0, 0.0, new)
                if n == BX:
                    new = jnp.where(gx == GX - 1, 0.0, new)
                u[n] = new
                mine = first <= n < first + count or (n == -1 and first == 0) or (n == BX and first + count == BX)
                if not final and mine and -1 <= n <= BX:
                    ub[r + 1, c, n + 3, zr] = new
            pack = jnp.zeros((8, 128), F32)
            for x in range(first, first + count):
                near_side, g = (side, x) if 0 <= x < BX else (extra, extra_group(x))
                side_p = roll(near_side, -(8 * g + 1))
                before = jnp.where(lane == 0, side_p, roll(p[x], 1))
                after = jnp.where(lane == 127, side_p, roll(p[x], -1))
                v = vb[r, c, x + 2, zr] - 0.5 * (after - before)
                side_v = roll(near_side, -(8 * g + 3))
                before = jnp.where(lane == 0, side_v, roll(v, 1))
                after = jnp.where(lane == 127, side_v, roll(v, -1))
                new_p = p[x] - speed * ((u[x + 1] - u[x - 1]) + (after - before))
                if x < 0:
                    new_p = jnp.where(gx == 0, 0.0, new_p)
                if x >= BX:
                    new_p = jnp.where(gx == GX - 1, 0.0, new_p)
                if final:
                    for f, value in enumerate((new_p, u[x], v)):
                        outv[pl.ds(f * NZ * BX + (c * ZC + 8 * t) * BX + x, 8, stride=BX), :] = value
                else:
                    pb[r + 1, c, x + 4, zr] = new_p
                    if 0 <= x < BX:
                        vb[r + 1, c, x + 2, zr] = v
                    if packs:
                        pack = jnp.where(group == x, roll(new_p, 8 * x + 2), pack)
            if packs:
                ok[r + 1, c, zr] = pack

        for t in range(TILES):
            tile(t)

    early, late = ((-2, 12), (10, 6)) if s > 0 else ((6, 12), (0, 6))

    def begin(c, carry):
        @pl.when(at_x & (c == CHUNKS // 2))
        def _():
            for k, far in enumerate((2, 1)):
                remote(RS + k, rsp, rsr.at[k], here(-far * s, 0)).wait_recv()
            for k in range(3):
                rsum[k] = rsp[k] + rsr[0, k] + rsr[1, k]
            start(strip_messages())

        arrive(inside(0, -s), FIRST + 5 * c + 3, lp.at[c], here(0, -s))
        arrive(inside(s, -s), FIRST + 5 * c + 4, cr.at[c], here(s, -s))

        @pl.when(jnp.logical_not(at_y))
        def _():
            for f in range(3):
                for t in range(TILES):
                    zr, w = pl.ds(8 * t, 8), t % 2
                    corner, side = cr[c, f, t // 2], lp[c, f, zr]
                    if s > 0:
                        qm[c, f, zr] = jnp.where(lane < 96, roll(side, -32), roll(corner, 96 - 64 * w))
                        qe[c, f, zr] = jnp.where(
                            lane < 16, roll(side, -16), jnp.where(lane < 32, roll(corner, -16 - 64 * w), roll(side, 32))
                        )
                    else:
                        qm[c, f, zr] = jnp.where(lane < 32, roll(corner, -16 - 64 * w), roll(side, 32))
                        qe[c, f, zr] = jnp.where(lane < 16, roll(corner, -64 * w), roll(side, -80))

        for f in range(3):
            mine = yp[c, f]
            bm[c, f] = roll(mine, -32 * s)
            be[c, f] = roll(mine, -16 if s > 0 else -80)
        assemble(c, True)

        @pl.when(gx == GX - 1 - ex)
        def _():
            pb[0, c, pl.ds(0 if s > 0 else 20, 4)] = jnp.zeros((4, ZC, 128), F32)

        lw, rw = windows(c)
        for dest, k in ((sd, 0), (sx, 1)):
            (pl_, vl_), (pr_, vr_) = [(w[0][k], w[2][k]) for w in (lw, rw)]
            pl_, pr_ = jnp.where(ends_l, 0.0, pl_), jnp.where(ends_r, 0.0, pr_)
            put_sides(dest, c, pl_, pr_, new_v(pl_, vl_, ends_l), new_v(pr_, vr_, ends_r))
        step(0, c, *early)
        start(near_messages(c))

        @pl.when(c + AHEAD < CHUNKS)
        def _():
            start(first_x(c + AHEAD))

        return carry

    lax.fori_loop(0, CHUNKS, begin, 0)

    @pl.when(at_x)
    def _():
        base = 28 if s > 0 else 30
        other = jnp.where(gy <= last, gy + 1, gy - 1)

        def weights(block, f, j):
            lower = base + 32 * gy + ((2 * j - 3) >> 3)
            frac = ((2 * j - 3) & 7).astype(F32) * 0.125
            valid = (kk >= PCOLS * f) & (kk < PCOLS * f + PCOLS)
            return jnp.where(valid, bilinear(PCOLS * block + kk - PCOLS * f, lower, frac), 0.0)

        ne = nn & 7
        for b, block in enumerate((gy, other)):
            kr = slice(128 * b, 128 * b + 128)
            for f in range(3):
                wr[f, kr] = weights(block, f, nn).astype(jnp.bfloat16)
                wr[3 + f, kr] = weights(block, f, ne - 4).astype(jnp.bfloat16)
                wr[6 + f, kr] = weights(block, f, ne + 124).astype(jnp.bfloat16)

    @pl.when(at_x)
    def _():
        @pl.when(gy <= last)
        def _():
            remote(NB, rsum, rnb, here(0, 1)).wait_recv()

        @pl.when(gy > last)
        def _():
            remote(NB + 1, rsum, rnb, here(0, -1)).wait_recv()

        group_z = iota((NZ, 128), 1) >> 3
        rows = jnp.concatenate([jnp.concatenate([rsum[k], rnb[k]], axis=1) for k in range(3)], axis=0)
        for n in range(9):
            total = split_dot(rows, wr[n])
            slots = [total[NZ * k : NZ * k + NZ] for k in range(3)]
            strips = [sum(w * x for w, x in zip(SLOTS[r], slots) if w) for r in range(4)]
            if n < 3:
                for r in range(4):
                    for c in range(CHUNKS):
                        fr[c, n, r] = strips[r][c * ZC : (c + 1) * ZC]
            else:
                total = jnp.zeros((NZ, 128), F32)
                for r in range(4):
                    total = jnp.where(group_z == strip + r, strips[r], total)
                for c in range(CHUNKS):
                    hfr[c, n - 3] = total[c * ZC : (c + 1) * ZC]

    def complete(c, carry):
        for f in range(3):
            arrive(inside(s, 0), FIRST + 5 * c + f, hx.at[c, f, pl.ds(0, counts[f])], here(s, 0))
        assemble(c, False)
        late_columns(c)

        @pl.when(at_x)
        def _():
            for r in range(4):
                for f, (dest, base, _, _) in enumerate(spans):
                    dest[0, c, base + strip + r] = fr[c, f, r]
            pb[0, c, pl.ds(20 if s > 0 else 2, 2)] = jnp.zeros((2, ZC, 128), F32)
            strip_rows = (group_c >= strip) & (group_c < strip + 4)
            for f in range(3):
                for dest, region in ((qm, 0 if s > 0 else 1), (bm, 1 if s > 0 else 0)):
                    dest[c, f] = jnp.where(strip_rows, hfr[c, 3 * region + f], dest[c, f])

        lw, rw = windows(c)
        speed = window_speed(c)
        lw = [(jnp.where(ends_l, 0.0, m), jnp.where(ends_l, 0.0, x)) for m, x in lw]
        rw = [(jnp.where(ends_r, 0.0, m), jnp.where(ends_r, 0.0, x)) for m, x in rw]
        pl1, vl1 = window_step(lw, ends_l, speed)
        pr1, vr1 = window_step(rw, ends_r, speed)
        put_sides(sd, c, lw[0][0], rw[0][0], vl1, vr1)
        step(0, c, *late)
        arrive(inside(s, 0), round_slot(1, c), p_rows(1, c, far_side), here(s, 0))
        vl2, vr2 = new_v(pl1, vl1, ends_l), new_v(pr1, vr1, ends_r)
        put_sides(sd, c, pl1, pr1, vl2, vr2)
        wv[c] = jnp.where(e_c < 5, roll(vl2, 1), roll(vr2, 1))
        step(1, c, 0, BX)
        start(round_messages(2, c))
        return carry

    def window_speed(c):
        return sp[pl.ds(pl.multiple_of(c * ZC, ZC), ZC), :]

    lax.fori_loop(0, CHUNKS, complete, 0)

    def gather(r, c):
        receive(r, c)
        mine = ok[r, c]
        halo = jnp.where(e_c < 2, lr[r, c, 0], jnp.where(e_c < 4, lr[r, c, 1], wv[c]))
        halo = jnp.where(ends_y, 0.0, halo)
        slope = jnp.where(e_c == 4, roll(mine, 2) - roll(halo, 4), roll(halo, 2) - roll(mine, 4))
        wind = jnp.where(ends_y, 0.0, halo - 0.5 * slope)
        wv[c] = wind
        sd[c] = jnp.where(
            e_c == 0,
            roll(halo, -2),
            jnp.where(e_c == 1, halo, jnp.where(e_c == 2, roll(wind, -3), roll(wind, -1))),
        )

    def middle(c, carry):
        gather(2, c)
        step(2, c, 0, BX)
        start(round_messages(3, c))
        return carry

    lax.fori_loop(0, CHUNKS, middle, 0)

    def finish(c, carry):
        gather(3, c)
        step(3, c, 0, BX)
        for f in range(3):
            store(c, f).start()
        return carry

    lax.fori_loop(0, CHUNKS, finish, 0)

    sent(column_messages())
    sent(row_messages())
    sent(strip_messages())

    def settle(c, carry):
        sent(first_x(c))
        sent(first_y(c))
        sent(near_messages(c))
        for r in range(2, 4):
            sent(round_messages(r, c))
        for f in range(3):
            store(c, f).wait()
        return carry

    lax.fori_loop(0, CHUNKS, settle, 0)


def move(s, state, parent, stiffness, offsets):
    vmem = lambda *shape: pltpu.VMEM(shape, F32)
    sems = 14 + CHUNKS * 5 + 3 * CHUNKS * 4
    scratch = [
        vmem(3 * NZ * BX, 128),
        vmem(3 * PROWS, PCOLS, NZ),
        vmem(NZ, 128),
        vmem(CHUNKS, 3, BX, ZC, 128),
        vmem(CHUNKS, 3, 6, ZC, 128),
        vmem(CHUNKS, 3, ZC, 128),
        vmem(CHUNKS, 3, ZC, 128),
        vmem(CHUNKS, 3, TILES // 2, 8, 128),
        vmem(CHUNKS, 3, TILES // 2, 8, 128),
        vmem(CHUNKS, 3, ZC, 128),
        vmem(CHUNKS, 3, ZC, 128),
        vmem(4, CHUNKS, 24, ZC, 128),
        vmem(4, CHUNKS, 22, ZC, 128),
        vmem(4, CHUNKS, 20, ZC, 128),
        vmem(4, CHUNKS, ZC, 128),
        vmem(4, CHUNKS, 2, ZC, 128),
        vmem(CHUNKS, 3, ZC, 128),
        vmem(CHUNKS, 3, ZC, 128),
        vmem(CHUNKS, ZC, 128),
        vmem(CHUNKS, ZC, 128),
        vmem(CHUNKS, ZC, 128),
        vmem(3 * NZ * BX, 128),
        vmem(4, 128, 128),
        vmem(3, NZ, 128),
        vmem(2, 3, NZ, 128),
        vmem(3, NZ, 128),
        vmem(3, NZ, 128),
        pltpu.VMEM((9, 256, 128), jnp.bfloat16),
        vmem(CHUNKS, 3, 4, ZC, 128),
        vmem(CHUNKS, 6, ZC, 128),
        vmem(32, 128),
        vmem(4, 32, 128),
        pltpu.VMEM((3, 2, 512, 128), jnp.bfloat16),
        pltpu.SMEM((4,), jnp.int32),
        pltpu.SMEM((NZ,), F32),
        pltpu.SemaphoreType.DMA((CHUNKS, 3)),
        pltpu.SemaphoreType.DMA,
        pltpu.SemaphoreType.DMA((2,)),
        pltpu.SemaphoreType.DMA((CHUNKS, 3)),
        pltpu.SemaphoreType.DMA((sems,)),
        pltpu.SemaphoreType.DMA((sems,)),
    ]
    hbm = pl.BlockSpec(memory_space=pltpu.HBM)
    return pl.pallas_call(
        functools.partial(kernel, s),
        out_shape=jax.ShapeDtypeStruct((3 * NZ * BX, BY), F32),
        in_specs=[hbm, hbm, hbm, hbm],
        out_specs=hbm,
        scratch_shapes=scratch,
        compiler_params=pltpu.CompilerParams(
            collective_id=0 if s > 0 else 1, has_side_effects=True, vmem_limit_bytes=48 * 2**20
        ),
    )(offsets, stiffness, state, parent)


def per_device(state, parent, stiffness, offsets):
    flat = state.reshape(3 * NZ * BX, BY)
    cells = parent.transpose(0, 2, 3, 1).reshape(3 * PROWS, PCOLS, NZ)
    out = lax.cond(
        offsets[2] > 0, functools.partial(move, 1), functools.partial(move, -1), flat, cells, stiffness, offsets
    )
    return out.reshape(3, NZ, BX, BY)


def solution(mesh):
    return jax.shard_map(
        per_device,
        mesh=mesh,
        in_specs=(P(None, None, "gx", "gy"), P(None, None, "gx", "gy"), P(), P()),
        out_specs=P(None, None, "gx", "gy"),
        check_vma=False,
    )
```

```python
import functools

import jax
import jax.numpy as jnp
from jax import lax
from jax.experimental import pallas as pl
from jax.experimental.pallas import tpu as pltpu
from jax.sharding import PartitionSpec as P

MESH = pl.DeviceIdType.MESH
F32 = jnp.float32
GX, GY = 8, 16
NZ, BX, BY = 64, 16, 128
CHUNKS = 4
AHEAD = 2
ZC = NZ // CHUNKS
TILES = ZC // 8
PROWS, PCOLS = 6, 34
SLOTS = ((0.375, 0.625, 0.0), (0.125, 0.875, 0.0), (0.0, 0.875, 0.125), (0.0, 0.625, 0.375))


def roll(x, shift):
    shift = shift % 128
    return x if shift == 0 else pltpu.roll(x, shift, 1)


def iota(shape, dim):
    return lax.broadcasted_iota(jnp.int32, shape, dim)


def split_dot(a, b):
    high = a.astype(jnp.bfloat16)
    low = (a - high.astype(F32)).astype(jnp.bfloat16)
    both = jnp.dot(jnp.concatenate([high, low], axis=0), b, preferred_element_type=F32)
    return both[: a.shape[0]] + both[a.shape[0] :]


def bilinear(cell, lower, frac):
    return jnp.where(cell == lower, 1.0 - frac, 0.0) + jnp.where(cell == lower + 1, frac, 0.0)


def kernel(
    s,
    off_hbm,
    stiff_hbm,
    st_hbm,
    par_hbm,
    out_ref,
    st,
    pin,
    sp,
    own,
    hx,
    yp,
    lp,
    cp,
    cr,
    qm,
    qe,
    pb,
    ub,
    vb,
    ok,
    lr,
    bm,
    be,
    wv,
    sd,
    sx,
    tb,
    rsp,
    rsr,
    rsum,
    rnb,
    wr,
    fr,
    hfr,
    csm,
    csr,
    wc,
    off_ref,
    stiff_ref,
    in_sem,
    par_sem,
    smem_sem,
    send_sem,
    recv_sem,
):
    gx, gy = lax.axis_index("gx"), lax.axis_index("gy")
    here = lambda dx, dy: {"gx": gx + dx, "gy": gy + dy}
    inside = lambda dx, dy: (gx + dx >= 0) & (gx + dx < GX) & (gy + dy >= 0) & (gy + dy < GY)
    ex = GX - 1 if s > 0 else 0
    ey = 0 if s > 0 else GY - 1
    at_x, at_y = gx == ex, gy == ey
    last = 13 if s > 0 else 14

    def lo(d):
        return (2 * d) // 3

    def feeds(src, dst):
        return (src >= lo(dst)) & (src <= lo(dst) + 3) & (dst >= 0) & (dst < GX) & (src >= 0) & (src < GX)

    partners = [(dx, dy, inside(dx, dy)) for dx, dy in ((-1, 0), (1, 0), (0, -1), (0, 1), (-1, 1), (1, -1))]
    partners.append((2 * s, 0, gx == ex - 2 * s))
    partners.append((-2 * s, 0, at_x))
    for d in (-3, -2, 2, 3):
        partners.append((d, 0, at_y & (feeds(gx, gx + d) | feeds(gx + d, gx))))
    barrier = pltpu.get_barrier_semaphore()
    for dx, dy, cond in partners:

        @pl.when(cond)
        def _():
            pl.semaphore_signal(barrier, inc=1, device_id=here(dx, dy), device_id_type=MESH)

    def remote(slot, src, dst, device, recv_slot=None):
        return pltpu.make_async_remote_copy(
            src_ref=src,
            dst_ref=dst,
            send_sem=send_sem.at[slot],
            recv_sem=recv_sem.at[slot if recv_slot is None else recv_slot],
            device_id=device,
            device_id_type=MESH,
        )

    def start(messages):
        for cond, *copy in messages:

            @pl.when(cond)
            def _():
                remote(*copy).start()

    def sent(messages):
        for cond, *copy in messages:

            @pl.when(cond)
            def _():
                remote(*copy).wait_send()

    def arrive(cond, slot, ref, device):
        @pl.when(cond)
        def _():
            remote(slot, ref, ref, device).wait_recv()

    CS_RECV, CS_SEND, RS, NB, FIRST = 0, 4, 10, 12, 14
    ROUND = FIRST + 5 * CHUNKS
    counts = (6, 5, 4)

    def column_messages():
        return [
            (
                at_y & feeds(gx, gx + d),
                CS_SEND + k,
                csm,
                csr.at[gx - lo(gx + d)],
                here(d, 0),
                CS_RECV + gx - lo(gx + d),
            )
            for k, d in enumerate((-3, -2, -1, 1, 2, 3))
        ]

    def row_messages():
        return [(gx == ex - far * s, RS + k, rsp, rsr.at[k], here(far * s, 0)) for k, far in enumerate((2, 1))]

    def strip_messages():
        return [
            (at_x & (gy >= 1) & (gy - 1 <= last), NB, rsum, rnb, here(0, -1)),
            (at_x & (gy + 1 > last) & (gy + 1 < GY), NB + 1, rsum, rnb, here(0, 1)),
        ]

    def first_rows(f):
        return pl.ds(0 if s > 0 else BX - counts[f], counts[f])

    def first_x(c):
        return [
            (
                inside(-s, 0),
                FIRST + 5 * c + f,
                own.at[c, f, first_rows(f)],
                hx.at[c, f, pl.ds(0, counts[f])],
                here(-s, 0),
            )
            for f in range(3)
        ]

    def first_y(c):
        return [
            (inside(0, s), FIRST + 5 * c + 3, yp.at[c], lp.at[c], here(0, s)),
            (inside(-s, s), FIRST + 5 * c + 4, cp.at[c], cr.at[c], here(-s, s)),
        ]

    def p_rows(r, c, first):
        return pb.at[r, c, pl.ds(first + 4, 2)]

    near, far_side = (0, BX) if s > 0 else (BX - 2, -2)

    def near_messages(c):
        return [(inside(-s, 0), round_slot(1, c), p_rows(1, c, near), p_rows(1, c, far_side), here(-s, 0))]

    def round_slot(r, c):
        return ROUND + ((r - 1) * CHUNKS + c) * 4

    def round_messages(r, c):
        k = round_slot(r, c)
        return [
            (inside(-1, 0), k, p_rows(r, c, 0), p_rows(r, c, BX), here(-1, 0)),
            (inside(1, 0), k + 1, p_rows(r, c, BX - 2), p_rows(r, c, -2), here(1, 0)),
            (inside(0, -1), k + 2, ok.at[r, c], lr.at[r, c, 1], here(0, -1)),
            (inside(0, 1), k + 3, ok.at[r, c], lr.at[r, c, 0], here(0, 1)),
        ]

    def receive(r, c):
        k = round_slot(r, c)
        arrive(inside(1, 0), k, p_rows(r, c, BX), here(1, 0))
        arrive(inside(-1, 0), k + 1, p_rows(r, c, -2), here(-1, 0))
        arrive(inside(0, 1), k + 2, lr.at[r, c, 1], here(0, 1))
        arrive(inside(0, -1), k + 3, lr.at[r, c, 0], here(0, -1))

    def load(c):
        rows = pl.ds(c * ZC * BX, ZC * BX)
        return pltpu.make_async_copy(st_hbm.at[:, rows], st.at[:, rows], in_sem.at[c])

    def state_row(c, f, x):
        return st[f, pl.ds(c * ZC * BX + x, ZC, stride=BX), :]

    par_copy = pltpu.make_async_copy(par_hbm, pin, par_sem)
    load(0).start()
    par_copy.start()
    scalars = [
        pltpu.make_async_copy(off_hbm, off_ref, smem_sem.at[0]),
        pltpu.make_async_copy(stiff_hbm, stiff_ref, smem_sem.at[1]),
    ]
    for copy in scalars:
        copy.start()
    for c in range(1, CHUNKS):
        load(c).start()

    lane = iota((8, 128), 1)
    group, e = lane >> 3, lane & 7
    lane_c = iota((ZC, 128), 1)
    group_c, e_c = lane_c >> 3, lane_c & 7

    par_copy.wait()
    for copy in scalars:
        copy.wait()
    use_rows = (gx >= 5) if s > 0 else (gx <= 2)
    ox = off_ref[0]

    @pl.when(use_rows)
    def _():
        low = ox + 31 if s > 0 else ox - 2
        for k in range(3):
            tb[k] = jnp.zeros((128, 128), F32)
            weight = [jnp.where(PROWS * gx + row == low + k, 1.0, 0.0) for row in range(PROWS)]
            for f in range(3):
                tb[k, PCOLS * f : PCOLS * f + PCOLS, 0:NZ] = sum(
                    weight[row] * pin[PROWS * f + row] for row in range(PROWS)
                )
        for k in range(3):
            rsp[k] = jnp.transpose(tb[k])[0:NZ]

    sent_rows = [range(n) if s > 0 else range(BX - n, BX) for n in counts]
    for c in range(CHUNKS):
        load(c).wait()
        for f in range(3):
            for x in sent_rows[f]:
                own[c, f, x] = state_row(c, f, x)
        if c == 0:
            pl.semaphore_wait(barrier, sum(cond.astype(jnp.int32) for _, _, cond in partners))
            if s < 0:
                start(row_messages())
        if c < AHEAD:
            start(first_x(c))
        if c == 0 and s > 0:
            start(row_messages())

    def pack(c, carry):
        for f in range(3):
            packed = jnp.zeros((ZC, 128), F32)
            for x in range(BX):
                if x in sent_rows[f]:
                    row = own[c, f, x]
                else:
                    row = state_row(c, f, x)
                    own[c, f, x] = row
                packed = jnp.where(group_c == x, roll(row, 8 * x + (8 if s > 0 else 0)), packed)
            yp[c, f] = packed
            for q in range(TILES // 2):
                one, two = packed[16 * q : 16 * q + 8], packed[16 * q + 8 : 16 * q + 16]
                turn = 0 if s > 0 else 48
                cp[c, f, q] = jnp.where(lane < 64, roll(one, turn), roll(two, turn + 64))
        start(first_y(c))
        return carry

    lax.fori_loop(0, CHUNKS, pack, 0)

    @pl.when(at_y)
    def _():
        first_col = 27 if s > 0 else 30
        tb[3] = jnp.zeros((128, 128), F32)
        for row in range(PROWS):
            for f in range(3):
                at = 9 * row + 3 * f
                tb[3, at : at + 3, 0:NZ] = pin[PROWS * f + row, first_col : first_col + 3]
        turned = jnp.transpose(tb[3])
        csm[...] = turned[0:32] + roll(turned[32:64], 64)

    start(column_messages())

    sub = iota((8, 128), 0)
    for t in range(NZ // 8):
        value = jnp.zeros((8, 128), F32)
        for q in range(8):
            value = jnp.where(sub == q, stiff_ref[8 * t + q], value)
        sp[pl.ds(8 * t, 8), :] = 0.5 * value

    def ends(c, carry):
        for r in range(1, 4):

            @pl.when(gx == 0)
            def _():
                pb[r, c, 2:4] = jnp.zeros((2, ZC, 128), F32)

            @pl.when(gx == GX - 1)
            def _():
                pb[r, c, 20:22] = jnp.zeros((2, ZC, 128), F32)

            @pl.when(gy == 0)
            def _():
                lr[r, c, 0] = jnp.zeros((ZC, 128), F32)

            @pl.when(gy == GY - 1)
            def _():
                lr[r, c, 1] = jnp.zeros((ZC, 128), F32)

        return carry

    lax.fori_loop(0, CHUNKS, ends, 0)

    kk = iota((128, 128), 0)
    nn = iota((128, 128), 1)

    @pl.when(at_y)
    def _():
        krow = (kk * 57) >> 9
        krem = kk - 9 * krow
        kf = (krem >= 3).astype(jnp.int32) + (krem >= 6).astype(jnp.int32)
        ks = krem - 3 * kf
        ne = nn & 7
        col = (ne - 4) if s > 0 else ne
        wy = bilinear(ks, (2 * col + 5) >> 3, ((2 * col + 5) & 7).astype(F32) * 0.125)
        wy = jnp.where((col >= 0) & (col < 4) & (kk < 54), wy, 0.0)
        g = nn >> 3
        rows = (g, jnp.where(g < 2, g - 2, jnp.where(g < 4, g + 14, jnp.where(g < 6, g - 8 if s > 0 else g + 14, 0))))
        for k in range(4):
            for m in range(2):
                i = rows[m]
                lower = ox + s + 4 * gx + ((2 * i - 3) >> 3)
                wx = bilinear(PROWS * (lo(gx) + k) + krow, lower, ((2 * i - 3) & 7).astype(F32) * 0.125)
                for f in range(3):
                    wc[f, m, 128 * k : 128 * k + 128] = jnp.where(kf == f, wx * wy, 0.0).astype(jnp.bfloat16)

        for k in range(4):
            src = lo(gx) + k

            @pl.when(src == gx)
            def _():
                csr[k] = csm[...]

            @pl.when(src != gx)
            def _():
                remote(CS_RECV + k, csm, csr.at[k], here(src - gx, 0)).wait_recv()

        parts = [jnp.concatenate([csr[k], roll(csr[k], 64)], axis=0) for k in range(4)]
        column = jnp.concatenate(parts, axis=1)
        for f in range(3):
            for m, dest in enumerate((qm, qe)):
                total = split_dot(column, wc[f, m])
                for c in range(CHUNKS):
                    dest[c, f] = total[c * ZC : (c + 1) * ZC]

    edge = lane_c < 4 if s > 0 else lane_c >= 124
    strip = 12 if s > 0 else 0
    ends_x = ((gx == 0) & (lane_c < 16)) | ((gx == GX - 1) & (lane_c >= 16) & (lane_c < 32))
    ends_l, ends_r = (gy == 0) & (e_c < 4), (gy == GY - 1) & (e_c >= 4)
    ends_y = ((gy == 0) & ((e_c < 2) | (e_c == 4))) | ((gy == GY - 1) & ((e_c == 2) | (e_c == 3) | (e_c == 5)))
    spans = ((pb, 4, -4, 22), (ub, 3, -3, 20), (vb, 2, -2, 18)) if s > 0 else ((pb, 4, -2, 22), (ub, 3, -1, 20), (vb, 2, 0, 18))

    def held(i):
        return 0 <= i + 4 * s < BX

    def source(c, f, i):
        old = i + 4 * s
        if held(i):
            return own[c, f, old]
        return hx[c, f, old - BX if s > 0 else old + counts[f]]

    def extra_group(i):
        return {-4: 4, -3: 5, -2: 0, -1: 1, 16: 2, 17: 3, 18: 4, 19: 5}[i]

    def assemble(c, mine):
        for f, (dest, base, first, count) in enumerate(spans):
            main, extra = qm[c, f], qe[c, f]
            for i in range(first, first + count):
                if held(i) != mine:
                    continue
                if 0 <= i < BX:
                    side = roll(main, -(8 * i + 4))
                else:
                    side = roll(extra, -(8 * extra_group(i) + 4))
                dest[0, c, i + base] = jnp.where(edge, side, roll(source(c, f, i), 4 * s))

    def late_columns(c):
        for f, last_row in enumerate(((18, -2), (17, -1), (16, 0))):
            main, extra = bm[c, f], be[c, f]
            for i in range(12, last_row[0]) if s > 0 else range(last_row[1], 4):
                row = source(c, f, i)
                if 0 <= i < BX:
                    main = jnp.where(group_c == i, roll(row, 8 * i + (8 if s > 0 else 0)), main)
                else:
                    g = extra_group(i)
                    extra = jnp.where(group_c == g, roll(row, 8 * g + (8 if s > 0 else 0)), extra)
            bm[c, f] = main
            be[c, f] = extra

    def windows(c):
        q = [(qm[c, f], jnp.where(ends_x, 0.0, qe[c, f])) for f in range(3)]
        b = [(bm[c, f], jnp.where(ends_x, 0.0, be[c, f])) for f in range(3)]
        return (q, b) if s > 0 else (b, q)

    def new_v(p, v, ends):
        return jnp.where(ends, 0.0, v - 0.5 * (roll(p, -1) - roll(p, 1)))

    def put_sides(dest, c, pl_, pr_, vl_, vr_):
        dest[c] = jnp.where(
            e_c == 0, roll(pr_, -4), jnp.where(e_c == 1, roll(pl_, -2), jnp.where(e_c == 2, roll(vr_, -2), vl_))
        )

    def up(main, extra):
        return jnp.where(lane_c < 8, roll(extra, -8), roll(main, 8))

    def down(main, extra):
        return jnp.where(lane_c >= 120, roll(extra, 104), roll(main, -8))

    def window_step(fields, ends, speed):
        (p, px), (u, ux), (v, _) = fields
        u1 = u - 0.5 * (down(p, px) - up(p, px))
        slope = jnp.where(lane_c < 16, roll(p, 8) - roll(px, 8), roll(px, -8) - roll(p, 24))
        u1x = jnp.where(ends_x, 0.0, ux - 0.5 * slope)
        v1 = new_v(p, v, ends)
        p1 = p - speed * ((down(u1, u1x) - up(u1, u1x)) + (roll(v1, -1) - roll(v1, 1)))
        return jnp.where(ends, 0.0, p1), v1

    def step(r, c, first, count):
        final = isinstance(r, int) and r == 3
        packs = not final and not (isinstance(r, int) and r == 0)

        def tile(t):
            zr = pl.ds(8 * t, 8)
            side, extra = sd[c, zr], sx[c, zr]
            speed = sp[pl.ds(pl.multiple_of(c * ZC + 8 * t, 8), 8), :]
            p = {n: pb[r, c, n + 4, zr] for n in range(first - 2, first + count + 2)}
            u = {}
            for n in range(first - 1, first + count + 1):
                new = ub[r, c, n + 3, zr] - 0.5 * (p[n + 1] - p[n - 1])
                if n == -1:
                    new = jnp.where(gx == 0, 0.0, new)
                if n == BX:
                    new = jnp.where(gx == GX - 1, 0.0, new)
                u[n] = new
                mine = first <= n < first + count or (n == -1 and first == 0) or (n == BX and first + count == BX)
                if not final and mine and -1 <= n <= BX:
                    ub[r + 1, c, n + 3, zr] = new
            pack = jnp.zeros((8, 128), F32)
            for x in range(first, first + count):
                near_side, g = (side, x) if 0 <= x < BX else (extra, extra_group(x))
                side_p = roll(near_side, -(8 * g + 1))
                before = jnp.where(lane == 0, side_p, roll(p[x], 1))
                after = jnp.where(lane == 127, side_p, roll(p[x], -1))
                v = vb[r, c, x + 2, zr] - 0.5 * (after - before)
                side_v = roll(near_side, -(8 * g + 3))
                before = jnp.where(lane == 0, side_v, roll(v, 1))
                after = jnp.where(lane == 127, side_v, roll(v, -1))
                new_p = p[x] - speed * ((u[x + 1] - u[x - 1]) + (after - before))
                if x < 0:
                    new_p = jnp.where(gx == 0, 0.0, new_p)
                if x >= BX:
                    new_p = jnp.where(gx == GX - 1, 0.0, new_p)
                if final:
                    for f, value in enumerate((new_p, u[x], v)):
                        out_ref[pl.ds(f * NZ * BX + (c * ZC + 8 * t) * BX + x, 8, stride=BX), :] = value
                else:
                    pb[r + 1, c, x + 4, zr] = new_p
                    if 0 <= x < BX:
                        vb[r + 1, c, x + 2, zr] = v
                    if packs:
                        pack = jnp.where(group == x, roll(new_p, 8 * x + 2), pack)
            if packs:
                ok[r + 1, c, zr] = pack

        for t in range(TILES):
            tile(t)

    early, late = ((-2, 12), (10, 6)) if s > 0 else ((6, 12), (0, 6))

    def begin(c, carry):
        @pl.when(at_x & (c == CHUNKS // 2))
        def _():
            for k, far in enumerate((2, 1)):
                remote(RS + k, rsp, rsr.at[k], here(-far * s, 0)).wait_recv()
            for k in range(3):
                rsum[k] = rsp[k] + rsr[0, k] + rsr[1, k]
            start(strip_messages())

        arrive(inside(0, -s), FIRST + 5 * c + 3, lp.at[c], here(0, -s))
        arrive(inside(s, -s), FIRST + 5 * c + 4, cr.at[c], here(s, -s))

        @pl.when(jnp.logical_not(at_y))
        def _():
            for f in range(3):
                for t in range(TILES):
                    zr, w = pl.ds(8 * t, 8), t % 2
                    corner, side = cr[c, f, t // 2], lp[c, f, zr]
                    if s > 0:
                        qm[c, f, zr] = jnp.where(lane < 96, roll(side, -32), roll(corner, 96 - 64 * w))
                        qe[c, f, zr] = jnp.where(
                            lane < 16, roll(side, -16), jnp.where(lane < 32, roll(corner, -16 - 64 * w), roll(side, 32))
                        )
                    else:
                        qm[c, f, zr] = jnp.where(lane < 32, roll(corner, -16 - 64 * w), roll(side, 32))
                        qe[c, f, zr] = jnp.where(lane < 16, roll(corner, -64 * w), roll(side, -80))

        for f in range(3):
            mine = yp[c, f]
            bm[c, f] = roll(mine, -32 * s)
            be[c, f] = roll(mine, -16 if s > 0 else -80)
        assemble(c, True)

        @pl.when(gx == GX - 1 - ex)
        def _():
            pb[0, c, pl.ds(0 if s > 0 else 20, 4)] = jnp.zeros((4, ZC, 128), F32)

        lw, rw = windows(c)
        for dest, k in ((sd, 0), (sx, 1)):
            (pl_, vl_), (pr_, vr_) = [(w[0][k], w[2][k]) for w in (lw, rw)]
            pl_, pr_ = jnp.where(ends_l, 0.0, pl_), jnp.where(ends_r, 0.0, pr_)
            put_sides(dest, c, pl_, pr_, new_v(pl_, vl_, ends_l), new_v(pr_, vr_, ends_r))
        step(0, c, *early)
        start(near_messages(c))

        @pl.when(c + AHEAD < CHUNKS)
        def _():
            start(first_x(c + AHEAD))

        return carry

    lax.fori_loop(0, CHUNKS, begin, 0)

    @pl.when(at_x)
    def _():
        base = 28 if s > 0 else 30
        other = jnp.where(gy <= last, gy + 1, gy - 1)

        def weights(block, f, j):
            lower = base + 32 * gy + ((2 * j - 3) >> 3)
            frac = ((2 * j - 3) & 7).astype(F32) * 0.125
            valid = (kk >= PCOLS * f) & (kk < PCOLS * f + PCOLS)
            return jnp.where(valid, bilinear(PCOLS * block + kk - PCOLS * f, lower, frac), 0.0)

        ne = nn & 7
        for b, block in enumerate((gy, other)):
            kr = slice(128 * b, 128 * b + 128)
            for f in range(3):
                wr[f, kr] = weights(block, f, nn).astype(jnp.bfloat16)
                wr[3 + f, kr] = weights(block, f, ne - 4).astype(jnp.bfloat16)
                wr[6 + f, kr] = weights(block, f, ne + 124).astype(jnp.bfloat16)

    @pl.when(at_x)
    def _():
        @pl.when(gy <= last)
        def _():
            remote(NB, rsum, rnb, here(0, 1)).wait_recv()

        @pl.when(gy > last)
        def _():
            remote(NB + 1, rsum, rnb, here(0, -1)).wait_recv()

        group_z = iota((NZ, 128), 1) >> 3
        rows = jnp.concatenate([jnp.concatenate([rsum[k], rnb[k]], axis=1) for k in range(3)], axis=0)
        for n in range(9):
            total = split_dot(rows, wr[n])
            slots = [total[NZ * k : NZ * k + NZ] for k in range(3)]
            strips = [sum(w * x for w, x in zip(SLOTS[r], slots) if w) for r in range(4)]
            if n < 3:
                for r in range(4):
                    for c in range(CHUNKS):
                        fr[c, n, r] = strips[r][c * ZC : (c + 1) * ZC]
            else:
                total = jnp.zeros((NZ, 128), F32)
                for r in range(4):
                    total = jnp.where(group_z == strip + r, strips[r], total)
                for c in range(CHUNKS):
                    hfr[c, n - 3] = total[c * ZC : (c + 1) * ZC]

    def complete(c, carry):
        for f in range(3):
            arrive(inside(s, 0), FIRST + 5 * c + f, hx.at[c, f, pl.ds(0, counts[f])], here(s, 0))
        assemble(c, False)
        late_columns(c)

        @pl.when(at_x)
        def _():
            for r in range(4):
                for f, (dest, base, _, _) in enumerate(spans):
                    dest[0, c, base + strip + r] = fr[c, f, r]
            pb[0, c, pl.ds(20 if s > 0 else 2, 2)] = jnp.zeros((2, ZC, 128), F32)
            strip_rows = (group_c >= strip) & (group_c < strip + 4)
            for f in range(3):
                for dest, region in ((qm, 0 if s > 0 else 1), (bm, 1 if s > 0 else 0)):
                    dest[c, f] = jnp.where(strip_rows, hfr[c, 3 * region + f], dest[c, f])

        lw, rw = windows(c)
        speed = window_speed(c)
        lw = [(jnp.where(ends_l, 0.0, m), jnp.where(ends_l, 0.0, x)) for m, x in lw]
        rw = [(jnp.where(ends_r, 0.0, m), jnp.where(ends_r, 0.0, x)) for m, x in rw]
        pl1, vl1 = window_step(lw, ends_l, speed)
        pr1, vr1 = window_step(rw, ends_r, speed)
        put_sides(sd, c, lw[0][0], rw[0][0], vl1, vr1)
        step(0, c, *late)
        arrive(inside(s, 0), round_slot(1, c), p_rows(1, c, far_side), here(s, 0))
        vl2, vr2 = new_v(pl1, vl1, ends_l), new_v(pr1, vr1, ends_r)
        put_sides(sd, c, pl1, pr1, vl2, vr2)
        wv[c] = jnp.where(e_c < 5, roll(vl2, 1), roll(vr2, 1))
        step(1, c, 0, BX)
        start(round_messages(2, c))
        return carry

    def window_speed(c):
        return sp[pl.ds(pl.multiple_of(c * ZC, ZC), ZC), :]

    lax.fori_loop(0, CHUNKS, complete, 0)

    def gather(r, c):
        receive(r, c)
        mine = ok[r, c]
        halo = jnp.where(e_c < 2, lr[r, c, 0], jnp.where(e_c < 4, lr[r, c, 1], wv[c]))
        halo = jnp.where(ends_y, 0.0, halo)
        slope = jnp.where(e_c == 4, roll(mine, 2) - roll(halo, 4), roll(halo, 2) - roll(mine, 4))
        wind = jnp.where(ends_y, 0.0, halo - 0.5 * slope)
        wv[c] = wind
        sd[c] = jnp.where(
            e_c == 0,
            roll(halo, -2),
            jnp.where(e_c == 1, halo, jnp.where(e_c == 2, roll(wind, -3), roll(wind, -1))),
        )

    def middle(c, carry):
        gather(2, c)
        step(2, c, 0, BX)
        start(round_messages(3, c))
        return carry

    lax.fori_loop(0, CHUNKS, middle, 0)

    def finish(c, carry):
        gather(3, c)
        step(3, c, 0, BX)
        return carry

    lax.fori_loop(0, CHUNKS, finish, 0)

    sent(column_messages())
    sent(row_messages())
    sent(strip_messages())

    def settle(c, carry):
        sent(first_x(c))
        sent(first_y(c))
        sent(near_messages(c))
        for r in range(2, 4):
            sent(round_messages(r, c))
        return carry

    lax.fori_loop(0, CHUNKS, settle, 0)


def move(s, state, parent, stiffness, offsets):
    vmem = lambda *shape: pltpu.VMEM(shape, F32)
    sems = 14 + CHUNKS * 5 + 3 * CHUNKS * 4
    scratch = [
        vmem(3, NZ * BX, 128),
        vmem(3 * PROWS, PCOLS, NZ),
        vmem(NZ, 128),
        vmem(CHUNKS, 3, BX, ZC, 128),
        vmem(CHUNKS, 3, 6, ZC, 128),
        vmem(CHUNKS, 3, ZC, 128),
        vmem(CHUNKS, 3, ZC, 128),
        vmem(CHUNKS, 3, TILES // 2, 8, 128),
        vmem(CHUNKS, 3, TILES // 2, 8, 128),
        vmem(CHUNKS, 3, ZC, 128),
        vmem(CHUNKS, 3, ZC, 128),
        vmem(4, CHUNKS, 24, ZC, 128),
        vmem(4, CHUNKS, 22, ZC, 128),
        vmem(4, CHUNKS, 20, ZC, 128),
        vmem(4, CHUNKS, ZC, 128),
        vmem(4, CHUNKS, 2, ZC, 128),
        vmem(CHUNKS, 3, ZC, 128),
        vmem(CHUNKS, 3, ZC, 128),
        vmem(CHUNKS, ZC, 128),
        vmem(CHUNKS, ZC, 128),
        vmem(CHUNKS, ZC, 128),
        vmem(4, 128, 128),
        vmem(3, NZ, 128),
        vmem(2, 3, NZ, 128),
        vmem(3, NZ, 128),
        vmem(3, NZ, 128),
        pltpu.VMEM((9, 256, 128), jnp.bfloat16),
        vmem(CHUNKS, 3, 4, ZC, 128),
        vmem(CHUNKS, 6, ZC, 128),
        vmem(32, 128),
        vmem(4, 32, 128),
        pltpu.VMEM((3, 2, 512, 128), jnp.bfloat16),
        pltpu.SMEM((4,), jnp.int32),
        pltpu.SMEM((NZ,), F32),
        pltpu.SemaphoreType.DMA((CHUNKS,)),
        pltpu.SemaphoreType.DMA,
        pltpu.SemaphoreType.DMA((2,)),
        pltpu.SemaphoreType.DMA((sems,)),
        pltpu.SemaphoreType.DMA((sems,)),
    ]
    hbm = pl.BlockSpec(memory_space=pltpu.HBM)
    return pl.pallas_call(
        functools.partial(kernel, s),
        out_shape=jax.ShapeDtypeStruct((3 * NZ * BX, BY), F32),
        in_specs=[hbm, hbm, hbm, hbm],
        out_specs=pl.BlockSpec(memory_space=pltpu.VMEM),
        scratch_shapes=scratch,
        compiler_params=pltpu.CompilerParams(
            collective_id=0 if s > 0 else 1, has_side_effects=True, vmem_limit_bytes=48 * 2**20
        ),
    )(offsets, stiffness, state, parent)


def per_device(state, parent, stiffness, offsets):
    flat = state.reshape(3, NZ * BX, BY)
    cells = parent.transpose(0, 2, 3, 1).reshape(3 * PROWS, PCOLS, NZ)
    out = lax.cond(
        offsets[2] > 0, functools.partial(move, 1), functools.partial(move, -1), flat, cells, stiffness, offsets
    )
    return out.reshape(3, NZ, BX, BY)


def solution(mesh):
    return jax.shard_map(
        per_device,
        mesh=mesh,
        in_specs=(P(None, None, "gx", "gy"), P(None, None, "gx", "gy"), P(), P()),
        out_specs=P(None, None, "gx", "gy"),
        check_vma=False,
    )
```

```python
import functools

import jax
import jax.numpy as jnp
from jax import lax
from jax.experimental import pallas as pl
from jax.experimental.pallas import tpu as pltpu
from jax.sharding import PartitionSpec as P

MESH = pl.DeviceIdType.MESH
F32 = jnp.float32
GX, GY = 8, 16
NZ, BX, BY = 64, 16, 128
CHUNKS = 4
AHEAD = 2
ZC = NZ // CHUNKS
TILES = ZC // 8
PROWS, PCOLS = 6, 34
SLOTS = ((0.375, 0.625, 0.0), (0.125, 0.875, 0.0), (0.0, 0.875, 0.125), (0.0, 0.625, 0.375))


def roll(x, shift):
    shift = shift % 128
    return x if shift == 0 else pltpu.roll(x, shift, 1)


def iota(shape, dim):
    return lax.broadcasted_iota(jnp.int32, shape, dim)


def split_dot(a, b):
    high = a.astype(jnp.bfloat16)
    low = (a - high.astype(F32)).astype(jnp.bfloat16)
    both = jnp.dot(jnp.concatenate([high, low], axis=0), b, preferred_element_type=F32)
    return both[: a.shape[0]] + both[a.shape[0] :]


def bilinear(cell, lower, frac):
    return jnp.where(cell == lower, 1.0 - frac, 0.0) + jnp.where(cell == lower + 1, frac, 0.0)


def kernel(
    s,
    off_hbm,
    stiff_hbm,
    st_hbm,
    par_hbm,
    out_ref,
    st,
    pin,
    sp,
    own,
    hs,
    hx,
    yp,
    lp,
    cp,
    cr,
    qm,
    qe,
    pb,
    ub,
    vb,
    ok,
    lr,
    bm,
    be,
    wv,
    sd,
    sx,
    tb,
    rsp,
    rsr,
    rsum,
    rnb,
    wr,
    fr,
    hfr,
    csm,
    csr,
    wc,
    off_ref,
    stiff_ref,
    in_sem,
    par_sem,
    smem_sem,
    send_sem,
    recv_sem,
):
    gx, gy = lax.axis_index("gx"), lax.axis_index("gy")
    here = lambda dx, dy: {"gx": gx + dx, "gy": gy + dy}
    inside = lambda dx, dy: (gx + dx >= 0) & (gx + dx < GX) & (gy + dy >= 0) & (gy + dy < GY)
    ex = GX - 1 if s > 0 else 0
    ey = 0 if s > 0 else GY - 1
    at_x, at_y = gx == ex, gy == ey
    last = 13 if s > 0 else 14

    def lo(d):
        return (2 * d) // 3

    def feeds(src, dst):
        return (src >= lo(dst)) & (src <= lo(dst) + 3) & (dst >= 0) & (dst < GX) & (src >= 0) & (src < GX)

    partners = [(dx, dy, inside(dx, dy)) for dx, dy in ((-1, 0), (1, 0), (0, -1), (0, 1), (-1, 1), (1, -1))]
    partners.append((2 * s, 0, gx == ex - 2 * s))
    partners.append((-2 * s, 0, at_x))
    for d in (-3, -2, 2, 3):
        partners.append((d, 0, at_y & (feeds(gx, gx + d) | feeds(gx + d, gx))))
    barrier = pltpu.get_barrier_semaphore()
    for dx, dy, cond in partners:

        @pl.when(cond)
        def _():
            pl.semaphore_signal(barrier, inc=1, device_id=here(dx, dy), device_id_type=MESH)

    def remote(slot, src, dst, device, recv_slot=None):
        return pltpu.make_async_remote_copy(
            src_ref=src,
            dst_ref=dst,
            send_sem=send_sem.at[slot],
            recv_sem=recv_sem.at[slot if recv_slot is None else recv_slot],
            device_id=device,
            device_id_type=MESH,
        )

    def start(messages):
        for cond, *copy in messages:

            @pl.when(cond)
            def _():
                remote(*copy).start()

    def sent(messages):
        for cond, *copy in messages:

            @pl.when(cond)
            def _():
                remote(*copy).wait_send()

    def arrive(cond, slot, ref, device):
        @pl.when(cond)
        def _():
            remote(slot, ref, ref, device).wait_recv()

    CS_RECV, CS_SEND, RS, NB, FIRST = 0, 4, 10, 12, 14
    ROUND = FIRST + 5 * CHUNKS
    counts, starts = (6, 5, 4), (0, 6, 11)

    def column_messages():
        return [
            (
                at_y & feeds(gx, gx + d),
                CS_SEND + k,
                csm,
                csr.at[gx - lo(gx + d)],
                here(d, 0),
                CS_RECV + gx - lo(gx + d),
            )
            for k, d in enumerate((-3, -2, -1, 1, 2, 3))
        ]

    def row_messages():
        return [(gx == ex - far * s, RS + k, rsp, rsr.at[k], here(far * s, 0)) for k, far in enumerate((2, 1))]

    def strip_messages():
        return [
            (at_x & (gy >= 1) & (gy - 1 <= last), NB, rsum, rnb, here(0, -1)),
            (at_x & (gy + 1 > last) & (gy + 1 < GY), NB + 1, rsum, rnb, here(0, 1)),
        ]

    def first_x(c):
        return [(inside(-s, 0), FIRST + 5 * c, hs.at[c], hx.at[c], here(-s, 0))]

    def first_y(c):
        return [
            (inside(0, s), FIRST + 5 * c + 3, yp.at[c], lp.at[c], here(0, s)),
            (inside(-s, s), FIRST + 5 * c + 4, cp.at[c], cr.at[c], here(-s, s)),
        ]

    def p_rows(r, c, first):
        return pb.at[r, c, pl.ds(first + 4, 2)]

    near, far_side = (0, BX) if s > 0 else (BX - 2, -2)

    def near_messages(c):
        return [(inside(-s, 0), round_slot(1, c), p_rows(1, c, near), p_rows(1, c, far_side), here(-s, 0))]

    def round_slot(r, c):
        return ROUND + ((r - 1) * CHUNKS + c) * 4

    def round_messages(r, c):
        k = round_slot(r, c)
        return [
            (inside(-1, 0), k, p_rows(r, c, 0), p_rows(r, c, BX), here(-1, 0)),
            (inside(1, 0), k + 1, p_rows(r, c, BX - 2), p_rows(r, c, -2), here(1, 0)),
            (inside(0, -1), k + 2, ok.at[r, c], lr.at[r, c, 1], here(0, -1)),
            (inside(0, 1), k + 3, ok.at[r, c], lr.at[r, c, 0], here(0, 1)),
        ]

    def receive(r, c):
        k = round_slot(r, c)
        arrive(inside(1, 0), k, p_rows(r, c, BX), here(1, 0))
        arrive(inside(-1, 0), k + 1, p_rows(r, c, -2), here(-1, 0))
        arrive(inside(0, 1), k + 2, lr.at[r, c, 1], here(0, 1))
        arrive(inside(0, -1), k + 3, lr.at[r, c, 0], here(0, -1))

    def load(c):
        rows = pl.ds(c * ZC * BX, ZC * BX)
        return pltpu.make_async_copy(st_hbm.at[:, rows], st.at[:, rows], in_sem.at[c])

    def state_row(c, f, x):
        return st[f, pl.ds(c * ZC * BX + x, ZC, stride=BX), :]

    par_copy = pltpu.make_async_copy(par_hbm, pin, par_sem)
    load(0).start()
    par_copy.start()
    scalars = [
        pltpu.make_async_copy(off_hbm, off_ref, smem_sem.at[0]),
        pltpu.make_async_copy(stiff_hbm, stiff_ref, smem_sem.at[1]),
    ]
    for copy in scalars:
        copy.start()
    for c in range(1, CHUNKS):
        load(c).start()

    lane = iota((8, 128), 1)
    group, e = lane >> 3, lane & 7
    lane_c = iota((ZC, 128), 1)
    group_c, e_c = lane_c >> 3, lane_c & 7

    par_copy.wait()
    for copy in scalars:
        copy.wait()
    use_rows = (gx >= 5) if s > 0 else (gx <= 2)
    ox = off_ref[0]

    @pl.when(use_rows)
    def _():
        low = ox + 31 if s > 0 else ox - 2
        for k in range(3):
            tb[k] = jnp.zeros((128, 128), F32)
            weight = [jnp.where(PROWS * gx + row == low + k, 1.0, 0.0) for row in range(PROWS)]
            for f in range(3):
                tb[k, PCOLS * f : PCOLS * f + PCOLS, 0:NZ] = sum(
                    weight[row] * pin[PROWS * f + row] for row in range(PROWS)
                )
        for k in range(3):
            rsp[k] = jnp.transpose(tb[k])[0:NZ]

    sent_rows = [range(n) if s > 0 else range(BX - n, BX) for n in counts]
    for c in range(CHUNKS):
        load(c).wait()
        for f in range(3):
            for n, x in enumerate(sent_rows[f]):
                hs[c, starts[f] + n] = state_row(c, f, x)
        if c == 0:
            pl.semaphore_wait(barrier, sum(cond.astype(jnp.int32) for _, _, cond in partners))
            if s < 0:
                start(row_messages())
        if c < AHEAD:
            start(first_x(c))
        if c == 0 and s > 0:
            start(row_messages())

    def pack(c, carry):
        for f in range(3):
            packed = jnp.zeros((ZC, 128), F32)
            for x in range(BX):
                row = state_row(c, f, x)
                own[c, f, x] = row
                packed = jnp.where(group_c == x, roll(row, 8 * x + (8 if s > 0 else 0)), packed)
            yp[c, f] = packed
            for q in range(TILES // 2):
                one, two = packed[16 * q : 16 * q + 8], packed[16 * q + 8 : 16 * q + 16]
                turn = 0 if s > 0 else 48
                cp[c, f, q] = jnp.where(lane < 64, roll(one, turn), roll(two, turn + 64))
        start(first_y(c))
        return carry

    lax.fori_loop(0, CHUNKS, pack, 0)

    @pl.when(at_y)
    def _():
        first_col = 27 if s > 0 else 30
        tb[3] = jnp.zeros((128, 128), F32)
        for row in range(PROWS):
            for f in range(3):
                at = 9 * row + 3 * f
                tb[3, at : at + 3, 0:NZ] = pin[PROWS * f + row, first_col : first_col + 3]
        turned = jnp.transpose(tb[3])
        csm[...] = turned[0:32] + roll(turned[32:64], 64)

    start(column_messages())

    sub = iota((8, 128), 0)
    for t in range(NZ // 8):
        value = jnp.zeros((8, 128), F32)
        for q in range(8):
            value = jnp.where(sub == q, stiff_ref[8 * t + q], value)
        sp[pl.ds(8 * t, 8), :] = 0.5 * value

    def ends(c, carry):
        for r in range(1, 4):

            @pl.when(gx == 0)
            def _():
                pb[r, c, 2:4] = jnp.zeros((2, ZC, 128), F32)

            @pl.when(gx == GX - 1)
            def _():
                pb[r, c, 20:22] = jnp.zeros((2, ZC, 128), F32)

            @pl.when(gy == 0)
            def _():
                lr[r, c, 0] = jnp.zeros((ZC, 128), F32)

            @pl.when(gy == GY - 1)
            def _():
                lr[r, c, 1] = jnp.zeros((ZC, 128), F32)

        return carry

    lax.fori_loop(0, CHUNKS, ends, 0)

    kk = iota((128, 128), 0)
    nn = iota((128, 128), 1)

    @pl.when(at_y)
    def _():
        krow = (kk * 57) >> 9
        krem = kk - 9 * krow
        kf = (krem >= 3).astype(jnp.int32) + (krem >= 6).astype(jnp.int32)
        ks = krem - 3 * kf
        ne = nn & 7
        col = (ne - 4) if s > 0 else ne
        wy = bilinear(ks, (2 * col + 5) >> 3, ((2 * col + 5) & 7).astype(F32) * 0.125)
        wy = jnp.where((col >= 0) & (col < 4) & (kk < 54), wy, 0.0)
        g = nn >> 3
        rows = (g, jnp.where(g < 2, g - 2, jnp.where(g < 4, g + 14, jnp.where(g < 6, g - 8 if s > 0 else g + 14, 0))))
        for k in range(4):
            for m in range(2):
                i = rows[m]
                lower = ox + s + 4 * gx + ((2 * i - 3) >> 3)
                wx = bilinear(PROWS * (lo(gx) + k) + krow, lower, ((2 * i - 3) & 7).astype(F32) * 0.125)
                for f in range(3):
                    wc[f, m, 128 * k : 128 * k + 128] = jnp.where(kf == f, wx * wy, 0.0).astype(jnp.bfloat16)

        for k in range(4):
            src = lo(gx) + k

            @pl.when(src == gx)
            def _():
                csr[k] = csm[...]

            @pl.when(src != gx)
            def _():
                remote(CS_RECV + k, csm, csr.at[k], here(src - gx, 0)).wait_recv()

        parts = [jnp.concatenate([csr[k], roll(csr[k], 64)], axis=0) for k in range(4)]
        column = jnp.concatenate(parts, axis=1)
        for f in range(3):
            for m, dest in enumerate((qm, qe)):
                total = split_dot(column, wc[f, m])
                for c in range(CHUNKS):
                    dest[c, f] = total[c * ZC : (c + 1) * ZC]

    edge = lane_c < 4 if s > 0 else lane_c >= 124
    strip = 12 if s > 0 else 0
    ends_x = ((gx == 0) & (lane_c < 16)) | ((gx == GX - 1) & (lane_c >= 16) & (lane_c < 32))
    ends_l, ends_r = (gy == 0) & (e_c < 4), (gy == GY - 1) & (e_c >= 4)
    ends_y = ((gy == 0) & ((e_c < 2) | (e_c == 4))) | ((gy == GY - 1) & ((e_c == 2) | (e_c == 3) | (e_c == 5)))
    spans = ((pb, 4, -4, 22), (ub, 3, -3, 20), (vb, 2, -2, 18)) if s > 0 else ((pb, 4, -2, 22), (ub, 3, -1, 20), (vb, 2, 0, 18))

    def held(i):
        return 0 <= i + 4 * s < BX

    def source(c, f, i):
        old = i + 4 * s
        if held(i):
            return own[c, f, old]
        return hx[c, starts[f] + (old - BX if s > 0 else old + counts[f])]

    def extra_group(i):
        return {-4: 4, -3: 5, -2: 0, -1: 1, 16: 2, 17: 3, 18: 4, 19: 5}[i]

    def assemble(c, mine):
        for f, (dest, base, first, count) in enumerate(spans):
            main, extra = qm[c, f], qe[c, f]
            for i in range(first, first + count):
                if held(i) != mine:
                    continue
                if 0 <= i < BX:
                    side = roll(main, -(8 * i + 4))
                else:
                    side = roll(extra, -(8 * extra_group(i) + 4))
                dest[0, c, i + base] = jnp.where(edge, side, roll(source(c, f, i), 4 * s))

    def late_columns(c):
        for f, last_row in enumerate(((18, -2), (17, -1), (16, 0))):
            main, extra = bm[c, f], be[c, f]
            for i in range(12, last_row[0]) if s > 0 else range(last_row[1], 4):
                row = source(c, f, i)
                if 0 <= i < BX:
                    main = jnp.where(group_c == i, roll(row, 8 * i + (8 if s > 0 else 0)), main)
                else:
                    g = extra_group(i)
                    extra = jnp.where(group_c == g, roll(row, 8 * g + (8 if s > 0 else 0)), extra)
            bm[c, f] = main
            be[c, f] = extra

    def windows(c):
        q = [(qm[c, f], jnp.where(ends_x, 0.0, qe[c, f])) for f in range(3)]
        b = [(bm[c, f], jnp.where(ends_x, 0.0, be[c, f])) for f in range(3)]
        return (q, b) if s > 0 else (b, q)

    def new_v(p, v, ends):
        return jnp.where(ends, 0.0, v - 0.5 * (roll(p, -1) - roll(p, 1)))

    def put_sides(dest, c, pl_, pr_, vl_, vr_):
        dest[c] = jnp.where(
            e_c == 0, roll(pr_, -4), jnp.where(e_c == 1, roll(pl_, -2), jnp.where(e_c == 2, roll(vr_, -2), vl_))
        )

    def up(main, extra):
        return jnp.where(lane_c < 8, roll(extra, -8), roll(main, 8))

    def down(main, extra):
        return jnp.where(lane_c >= 120, roll(extra, 104), roll(main, -8))

    def window_step(fields, ends, speed):
        (p, px), (u, ux), (v, _) = fields
        u1 = u - 0.5 * (down(p, px) - up(p, px))
        slope = jnp.where(lane_c < 16, roll(p, 8) - roll(px, 8), roll(px, -8) - roll(p, 24))
        u1x = jnp.where(ends_x, 0.0, ux - 0.5 * slope)
        v1 = new_v(p, v, ends)
        p1 = p - speed * ((down(u1, u1x) - up(u1, u1x)) + (roll(v1, -1) - roll(v1, 1)))
        return jnp.where(ends, 0.0, p1), v1

    def step(r, c, first, count):
        final = isinstance(r, int) and r == 3
        packs = not final and not (isinstance(r, int) and r == 0)

        def tile(t):
            zr = pl.ds(8 * t, 8)
            side, extra = sd[c, zr], sx[c, zr]
            speed = sp[pl.ds(pl.multiple_of(c * ZC + 8 * t, 8), 8), :]
            p = {n: pb[r, c, n + 4, zr] for n in range(first - 2, first + count + 2)}
            u = {}
            for n in range(first - 1, first + count + 1):
                new = ub[r, c, n + 3, zr] - 0.5 * (p[n + 1] - p[n - 1])
                if n == -1:
                    new = jnp.where(gx == 0, 0.0, new)
                if n == BX:
                    new = jnp.where(gx == GX - 1, 0.0, new)
                u[n] = new
                mine = first <= n < first + count or (n == -1 and first == 0) or (n == BX and first + count == BX)
                if not final and mine and -1 <= n <= BX:
                    ub[r + 1, c, n + 3, zr] = new
            pack = jnp.zeros((8, 128), F32)
            for x in range(first, first + count):
                near_side, g = (side, x) if 0 <= x < BX else (extra, extra_group(x))
                side_p = roll(near_side, -(8 * g + 1))
                before = jnp.where(lane == 0, side_p, roll(p[x], 1))
                after = jnp.where(lane == 127, side_p, roll(p[x], -1))
                v = vb[r, c, x + 2, zr] - 0.5 * (after - before)
                side_v = roll(near_side, -(8 * g + 3))
                before = jnp.where(lane == 0, side_v, roll(v, 1))
                after = jnp.where(lane == 127, side_v, roll(v, -1))
                new_p = p[x] - speed * ((u[x + 1] - u[x - 1]) + (after - before))
                if x < 0:
                    new_p = jnp.where(gx == 0, 0.0, new_p)
                if x >= BX:
                    new_p = jnp.where(gx == GX - 1, 0.0, new_p)
                if final:
                    for f, value in enumerate((new_p, u[x], v)):
                        out_ref[pl.ds(f * NZ * BX + (c * ZC + 8 * t) * BX + x, 8, stride=BX), :] = value
                else:
                    pb[r + 1, c, x + 4, zr] = new_p
                    if 0 <= x < BX:
                        vb[r + 1, c, x + 2, zr] = v
                    if packs:
                        pack = jnp.where(group == x, roll(new_p, 8 * x + 2), pack)
            if packs:
                ok[r + 1, c, zr] = pack

        for t in range(TILES):
            tile(t)

    early, late = ((-2, 12), (10, 6)) if s > 0 else ((6, 12), (0, 6))

    def begin(c, carry):
        @pl.when(at_x & (c == CHUNKS // 2))
        def _():
            for k, far in enumerate((2, 1)):
                remote(RS + k, rsp, rsr.at[k], here(-far * s, 0)).wait_recv()
            for k in range(3):
                rsum[k] = rsp[k] + rsr[0, k] + rsr[1, k]
            start(strip_messages())

        arrive(inside(0, -s), FIRST + 5 * c + 3, lp.at[c], here(0, -s))
        arrive(inside(s, -s), FIRST + 5 * c + 4, cr.at[c], here(s, -s))

        @pl.when(jnp.logical_not(at_y))
        def _():
            for f in range(3):
                for t in range(TILES):
                    zr, w = pl.ds(8 * t, 8), t % 2
                    corner, side = cr[c, f, t // 2], lp[c, f, zr]
                    if s > 0:
                        qm[c, f, zr] = jnp.where(lane < 96, roll(side, -32), roll(corner, 96 - 64 * w))
                        qe[c, f, zr] = jnp.where(
                            lane < 16, roll(side, -16), jnp.where(lane < 32, roll(corner, -16 - 64 * w), roll(side, 32))
                        )
                    else:
                        qm[c, f, zr] = jnp.where(lane < 32, roll(corner, -16 - 64 * w), roll(side, 32))
                        qe[c, f, zr] = jnp.where(lane < 16, roll(corner, -64 * w), roll(side, -80))

        for f in range(3):
            mine = yp[c, f]
            bm[c, f] = roll(mine, -32 * s)
            be[c, f] = roll(mine, -16 if s > 0 else -80)
        assemble(c, True)

        @pl.when(gx == GX - 1 - ex)
        def _():
            pb[0, c, pl.ds(0 if s > 0 else 20, 4)] = jnp.zeros((4, ZC, 128), F32)

        lw, rw = windows(c)
        for dest, k in ((sd, 0), (sx, 1)):
            (pl_, vl_), (pr_, vr_) = [(w[0][k], w[2][k]) for w in (lw, rw)]
            pl_, pr_ = jnp.where(ends_l, 0.0, pl_), jnp.where(ends_r, 0.0, pr_)
            put_sides(dest, c, pl_, pr_, new_v(pl_, vl_, ends_l), new_v(pr_, vr_, ends_r))
        step(0, c, *early)
        start(near_messages(c))

        @pl.when(c == 0)
        def _():
            start(first_x(2))

        @pl.when(c == 2)
        def _():
            start(first_x(3))

        return carry

    lax.fori_loop(0, CHUNKS, begin, 0)

    @pl.when(at_x)
    def _():
        base = 28 if s > 0 else 30
        other = jnp.where(gy <= last, gy + 1, gy - 1)

        def weights(block, f, j):
            lower = base + 32 * gy + ((2 * j - 3) >> 3)
            frac = ((2 * j - 3) & 7).astype(F32) * 0.125
            valid = (kk >= PCOLS * f) & (kk < PCOLS * f + PCOLS)
            return jnp.where(valid, bilinear(PCOLS * block + kk - PCOLS * f, lower, frac), 0.0)

        ne = nn & 7
        for b, block in enumerate((gy, other)):
            kr = slice(128 * b, 128 * b + 128)
            for f in range(3):
                wr[f, kr] = weights(block, f, nn).astype(jnp.bfloat16)
                wr[3 + f, kr] = weights(block, f, ne - 4).astype(jnp.bfloat16)
                wr[6 + f, kr] = weights(block, f, ne + 124).astype(jnp.bfloat16)

    @pl.when(at_x)
    def _():
        @pl.when(gy <= last)
        def _():
            remote(NB, rsum, rnb, here(0, 1)).wait_recv()

        @pl.when(gy > last)
        def _():
            remote(NB + 1, rsum, rnb, here(0, -1)).wait_recv()

        group_z = iota((NZ, 128), 1) >> 3
        rows = jnp.concatenate([jnp.concatenate([rsum[k], rnb[k]], axis=1) for k in range(3)], axis=0)
        for n in range(9):
            total = split_dot(rows, wr[n])
            slots = [total[NZ * k : NZ * k + NZ] for k in range(3)]
            strips = [sum(w * x for w, x in zip(SLOTS[r], slots) if w) for r in range(4)]
            if n < 3:
                for r in range(4):
                    for c in range(CHUNKS):
                        fr[c, n, r] = strips[r][c * ZC : (c + 1) * ZC]
            else:
                total = jnp.zeros((NZ, 128), F32)
                for r in range(4):
                    total = jnp.where(group_z == strip + r, strips[r], total)
                for c in range(CHUNKS):
                    hfr[c, n - 3] = total[c * ZC : (c + 1) * ZC]

    def complete(c, carry):
        arrive(inside(s, 0), FIRST + 5 * c, hx.at[c], here(s, 0))
        assemble(c, False)
        late_columns(c)

        @pl.when(at_x)
        def _():
            for r in range(4):
                for f, (dest, base, _, _) in enumerate(spans):
                    dest[0, c, base + strip + r] = fr[c, f, r]
            pb[0, c, pl.ds(20 if s > 0 else 2, 2)] = jnp.zeros((2, ZC, 128), F32)
            strip_rows = (group_c >= strip) & (group_c < strip + 4)
            for f in range(3):
                for dest, region in ((qm, 0 if s > 0 else 1), (bm, 1 if s > 0 else 0)):
                    dest[c, f] = jnp.where(strip_rows, hfr[c, 3 * region + f], dest[c, f])

        lw, rw = windows(c)
        speed = window_speed(c)
        lw = [(jnp.where(ends_l, 0.0, m), jnp.where(ends_l, 0.0, x)) for m, x in lw]
        rw = [(jnp.where(ends_r, 0.0, m), jnp.where(ends_r, 0.0, x)) for m, x in rw]
        pl1, vl1 = window_step(lw, ends_l, speed)
        pr1, vr1 = window_step(rw, ends_r, speed)
        put_sides(sd, c, lw[0][0], rw[0][0], vl1, vr1)
        step(0, c, *late)
        arrive(inside(s, 0), round_slot(1, c), p_rows(1, c, far_side), here(s, 0))
        vl2, vr2 = new_v(pl1, vl1, ends_l), new_v(pr1, vr1, ends_r)
        put_sides(sd, c, pl1, pr1, vl2, vr2)
        wv[c] = jnp.where(e_c < 5, roll(vl2, 1), roll(vr2, 1))
        step(1, c, 0, BX)
        start(round_messages(2, c))
        return carry

    def window_speed(c):
        return sp[pl.ds(pl.multiple_of(c * ZC, ZC), ZC), :]

    lax.fori_loop(0, CHUNKS, complete, 0)

    def gather(r, c):
        receive(r, c)
        mine = ok[r, c]
        halo = jnp.where(e_c < 2, lr[r, c, 0], jnp.where(e_c < 4, lr[r, c, 1], wv[c]))
        halo = jnp.where(ends_y, 0.0, halo)
        slope = jnp.where(e_c == 4, roll(mine, 2) - roll(halo, 4), roll(halo, 2) - roll(mine, 4))
        wind = jnp.where(ends_y, 0.0, halo - 0.5 * slope)
        wv[c] = wind
        sd[c] = jnp.where(
            e_c == 0,
            roll(halo, -2),
            jnp.where(e_c == 1, halo, jnp.where(e_c == 2, roll(wind, -3), roll(wind, -1))),
        )

    def middle(c, carry):
        gather(2, c)
        step(2, c, 0, BX)
        start(round_messages(3, c))
        return carry

    lax.fori_loop(0, CHUNKS, middle, 0)

    def finish(c, carry):
        gather(3, c)
        step(3, c, 0, BX)
        return carry

    lax.fori_loop(0, CHUNKS, finish, 0)

    sent(column_messages())
    sent(row_messages())
    sent(strip_messages())

    def settle(c, carry):
        sent(first_x(c))
        sent(first_y(c))
        sent(near_messages(c))
        for r in range(2, 4):
            sent(round_messages(r, c))
        return carry

    lax.fori_loop(0, CHUNKS, settle, 0)


def move(s, state, parent, stiffness, offsets):
    vmem = lambda *shape: pltpu.VMEM(shape, F32)
    sems = 14 + CHUNKS * 5 + 3 * CHUNKS * 4
    scratch = [
        vmem(3, NZ * BX, 128),
        vmem(3 * PROWS, PCOLS, NZ),
        vmem(NZ, 128),
        vmem(CHUNKS, 3, BX, ZC, 128),
        vmem(CHUNKS, 15, ZC, 128),
        vmem(CHUNKS, 15, ZC, 128),
        vmem(CHUNKS, 3, ZC, 128),
        vmem(CHUNKS, 3, ZC, 128),
        vmem(CHUNKS, 3, TILES // 2, 8, 128),
        vmem(CHUNKS, 3, TILES // 2, 8, 128),
        vmem(CHUNKS, 3, ZC, 128),
        vmem(CHUNKS, 3, ZC, 128),
        vmem(4, CHUNKS, 24, ZC, 128),
        vmem(4, CHUNKS, 22, ZC, 128),
        vmem(4, CHUNKS, 20, ZC, 128),
        vmem(4, CHUNKS, ZC, 128),
        vmem(4, CHUNKS, 2, ZC, 128),
        vmem(CHUNKS, 3, ZC, 128),
        vmem(CHUNKS, 3, ZC, 128),
        vmem(CHUNKS, ZC, 128),
        vmem(CHUNKS, ZC, 128),
        vmem(CHUNKS, ZC, 128),
        vmem(4, 128, 128),
        vmem(3, NZ, 128),
        vmem(2, 3, NZ, 128),
        vmem(3, NZ, 128),
        vmem(3, NZ, 128),
        pltpu.VMEM((9, 256, 128), jnp.bfloat16),
        vmem(CHUNKS, 3, 4, ZC, 128),
        vmem(CHUNKS, 6, ZC, 128),
        vmem(32, 128),
        vmem(4, 32, 128),
        pltpu.VMEM((3, 2, 512, 128), jnp.bfloat16),
        pltpu.SMEM((4,), jnp.int32),
        pltpu.SMEM((NZ,), F32),
        pltpu.SemaphoreType.DMA((CHUNKS,)),
        pltpu.SemaphoreType.DMA,
        pltpu.SemaphoreType.DMA((2,)),
        pltpu.SemaphoreType.DMA((sems,)),
        pltpu.SemaphoreType.DMA((sems,)),
    ]
    hbm = pl.BlockSpec(memory_space=pltpu.HBM)
    return pl.pallas_call(
        functools.partial(kernel, s),
        out_shape=jax.ShapeDtypeStruct((3 * NZ * BX, BY), F32),
        in_specs=[hbm, hbm, hbm, hbm],
        out_specs=pl.BlockSpec(memory_space=pltpu.VMEM),
        scratch_shapes=scratch,
        compiler_params=pltpu.CompilerParams(
            collective_id=0 if s > 0 else 1, has_side_effects=True, vmem_limit_bytes=48 * 2**20
        ),
    )(offsets, stiffness, state, parent)


def per_device(state, parent, stiffness, offsets):
    flat = state.reshape(3, NZ * BX, BY)
    cells = parent.transpose(0, 2, 3, 1).reshape(3 * PROWS, PCOLS, NZ)
    out = lax.cond(
        offsets[2] > 0, functools.partial(move, 1), functools.partial(move, -1), flat, cells, stiffness, offsets
    )
    return out.reshape(3, NZ, BX, BY)


def solution(mesh):
    return jax.shard_map(
        per_device,
        mesh=mesh,
        in_specs=(P(None, None, "gx", "gy"), P(None, None, "gx", "gy"), P(), P()),
        out_specs=P(None, None, "gx", "gy"),
        check_vma=False,
    )
```

```python
import functools

import jax
import jax.numpy as jnp
from jax import lax
from jax.experimental import pallas as pl
from jax.experimental.pallas import tpu as pltpu
from jax.sharding import PartitionSpec as P

MESH = pl.DeviceIdType.MESH
F32 = jnp.float32
GX, GY = 8, 16
NZ, BX, BY = 64, 16, 128
CHUNKS = 4
AHEAD = 2
ZC = NZ // CHUNKS
TILES = ZC // 8
PROWS, PCOLS = 6, 34
SLOTS = ((0.375, 0.625, 0.0), (0.125, 0.875, 0.0), (0.0, 0.875, 0.125), (0.0, 0.625, 0.375))


def roll(x, shift):
    shift = shift % 128
    return x if shift == 0 else pltpu.roll(x, shift, 1)


def iota(shape, dim):
    return lax.broadcasted_iota(jnp.int32, shape, dim)


def split_dot(a, b):
    high = a.astype(jnp.bfloat16)
    low = (a - high.astype(F32)).astype(jnp.bfloat16)
    both = jnp.dot(jnp.concatenate([high, low], axis=0), b, preferred_element_type=F32)
    return both[: a.shape[0]] + both[a.shape[0] :]


def bilinear(cell, lower, frac):
    return jnp.where(cell == lower, 1.0 - frac, 0.0) + jnp.where(cell == lower + 1, frac, 0.0)


def kernel(
    s,
    off_hbm,
    stiff_hbm,
    st_hbm,
    par_hbm,
    out_ref,
    st,
    pin,
    sp,
    own,
    hs,
    hx,
    yp,
    lp,
    cp,
    cr,
    qm,
    qe,
    pb,
    ub,
    vb,
    ok,
    lr,
    bm,
    be,
    wv,
    sd,
    sx,
    tb,
    rsp,
    rsr,
    rsum,
    rnb,
    wr,
    fr,
    hfr,
    csm,
    csr,
    wc,
    off_ref,
    stiff_ref,
    in_sem,
    par_sem,
    smem_sem,
    send_sem,
    recv_sem,
):
    gx, gy = lax.axis_index("gx"), lax.axis_index("gy")
    here = lambda dx, dy: {"gx": gx + dx, "gy": gy + dy}
    inside = lambda dx, dy: (gx + dx >= 0) & (gx + dx < GX) & (gy + dy >= 0) & (gy + dy < GY)
    ex = GX - 1 if s > 0 else 0
    ey = 0 if s > 0 else GY - 1
    at_x, at_y = gx == ex, gy == ey
    last = 13 if s > 0 else 14

    def lo(d):
        return (2 * d) // 3

    def feeds(src, dst):
        return (src >= lo(dst)) & (src <= lo(dst) + 3) & (dst >= 0) & (dst < GX) & (src >= 0) & (src < GX)

    partners = [(dx, dy, inside(dx, dy)) for dx, dy in ((-1, 0), (1, 0), (0, -1), (0, 1), (-1, 1), (1, -1))]
    partners.append((2 * s, 0, gx == ex - 2 * s))
    partners.append((-2 * s, 0, at_x))
    for d in (-3, -2, 2, 3):
        partners.append((d, 0, at_y & (feeds(gx, gx + d) | feeds(gx + d, gx))))
    barrier = pltpu.get_barrier_semaphore()
    for dx, dy, cond in partners:

        @pl.when(cond)
        def _():
            pl.semaphore_signal(barrier, inc=1, device_id=here(dx, dy), device_id_type=MESH)

    def remote(slot, src, dst, device, recv_slot=None):
        return pltpu.make_async_remote_copy(
            src_ref=src,
            dst_ref=dst,
            send_sem=send_sem.at[slot],
            recv_sem=recv_sem.at[slot if recv_slot is None else recv_slot],
            device_id=device,
            device_id_type=MESH,
        )

    def start(messages):
        for cond, *copy in messages:

            @pl.when(cond)
            def _():
                remote(*copy).start()

    def sent(messages):
        for cond, *copy in messages:

            @pl.when(cond)
            def _():
                remote(*copy).wait_send()

    def arrive(cond, slot, ref, device):
        @pl.when(cond)
        def _():
            remote(slot, ref, ref, device).wait_recv()

    CS_RECV, CS_SEND, RS, NB, FIRST = 0, 4, 10, 12, 14
    ROUND = FIRST + 5 * CHUNKS
    counts, starts = (6, 5, 4), (0, 6, 11)

    def column_messages():
        return [
            (
                at_y & feeds(gx, gx + d),
                CS_SEND + k,
                csm,
                csr.at[gx - lo(gx + d)],
                here(d, 0),
                CS_RECV + gx - lo(gx + d),
            )
            for k, d in enumerate((-3, -2, -1, 1, 2, 3))
        ]

    def row_messages():
        return [(gx == ex - far * s, RS + k, rsp, rsr.at[k], here(far * s, 0)) for k, far in enumerate((2, 1))]

    def strip_messages():
        return [
            (at_x & (gy >= 1) & (gy - 1 <= last), NB, rsum, rnb, here(0, -1)),
            (at_x & (gy + 1 > last) & (gy + 1 < GY), NB + 1, rsum, rnb, here(0, 1)),
        ]

    def first_x(c):
        return [(inside(-s, 0), FIRST + 5 * c, hs.at[c], hx.at[c], here(-s, 0))]

    def first_y(c):
        return [
            (inside(0, s), FIRST + 5 * c + 3, yp.at[c], lp.at[c], here(0, s)),
            (inside(-s, s), FIRST + 5 * c + 4, cp.at[c], cr.at[c], here(-s, s)),
        ]

    def p_rows(r, c, first):
        return pb.at[r, c, pl.ds(first + 4, 2)]

    near, far_side = (0, BX) if s > 0 else (BX - 2, -2)

    def near_messages(c):
        return [(inside(-s, 0), round_slot(1, c), p_rows(1, c, near), p_rows(1, c, far_side), here(-s, 0))]

    def round_slot(r, c):
        return ROUND + ((r - 1) * CHUNKS + c) * 4

    def round_messages(r, c):
        k = round_slot(r, c)
        return [
            (inside(-1, 0), k, p_rows(r, c, 0), p_rows(r, c, BX), here(-1, 0)),
            (inside(1, 0), k + 1, p_rows(r, c, BX - 2), p_rows(r, c, -2), here(1, 0)),
            (inside(0, -1), k + 2, ok.at[r, c], lr.at[r, c, 1], here(0, -1)),
            (inside(0, 1), k + 3, ok.at[r, c], lr.at[r, c, 0], here(0, 1)),
        ]

    def receive(r, c):
        k = round_slot(r, c)
        arrive(inside(1, 0), k, p_rows(r, c, BX), here(1, 0))
        arrive(inside(-1, 0), k + 1, p_rows(r, c, -2), here(-1, 0))
        arrive(inside(0, 1), k + 2, lr.at[r, c, 1], here(0, 1))
        arrive(inside(0, -1), k + 3, lr.at[r, c, 0], here(0, -1))

    def load(c):
        rows = pl.ds(c * ZC * BX, ZC * BX)
        return pltpu.make_async_copy(st_hbm.at[:, rows], st.at[:, rows], in_sem.at[c])

    def state_row(c, f, x):
        return st[f, pl.ds(c * ZC * BX + x, ZC, stride=BX), :]

    par_copy = pltpu.make_async_copy(par_hbm, pin, par_sem)
    load(0).start()
    par_copy.start()
    scalars = [
        pltpu.make_async_copy(off_hbm, off_ref, smem_sem.at[0]),
        pltpu.make_async_copy(stiff_hbm, stiff_ref, smem_sem.at[1]),
    ]
    for copy in scalars:
        copy.start()
    for c in range(1, CHUNKS):
        load(c).start()

    lane = iota((8, 128), 1)
    group, e = lane >> 3, lane & 7
    lane_c = iota((ZC, 128), 1)
    group_c, e_c = lane_c >> 3, lane_c & 7

    par_copy.wait()
    for copy in scalars:
        copy.wait()
    use_rows = (gx >= 5) if s > 0 else (gx <= 2)
    ox = off_ref[0]

    @pl.when(use_rows)
    def _():
        low = ox + 31 if s > 0 else ox - 2
        for k in range(3):
            tb[k] = jnp.zeros((128, 128), F32)
            weight = [jnp.where(PROWS * gx + row == low + k, 1.0, 0.0) for row in range(PROWS)]
            for f in range(3):
                tb[k, PCOLS * f : PCOLS * f + PCOLS, 0:NZ] = sum(
                    weight[row] * pin[PROWS * f + row] for row in range(PROWS)
                )
        for k in range(3):
            rsp[k] = jnp.transpose(tb[k])[0:NZ]

    sent_rows = [range(n) if s > 0 else range(BX - n, BX) for n in counts]
    for c in range(CHUNKS):
        load(c).wait()
        for f in range(3):
            for n, x in enumerate(sent_rows[f]):
                hs[c, starts[f] + n] = state_row(c, f, x)
        if c == 0:
            pl.semaphore_wait(barrier, sum(cond.astype(jnp.int32) for _, _, cond in partners))
            if s < 0:
                start(row_messages())
        if c < AHEAD:
            start(first_x(c))
        if c == 0 and s > 0:
            start(row_messages())

    def pack(c, carry):
        packs = []
        for f in range(3):
            packed = jnp.zeros((ZC, 128), F32)
            for x in range(BX):
                row = state_row(c, f, x)
                own[c, f, x] = row
                packed = jnp.where(group_c == x, roll(row, 8 * x + (8 if s > 0 else 0)), packed)
            yp[c, f] = packed
            packs.append(packed)
        p, u, v = [roll(value, turn) for value, turn in zip(packs, (0, 48, 88) if s > 0 else (-80, -40, -8))]
        cp[c] = jnp.where(lane_c < 48, p, jnp.where(lane_c < 88, u, v))
        start(first_y(c))
        return carry

    lax.fori_loop(0, CHUNKS, pack, 0)

    @pl.when(at_y)
    def _():
        first_col = 27 if s > 0 else 30
        tb[3] = jnp.zeros((128, 128), F32)
        for row in range(PROWS):
            for f in range(3):
                at = 9 * row + 3 * f
                tb[3, at : at + 3, 0:NZ] = pin[PROWS * f + row, first_col : first_col + 3]
        turned = jnp.transpose(tb[3])
        csm[...] = turned[0:32] + roll(turned[32:64], 64)

    start(column_messages())

    sub = iota((8, 128), 0)
    for t in range(NZ // 8):
        value = jnp.zeros((8, 128), F32)
        for q in range(8):
            value = jnp.where(sub == q, stiff_ref[8 * t + q], value)
        sp[pl.ds(8 * t, 8), :] = 0.5 * value

    def ends(c, carry):
        for r in range(1, 4):

            @pl.when(gx == 0)
            def _():
                pb[r, c, 2:4] = jnp.zeros((2, ZC, 128), F32)

            @pl.when(gx == GX - 1)
            def _():
                pb[r, c, 20:22] = jnp.zeros((2, ZC, 128), F32)

            @pl.when(gy == 0)
            def _():
                lr[r, c, 0] = jnp.zeros((ZC, 128), F32)

            @pl.when(gy == GY - 1)
            def _():
                lr[r, c, 1] = jnp.zeros((ZC, 128), F32)

        return carry

    lax.fori_loop(0, CHUNKS, ends, 0)

    kk = iota((128, 128), 0)
    nn = iota((128, 128), 1)

    @pl.when(at_y)
    def _():
        krow = (kk * 57) >> 9
        krem = kk - 9 * krow
        kf = (krem >= 3).astype(jnp.int32) + (krem >= 6).astype(jnp.int32)
        ks = krem - 3 * kf
        ne = nn & 7
        col = (ne - 4) if s > 0 else ne
        wy = bilinear(ks, (2 * col + 5) >> 3, ((2 * col + 5) & 7).astype(F32) * 0.125)
        wy = jnp.where((col >= 0) & (col < 4) & (kk < 54), wy, 0.0)
        g = nn >> 3
        rows = (g, jnp.where(g < 2, g - 2, jnp.where(g < 4, g + 14, jnp.where(g < 6, g - 8 if s > 0 else g + 14, 0))))
        for k in range(4):
            for m in range(2):
                i = rows[m]
                lower = ox + s + 4 * gx + ((2 * i - 3) >> 3)
                wx = bilinear(PROWS * (lo(gx) + k) + krow, lower, ((2 * i - 3) & 7).astype(F32) * 0.125)
                for f in range(3):
                    wc[f, m, 128 * k : 128 * k + 128] = jnp.where(kf == f, wx * wy, 0.0).astype(jnp.bfloat16)

        for k in range(4):
            src = lo(gx) + k

            @pl.when(src == gx)
            def _():
                csr[k] = csm[...]

            @pl.when(src != gx)
            def _():
                remote(CS_RECV + k, csm, csr.at[k], here(src - gx, 0)).wait_recv()

        parts = [jnp.concatenate([csr[k], roll(csr[k], 64)], axis=0) for k in range(4)]
        column = jnp.concatenate(parts, axis=1)
        for f in range(3):
            for m, dest in enumerate((qm, qe)):
                total = split_dot(column, wc[f, m])
                for c in range(CHUNKS):
                    dest[c, f] = total[c * ZC : (c + 1) * ZC]

    edge = lane_c < 4 if s > 0 else lane_c >= 124
    strip = 12 if s > 0 else 0
    ends_x = ((gx == 0) & (lane_c < 16)) | ((gx == GX - 1) & (lane_c >= 16) & (lane_c < 32))
    ends_l, ends_r = (gy == 0) & (e_c < 4), (gy == GY - 1) & (e_c >= 4)
    ends_y = ((gy == 0) & ((e_c < 2) | (e_c == 4))) | ((gy == GY - 1) & ((e_c == 2) | (e_c == 3) | (e_c == 5)))
    spans = ((pb, 4, -4, 22), (ub, 3, -3, 20), (vb, 2, -2, 18)) if s > 0 else ((pb, 4, -2, 22), (ub, 3, -1, 20), (vb, 2, 0, 18))

    def held(i):
        return 0 <= i + 4 * s < BX

    def source(c, f, i):
        old = i + 4 * s
        if held(i):
            return own[c, f, old]
        return hx[c, starts[f] + (old - BX if s > 0 else old + counts[f])]

    def extra_group(i):
        return {-4: 4, -3: 5, -2: 0, -1: 1, 16: 2, 17: 3, 18: 4, 19: 5}[i]

    def assemble(c, mine):
        for f, (dest, base, first, count) in enumerate(spans):
            main, extra = qm[c, f], qe[c, f]
            for i in range(first, first + count):
                if held(i) != mine:
                    continue
                if 0 <= i < BX:
                    side = roll(main, -(8 * i + 4))
                else:
                    side = roll(extra, -(8 * extra_group(i) + 4))
                dest[0, c, i + base] = jnp.where(edge, side, roll(source(c, f, i), 4 * s))

    def late_columns(c):
        for f, last_row in enumerate(((18, -2), (17, -1), (16, 0))):
            main, extra = bm[c, f], be[c, f]
            for i in range(12, last_row[0]) if s > 0 else range(last_row[1], 4):
                row = source(c, f, i)
                if 0 <= i < BX:
                    main = jnp.where(group_c == i, roll(row, 8 * i + (8 if s > 0 else 0)), main)
                else:
                    g = extra_group(i)
                    extra = jnp.where(group_c == g, roll(row, 8 * g + (8 if s > 0 else 0)), extra)
            bm[c, f] = main
            be[c, f] = extra

    def windows(c):
        q = [(qm[c, f], jnp.where(ends_x, 0.0, qe[c, f])) for f in range(3)]
        b = [(bm[c, f], jnp.where(ends_x, 0.0, be[c, f])) for f in range(3)]
        return (q, b) if s > 0 else (b, q)

    def new_v(p, v, ends):
        return jnp.where(ends, 0.0, v - 0.5 * (roll(p, -1) - roll(p, 1)))

    def put_sides(dest, c, pl_, pr_, vl_, vr_):
        dest[c] = jnp.where(
            e_c == 0, roll(pr_, -4), jnp.where(e_c == 1, roll(pl_, -2), jnp.where(e_c == 2, roll(vr_, -2), vl_))
        )

    def up(main, extra):
        return jnp.where(lane_c < 8, roll(extra, -8), roll(main, 8))

    def down(main, extra):
        return jnp.where(lane_c >= 120, roll(extra, 104), roll(main, -8))

    def window_step(fields, ends, speed):
        (p, px), (u, ux), (v, _) = fields
        u1 = u - 0.5 * (down(p, px) - up(p, px))
        slope = jnp.where(lane_c < 16, roll(p, 8) - roll(px, 8), roll(px, -8) - roll(p, 24))
        u1x = jnp.where(ends_x, 0.0, ux - 0.5 * slope)
        v1 = new_v(p, v, ends)
        p1 = p - speed * ((down(u1, u1x) - up(u1, u1x)) + (roll(v1, -1) - roll(v1, 1)))
        return jnp.where(ends, 0.0, p1), v1

    def step(r, c, first, count):
        final = isinstance(r, int) and r == 3
        packs = not final and not (isinstance(r, int) and r == 0)

        def tile(t):
            zr = pl.ds(8 * t, 8)
            side, extra = sd[c, zr], sx[c, zr]
            speed = sp[pl.ds(pl.multiple_of(c * ZC + 8 * t, 8), 8), :]
            p = {n: pb[r, c, n + 4, zr] for n in range(first - 2, first + count + 2)}
            u = {}
            for n in range(first - 1, first + count + 1):
                new = ub[r, c, n + 3, zr] - 0.5 * (p[n + 1] - p[n - 1])
                if n == -1:
                    new = jnp.where(gx == 0, 0.0, new)
                if n == BX:
                    new = jnp.where(gx == GX - 1, 0.0, new)
                u[n] = new
                mine = first <= n < first + count or (n == -1 and first == 0) or (n == BX and first + count == BX)
                if not final and mine and -1 <= n <= BX:
                    ub[r + 1, c, n + 3, zr] = new
            pack = jnp.zeros((8, 128), F32)
            for x in range(first, first + count):
                near_side, g = (side, x) if 0 <= x < BX else (extra, extra_group(x))
                side_p = roll(near_side, -(8 * g + 1))
                before = jnp.where(lane == 0, side_p, roll(p[x], 1))
                after = jnp.where(lane == 127, side_p, roll(p[x], -1))
                v = vb[r, c, x + 2, zr] - 0.5 * (after - before)
                side_v = roll(near_side, -(8 * g + 3))
                before = jnp.where(lane == 0, side_v, roll(v, 1))
                after = jnp.where(lane == 127, side_v, roll(v, -1))
                new_p = p[x] - speed * ((u[x + 1] - u[x - 1]) + (after - before))
                if x < 0:
                    new_p = jnp.where(gx == 0, 0.0, new_p)
                if x >= BX:
                    new_p = jnp.where(gx == GX - 1, 0.0, new_p)
                if final:
                    for f, value in enumerate((new_p, u[x], v)):
                        out_ref[pl.ds(f * NZ * BX + (c * ZC + 8 * t) * BX + x, 8, stride=BX), :] = value
                else:
                    pb[r + 1, c, x + 4, zr] = new_p
                    if 0 <= x < BX:
                        vb[r + 1, c, x + 2, zr] = v
                    if packs:
                        pack = jnp.where(group == x, roll(new_p, 8 * x + 2), pack)
            if packs:
                ok[r + 1, c, zr] = pack

        for t in range(TILES):
            tile(t)

    corner_at = (0, 48, 88) if s > 0 else (0, 40, 72)
    early, late = ((-2, 12), (10, 6)) if s > 0 else ((6, 12), (0, 6))

    def begin(c, carry):
        @pl.when(at_x & (c == CHUNKS // 2))
        def _():
            for k, far in enumerate((2, 1)):
                remote(RS + k, rsp, rsr.at[k], here(-far * s, 0)).wait_recv()
            for k in range(3):
                rsum[k] = rsp[k] + rsr[0, k] + rsr[1, k]
            start(strip_messages())

        arrive(inside(0, -s), FIRST + 5 * c + 3, lp.at[c], here(0, -s))
        arrive(inside(s, -s), FIRST + 5 * c + 4, cr.at[c], here(s, -s))

        @pl.when(jnp.logical_not(at_y))
        def _():
            for f in range(3):
                corner, side, at = cr[c], lp[c, f], corner_at[f]
                if s > 0:
                    qm[c, f] = jnp.where(lane_c < 96, roll(side, -32), roll(corner, 96 - at))
                    qe[c, f] = jnp.where(
                        lane_c < 16, roll(side, -16), jnp.where(lane_c < 32, roll(corner, -16 - at), roll(side, 32))
                    )
                else:
                    qm[c, f] = jnp.where(lane_c < 32, roll(corner, -16 - at), roll(side, 32))
                    qe[c, f] = jnp.where(lane_c < 16, roll(corner, -at), roll(side, -80))

        for f in range(3):
            mine = yp[c, f]
            bm[c, f] = roll(mine, -32 * s)
            be[c, f] = roll(mine, -16 if s > 0 else -80)
        assemble(c, True)

        @pl.when(gx == GX - 1 - ex)
        def _():
            pb[0, c, pl.ds(0 if s > 0 else 20, 4)] = jnp.zeros((4, ZC, 128), F32)

        lw, rw = windows(c)
        for dest, k in ((sd, 0), (sx, 1)):
            (pl_, vl_), (pr_, vr_) = [(w[0][k], w[2][k]) for w in (lw, rw)]
            pl_, pr_ = jnp.where(ends_l, 0.0, pl_), jnp.where(ends_r, 0.0, pr_)
            put_sides(dest, c, pl_, pr_, new_v(pl_, vl_, ends_l), new_v(pr_, vr_, ends_r))
        step(0, c, *early)
        start(near_messages(c))

        @pl.when(c == 0)
        def _():
            start(first_x(2))

        @pl.when(c == 2)
        def _():
            start(first_x(3))

        return carry

    lax.fori_loop(0, CHUNKS, begin, 0)

    @pl.when(at_x)
    def _():
        base = 28 if s > 0 else 30
        other = jnp.where(gy <= last, gy + 1, gy - 1)

        def weights(block, f, j):
            lower = base + 32 * gy + ((2 * j - 3) >> 3)
            frac = ((2 * j - 3) & 7).astype(F32) * 0.125
            valid = (kk >= PCOLS * f) & (kk < PCOLS * f + PCOLS)
            return jnp.where(valid, bilinear(PCOLS * block + kk - PCOLS * f, lower, frac), 0.0)

        ne = nn & 7
        for b, block in enumerate((gy, other)):
            kr = slice(128 * b, 128 * b + 128)
            for f in range(3):
                wr[f, kr] = weights(block, f, nn).astype(jnp.bfloat16)
                wr[3 + f, kr] = weights(block, f, ne - 4).astype(jnp.bfloat16)
                wr[6 + f, kr] = weights(block, f, ne + 124).astype(jnp.bfloat16)

    @pl.when(at_x)
    def _():
        @pl.when(gy <= last)
        def _():
            remote(NB, rsum, rnb, here(0, 1)).wait_recv()

        @pl.when(gy > last)
        def _():
            remote(NB + 1, rsum, rnb, here(0, -1)).wait_recv()

        group_z = iota((NZ, 128), 1) >> 3
        rows = jnp.concatenate([jnp.concatenate([rsum[k], rnb[k]], axis=1) for k in range(3)], axis=0)
        for n in range(9):
            total = split_dot(rows, wr[n])
            slots = [total[NZ * k : NZ * k + NZ] for k in range(3)]
            strips = [sum(w * x for w, x in zip(SLOTS[r], slots) if w) for r in range(4)]
            if n < 3:
                for r in range(4):
                    for c in range(CHUNKS):
                        fr[c, n, r] = strips[r][c * ZC : (c + 1) * ZC]
            else:
                total = jnp.zeros((NZ, 128), F32)
                for r in range(4):
                    total = jnp.where(group_z == strip + r, strips[r], total)
                for c in range(CHUNKS):
                    hfr[c, n - 3] = total[c * ZC : (c + 1) * ZC]

    def complete(c, carry):
        arrive(inside(s, 0), FIRST + 5 * c, hx.at[c], here(s, 0))
        assemble(c, False)
        late_columns(c)

        @pl.when(at_x)
        def _():
            for r in range(4):
                for f, (dest, base, _, _) in enumerate(spans):
                    dest[0, c, base + strip + r] = fr[c, f, r]
            pb[0, c, pl.ds(20 if s > 0 else 2, 2)] = jnp.zeros((2, ZC, 128), F32)
            strip_rows = (group_c >= strip) & (group_c < strip + 4)
            for f in range(3):
                for dest, region in ((qm, 0 if s > 0 else 1), (bm, 1 if s > 0 else 0)):
                    dest[c, f] = jnp.where(strip_rows, hfr[c, 3 * region + f], dest[c, f])

        lw, rw = windows(c)
        speed = window_speed(c)
        lw = [(jnp.where(ends_l, 0.0, m), jnp.where(ends_l, 0.0, x)) for m, x in lw]
        rw = [(jnp.where(ends_r, 0.0, m), jnp.where(ends_r, 0.0, x)) for m, x in rw]
        pl1, vl1 = window_step(lw, ends_l, speed)
        pr1, vr1 = window_step(rw, ends_r, speed)
        put_sides(sd, c, lw[0][0], rw[0][0], vl1, vr1)
        step(0, c, *late)
        arrive(inside(s, 0), round_slot(1, c), p_rows(1, c, far_side), here(s, 0))
        vl2, vr2 = new_v(pl1, vl1, ends_l), new_v(pr1, vr1, ends_r)
        put_sides(sd, c, pl1, pr1, vl2, vr2)
        wv[c] = jnp.where(e_c < 5, roll(vl2, 1), roll(vr2, 1))
        step(1, c, 0, BX)
        start(round_messages(2, c)[2:] + round_messages(2, c)[:2])
        return carry

    def window_speed(c):
        return sp[pl.ds(pl.multiple_of(c * ZC, ZC), ZC), :]

    lax.fori_loop(0, CHUNKS, complete, 0)

    def gather(r, c):
        receive(r, c)
        mine = ok[r, c]
        halo = jnp.where(e_c < 2, lr[r, c, 0], jnp.where(e_c < 4, lr[r, c, 1], wv[c]))
        halo = jnp.where(ends_y, 0.0, halo)
        slope = jnp.where(e_c == 4, roll(mine, 2) - roll(halo, 4), roll(halo, 2) - roll(mine, 4))
        wind = jnp.where(ends_y, 0.0, halo - 0.5 * slope)
        wv[c] = wind
        sd[c] = jnp.where(
            e_c == 0,
            roll(halo, -2),
            jnp.where(e_c == 1, halo, jnp.where(e_c == 2, roll(wind, -3), roll(wind, -1))),
        )

    def middle(c, carry):
        gather(2, c)
        step(2, c, 0, BX)
        start(round_messages(3, c)[2:] + round_messages(3, c)[:2])
        return carry

    lax.fori_loop(0, CHUNKS, middle, 0)

    def finish(c, carry):
        gather(3, c)
        step(3, c, 0, BX)
        return carry

    lax.fori_loop(0, CHUNKS, finish, 0)

    sent(column_messages())
    sent(row_messages())
    sent(strip_messages())

    def settle(c, carry):
        sent(first_x(c))
        sent(first_y(c))
        sent(near_messages(c))
        for r in range(2, 4):
            sent(round_messages(r, c))
        return carry

    lax.fori_loop(0, CHUNKS, settle, 0)


def move(s, state, parent, stiffness, offsets):
    vmem = lambda *shape: pltpu.VMEM(shape, F32)
    sems = 14 + CHUNKS * 5 + 3 * CHUNKS * 4
    scratch = [
        vmem(3, NZ * BX, 128),
        vmem(3 * PROWS, PCOLS, NZ),
        vmem(NZ, 128),
        vmem(CHUNKS, 3, BX, ZC, 128),
        vmem(CHUNKS, 15, ZC, 128),
        vmem(CHUNKS, 15, ZC, 128),
        vmem(CHUNKS, 3, ZC, 128),
        vmem(CHUNKS, 3, ZC, 128),
        vmem(CHUNKS, ZC, 128),
        vmem(CHUNKS, ZC, 128),
        vmem(CHUNKS, 3, ZC, 128),
        vmem(CHUNKS, 3, ZC, 128),
        vmem(4, CHUNKS, 24, ZC, 128),
        vmem(4, CHUNKS, 22, ZC, 128),
        vmem(4, CHUNKS, 20, ZC, 128),
        vmem(4, CHUNKS, ZC, 128),
        vmem(4, CHUNKS, 2, ZC, 128),
        vmem(CHUNKS, 3, ZC, 128),
        vmem(CHUNKS, 3, ZC, 128),
        vmem(CHUNKS, ZC, 128),
        vmem(CHUNKS, ZC, 128),
        vmem(CHUNKS, ZC, 128),
        vmem(4, 128, 128),
        vmem(3, NZ, 128),
        vmem(2, 3, NZ, 128),
        vmem(3, NZ, 128),
        vmem(3, NZ, 128),
        pltpu.VMEM((9, 256, 128), jnp.bfloat16),
        vmem(CHUNKS, 3, 4, ZC, 128),
        vmem(CHUNKS, 6, ZC, 128),
        vmem(32, 128),
        vmem(4, 32, 128),
        pltpu.VMEM((3, 2, 512, 128), jnp.bfloat16),
        pltpu.SMEM((4,), jnp.int32),
        pltpu.SMEM((NZ,), F32),
        pltpu.SemaphoreType.DMA((CHUNKS,)),
        pltpu.SemaphoreType.DMA,
        pltpu.SemaphoreType.DMA((2,)),
        pltpu.SemaphoreType.DMA((sems,)),
        pltpu.SemaphoreType.DMA((sems,)),
    ]
    hbm = pl.BlockSpec(memory_space=pltpu.HBM)
    return pl.pallas_call(
        functools.partial(kernel, s),
        out_shape=jax.ShapeDtypeStruct((3 * NZ * BX, BY), F32),
        in_specs=[hbm, hbm, hbm, hbm],
        out_specs=pl.BlockSpec(memory_space=pltpu.VMEM),
        scratch_shapes=scratch,
        compiler_params=pltpu.CompilerParams(
            collective_id=0 if s > 0 else 1, has_side_effects=True, vmem_limit_bytes=48 * 2**20
        ),
    )(offsets, stiffness, state, parent)


def per_device(state, parent, stiffness, offsets):
    flat = state.reshape(3, NZ * BX, BY)
    cells = parent.transpose(0, 2, 3, 1).reshape(3 * PROWS, PCOLS, NZ)
    out = lax.cond(
        offsets[2] > 0, functools.partial(move, 1), functools.partial(move, -1), flat, cells, stiffness, offsets
    )
    return out.reshape(3, NZ, BX, BY)


def solution(mesh):
    return jax.shard_map(
        per_device,
        mesh=mesh,
        in_specs=(P(None, None, "gx", "gy"), P(None, None, "gx", "gy"), P(), P()),
        out_specs=P(None, None, "gx", "gy"),
        check_vma=False,
    )
```

```python
import functools

import jax
import jax.numpy as jnp
from jax import lax
from jax.experimental import pallas as pl
from jax.experimental.pallas import tpu as pltpu
from jax.sharding import PartitionSpec as P

MESH = pl.DeviceIdType.MESH
F32 = jnp.float32
GX, GY = 8, 16
NZ, BX, BY = 64, 16, 128
CHUNKS = 4
AHEAD = 2
ZC = NZ // CHUNKS
TILES = ZC // 8
PROWS, PCOLS = 6, 34
SLOTS = ((0.375, 0.625, 0.0), (0.125, 0.875, 0.0), (0.0, 0.875, 0.125), (0.0, 0.625, 0.375))


def roll(x, shift):
    shift = shift % 128
    return x if shift == 0 else pltpu.roll(x, shift, 1)


def iota(shape, dim):
    return lax.broadcasted_iota(jnp.int32, shape, dim)


def split_dot(a, b):
    high = a.astype(jnp.bfloat16)
    low = (a - high.astype(F32)).astype(jnp.bfloat16)
    both = jnp.dot(jnp.concatenate([high, low], axis=0), b, preferred_element_type=F32)
    return both[: a.shape[0]] + both[a.shape[0] :]


def bilinear(cell, lower, frac):
    return jnp.where(cell == lower, 1.0 - frac, 0.0) + jnp.where(cell == lower + 1, frac, 0.0)


def kernel(
    s,
    off_hbm,
    stiff_hbm,
    st_hbm,
    par_hbm,
    out_ref,
    st,
    pin,
    sp,
    own,
    hs,
    hx,
    yp,
    lp,
    cp,
    cr,
    qm,
    qe,
    pb,
    ub,
    vb,
    ok,
    lr,
    bm,
    be,
    wv,
    sd,
    sx,
    tb,
    rsp,
    rsr,
    rsum,
    rnb,
    wr,
    fr,
    hfr,
    csm,
    csr,
    wc,
    off_ref,
    stiff_ref,
    in_sem,
    par_sem,
    smem_sem,
    send_sem,
    recv_sem,
):
    gx, gy = lax.axis_index("gx"), lax.axis_index("gy")
    here = lambda dx, dy: {"gx": gx + dx, "gy": gy + dy}
    inside = lambda dx, dy: (gx + dx >= 0) & (gx + dx < GX) & (gy + dy >= 0) & (gy + dy < GY)
    ex = GX - 1 if s > 0 else 0
    ey = 0 if s > 0 else GY - 1
    at_x, at_y = gx == ex, gy == ey
    last = 13 if s > 0 else 14

    def lo(d):
        return (2 * d) // 3

    def feeds(src, dst):
        return (src >= lo(dst)) & (src <= lo(dst) + 3) & (dst >= 0) & (dst < GX) & (src >= 0) & (src < GX)

    partners = [(dx, dy, inside(dx, dy)) for dx, dy in ((-1, 0), (1, 0), (0, -1), (0, 1), (-1, 1), (1, -1))]
    partners.append((2 * s, 0, gx == ex - 2 * s))
    partners.append((-2 * s, 0, at_x))
    for d in (-3, -2, 2, 3):
        partners.append((d, 0, at_y & (feeds(gx, gx + d) | feeds(gx + d, gx))))
    barrier = pltpu.get_barrier_semaphore()
    for dx, dy, cond in partners:

        @pl.when(cond)
        def _():
            pl.semaphore_signal(barrier, inc=1, device_id=here(dx, dy), device_id_type=MESH)

    def remote(slot, src, dst, device, recv_slot=None):
        return pltpu.make_async_remote_copy(
            src_ref=src,
            dst_ref=dst,
            send_sem=send_sem.at[slot],
            recv_sem=recv_sem.at[slot if recv_slot is None else recv_slot],
            device_id=device,
            device_id_type=MESH,
        )

    def start(messages):
        for cond, *copy in messages:

            @pl.when(cond)
            def _():
                remote(*copy).start()

    def sent(messages):
        for cond, *copy in messages:

            @pl.when(cond)
            def _():
                remote(*copy).wait_send()

    def arrive(cond, slot, ref, device):
        @pl.when(cond)
        def _():
            remote(slot, ref, ref, device).wait_recv()

    CS_RECV, CS_SEND, RS, NB, FIRST = 0, 4, 10, 12, 14
    ROUND = FIRST + 5 * CHUNKS
    counts, starts = (6, 5, 4), (0, 6, 11)

    def column_messages():
        return [
            (
                at_y & feeds(gx, gx + d),
                CS_SEND + k,
                csm,
                csr.at[gx - lo(gx + d)],
                here(d, 0),
                CS_RECV + gx - lo(gx + d),
            )
            for k, d in enumerate((-3, -2, -1, 1, 2, 3))
        ]

    def row_messages():
        return [(gx == ex - far * s, RS + k, rsp, rsr.at[k], here(far * s, 0)) for k, far in enumerate((2, 1))]

    def strip_messages():
        return [
            (at_x & (gy >= 1) & (gy - 1 <= last), NB, rsum, rnb, here(0, -1)),
            (at_x & (gy + 1 > last) & (gy + 1 < GY), NB + 1, rsum, rnb, here(0, 1)),
        ]

    def first_x(c):
        return [(inside(-s, 0), FIRST + 5 * c, hs.at[c], hx.at[c], here(-s, 0))]

    def first_y(c):
        return [
            (inside(0, s), FIRST + 5 * c + 3, yp.at[c], lp.at[c], here(0, s)),
            (inside(-s, s), FIRST + 5 * c + 4, cp.at[c], cr.at[c], here(-s, s)),
        ]

    def p_rows(r, c, first):
        return pb.at[r, c, pl.ds(first + 4, 2)]

    near, far_side = (0, BX) if s > 0 else (BX - 2, -2)

    def near_messages(c):
        return [(inside(-s, 0), round_slot(1, c), p_rows(1, c, near), p_rows(1, c, far_side), here(-s, 0))]

    def round_slot(r, c):
        return ROUND + ((r - 1) * CHUNKS + c) * 4

    def round_messages(r, c):
        k = round_slot(r, c)
        return [
            (inside(-1, 0), k, p_rows(r, c, 0), p_rows(r, c, BX), here(-1, 0)),
            (inside(1, 0), k + 1, p_rows(r, c, BX - 2), p_rows(r, c, -2), here(1, 0)),
            (inside(0, -1), k + 2, ok.at[r, c], lr.at[r, c, 1], here(0, -1)),
            (inside(0, 1), k + 3, ok.at[r, c], lr.at[r, c, 0], here(0, 1)),
        ]

    def receive(r, c):
        k = round_slot(r, c)
        arrive(inside(1, 0), k, p_rows(r, c, BX), here(1, 0))
        arrive(inside(-1, 0), k + 1, p_rows(r, c, -2), here(-1, 0))
        arrive(inside(0, 1), k + 2, lr.at[r, c, 1], here(0, 1))
        arrive(inside(0, -1), k + 3, lr.at[r, c, 0], here(0, -1))

    def load(c):
        rows = pl.ds(c * ZC * BX, ZC * BX)
        return pltpu.make_async_copy(st_hbm.at[:, rows], st.at[:, rows], in_sem.at[c])

    def state_row(c, f, x):
        return st[f, pl.ds(c * ZC * BX + x, ZC, stride=BX), :]

    par_copy = pltpu.make_async_copy(par_hbm, pin, par_sem)
    load(0).start()
    par_copy.start()
    scalars = [
        pltpu.make_async_copy(off_hbm, off_ref, smem_sem.at[0]),
        pltpu.make_async_copy(stiff_hbm, stiff_ref, smem_sem.at[1]),
    ]
    for copy in scalars:
        copy.start()
    for c in range(1, CHUNKS):
        load(c).start()

    lane = iota((8, 128), 1)
    group, e = lane >> 3, lane & 7
    lane_c = iota((ZC, 128), 1)
    group_c, e_c = lane_c >> 3, lane_c & 7

    par_copy.wait()
    for copy in scalars:
        copy.wait()
    use_rows = (gx >= 5) if s > 0 else (gx <= 2)
    ox = off_ref[0]

    @pl.when(use_rows)
    def _():
        low = ox + 31 if s > 0 else ox - 2
        for k in range(3):
            tb[k] = jnp.zeros((128, 128), F32)
            weight = [jnp.where(PROWS * gx + row == low + k, 1.0, 0.0) for row in range(PROWS)]
            for f in range(3):
                tb[k, PCOLS * f : PCOLS * f + PCOLS, 0:NZ] = sum(
                    weight[row] * pin[PROWS * f + row] for row in range(PROWS)
                )
        for k in range(3):
            rsp[k] = jnp.transpose(tb[k])[0:NZ]

    sent_rows = [range(n) if s > 0 else range(BX - n, BX) for n in counts]
    for c in range(CHUNKS):
        load(c).wait()
        for f in range(3):
            for n, x in enumerate(sent_rows[f]):
                hs[c, starts[f] + n] = state_row(c, f, x)
        if c == 0:
            pl.semaphore_wait(barrier, sum(cond.astype(jnp.int32) for _, _, cond in partners))
            if s < 0:
                start(row_messages())
        if c < AHEAD:
            start(first_x(c))
        if c == 0 and s > 0:
            start(row_messages())

    def pack(c, carry):
        packs = []
        for f in range(3):
            packed = jnp.zeros((ZC, 128), F32)
            for x in range(BX):
                row = state_row(c, f, x)
                own[c, f, x] = row
                packed = jnp.where(group_c == x, roll(row, 8 * x + (8 if s > 0 else 0)), packed)
            yp[c, f] = packed
            packs.append(packed)
        p, u, v = [roll(value, turn) for value, turn in zip(packs, (0, 48, 88) if s > 0 else (-80, -40, -8))]
        cp[c] = jnp.where(lane_c < 48, p, jnp.where(lane_c < 88, u, v))
        start(first_y(c))
        return carry

    lax.fori_loop(0, CHUNKS, pack, 0)

    @pl.when(at_y)
    def _():
        first_col = 27 if s > 0 else 30
        tb[3] = jnp.zeros((128, 128), F32)
        for row in range(PROWS):
            for f in range(3):
                at = 9 * row + 3 * f
                tb[3, at : at + 3, 0:NZ] = pin[PROWS * f + row, first_col : first_col + 3]
        turned = jnp.transpose(tb[3])
        csm[...] = turned[0:32] + roll(turned[32:64], 64)

    start(column_messages())

    sub = iota((8, 128), 0)
    for t in range(NZ // 8):
        value = jnp.zeros((8, 128), F32)
        for q in range(8):
            value = jnp.where(sub == q, stiff_ref[8 * t + q], value)
        sp[pl.ds(8 * t, 8), :] = 0.5 * value

    def ends(c, carry):
        for r in range(1, 4):

            @pl.when(gx == 0)
            def _():
                pb[r, c, 2:4] = jnp.zeros((2, ZC, 128), F32)

            @pl.when(gx == GX - 1)
            def _():
                pb[r, c, 20:22] = jnp.zeros((2, ZC, 128), F32)

            @pl.when(gy == 0)
            def _():
                lr[r, c, 0] = jnp.zeros((ZC, 128), F32)

            @pl.when(gy == GY - 1)
            def _():
                lr[r, c, 1] = jnp.zeros((ZC, 128), F32)

        return carry

    lax.fori_loop(0, CHUNKS, ends, 0)

    kk = iota((128, 128), 0)
    nn = iota((128, 128), 1)

    @pl.when(at_y)
    def _():
        krow = (kk * 57) >> 9
        krem = kk - 9 * krow
        kf = (krem >= 3).astype(jnp.int32) + (krem >= 6).astype(jnp.int32)
        ks = krem - 3 * kf
        ne = nn & 7
        col = (ne - 4) if s > 0 else ne
        wy = bilinear(ks, (2 * col + 5) >> 3, ((2 * col + 5) & 7).astype(F32) * 0.125)
        wy = jnp.where((col >= 0) & (col < 4) & (kk < 54), wy, 0.0)
        g = nn >> 3
        rows = (g, jnp.where(g < 2, g - 2, jnp.where(g < 4, g + 14, jnp.where(g < 6, g - 8 if s > 0 else g + 14, 0))))
        for k in range(4):
            for m in range(2):
                i = rows[m]
                lower = ox + s + 4 * gx + ((2 * i - 3) >> 3)
                wx = bilinear(PROWS * (lo(gx) + k) + krow, lower, ((2 * i - 3) & 7).astype(F32) * 0.125)
                for f in range(3):
                    wc[f, m, 128 * k : 128 * k + 128] = jnp.where(kf == f, wx * wy, 0.0).astype(jnp.bfloat16)

        for k in range(4):
            src = lo(gx) + k

            @pl.when(src == gx)
            def _():
                csr[k] = csm[...]

            @pl.when(src != gx)
            def _():
                remote(CS_RECV + k, csm, csr.at[k], here(src - gx, 0)).wait_recv()

        parts = [jnp.concatenate([csr[k], roll(csr[k], 64)], axis=0) for k in range(4)]
        column = jnp.concatenate(parts, axis=1)
        for f in range(3):
            for m, dest in enumerate((qm, qe)):
                total = split_dot(column, wc[f, m])
                for c in range(CHUNKS):
                    dest[c, f] = total[c * ZC : (c + 1) * ZC]

    edge = lane_c < 4 if s > 0 else lane_c >= 124
    strip = 12 if s > 0 else 0
    ends_x = ((gx == 0) & (lane_c < 16)) | ((gx == GX - 1) & (lane_c >= 16) & (lane_c < 32))
    ends_l, ends_r = (gy == 0) & (e_c < 4), (gy == GY - 1) & (e_c >= 4)
    ends_y = ((gy == 0) & ((e_c < 2) | (e_c == 4))) | ((gy == GY - 1) & ((e_c == 2) | (e_c == 3) | (e_c == 5)))
    spans = ((pb, 4, -4, 22), (ub, 3, -3, 20), (vb, 2, -2, 18)) if s > 0 else ((pb, 4, -2, 22), (ub, 3, -1, 20), (vb, 2, 0, 18))

    def held(i):
        return 0 <= i + 4 * s < BX

    def source(c, f, i):
        old = i + 4 * s
        if held(i):
            return own[c, f, old]
        return hx[c, starts[f] + (old - BX if s > 0 else old + counts[f])]

    def extra_group(i):
        return {-4: 4, -3: 5, -2: 0, -1: 1, 16: 2, 17: 3, 18: 4, 19: 5}[i]

    def assemble(c, mine):
        for f, (dest, base, first, count) in enumerate(spans):
            main, extra = qm[c, f], qe[c, f]
            for i in range(first, first + count):
                if held(i) != mine:
                    continue
                if 0 <= i < BX:
                    side = roll(main, -(8 * i + 4))
                else:
                    side = roll(extra, -(8 * extra_group(i) + 4))
                dest[0, c, i + base] = jnp.where(edge, side, roll(source(c, f, i), 4 * s))

    def late_columns(c):
        for f, last_row in enumerate(((18, -2), (17, -1), (16, 0))):
            main, extra = bm[c, f], be[c, f]
            for i in range(12, last_row[0]) if s > 0 else range(last_row[1], 4):
                row = source(c, f, i)
                if 0 <= i < BX:
                    main = jnp.where(group_c == i, roll(row, 8 * i + (8 if s > 0 else 0)), main)
                else:
                    g = extra_group(i)
                    extra = jnp.where(group_c == g, roll(row, 8 * g + (8 if s > 0 else 0)), extra)
            bm[c, f] = main
            be[c, f] = extra

    def windows(c):
        q = [(qm[c, f], jnp.where(ends_x, 0.0, qe[c, f])) for f in range(3)]
        b = [(bm[c, f], jnp.where(ends_x, 0.0, be[c, f])) for f in range(3)]
        return (q, b) if s > 0 else (b, q)

    def new_v(p, v, ends):
        return jnp.where(ends, 0.0, v - 0.5 * (roll(p, -1) - roll(p, 1)))

    def put_sides(dest, c, pl_, pr_, vl_, vr_):
        dest[c] = jnp.where(
            e_c == 0, roll(pr_, -4), jnp.where(e_c == 1, roll(pl_, -2), jnp.where(e_c == 2, roll(vr_, -2), vl_))
        )

    def up(main, extra):
        return jnp.where(lane_c < 8, roll(extra, -8), roll(main, 8))

    def down(main, extra):
        return jnp.where(lane_c >= 120, roll(extra, 104), roll(main, -8))

    def window_step(fields, ends, speed):
        (p, px), (u, ux), (v, _) = fields
        u1 = u - 0.5 * (down(p, px) - up(p, px))
        slope = jnp.where(lane_c < 16, roll(p, 8) - roll(px, 8), roll(px, -8) - roll(p, 24))
        u1x = jnp.where(ends_x, 0.0, ux - 0.5 * slope)
        v1 = new_v(p, v, ends)
        p1 = p - speed * ((down(u1, u1x) - up(u1, u1x)) + (roll(v1, -1) - roll(v1, 1)))
        return jnp.where(ends, 0.0, p1), v1

    def step(r, c, first, count):
        final = isinstance(r, int) and r == 3
        packs = not final and not (isinstance(r, int) and r == 0)

        def tile(t):
            zr = pl.ds(8 * t, 8)
            side, extra = sd[c, zr], sx[c, zr]
            speed = sp[pl.ds(pl.multiple_of(c * ZC + 8 * t, 8), 8), :]
            p = {n: pb[r, c, n + 4, zr] for n in range(first - 2, first + count + 2)}
            u = {}
            for n in range(first - 1, first + count + 1):
                new = ub[r, c, n + 3, zr] - 0.5 * (p[n + 1] - p[n - 1])
                if n == -1:
                    new = jnp.where(gx == 0, 0.0, new)
                if n == BX:
                    new = jnp.where(gx == GX - 1, 0.0, new)
                u[n] = new
                mine = first <= n < first + count or (n == -1 and first == 0) or (n == BX and first + count == BX)
                if not final and mine and -1 <= n <= BX:
                    ub[r + 1, c, n + 3, zr] = new
            pack = ok[r + 1, c, zr] if packs and first > 0 else jnp.zeros((8, 128), F32)
            for x in range(first, first + count):
                near_side, g = (side, x) if 0 <= x < BX else (extra, extra_group(x))
                side_p = roll(near_side, -(8 * g + 1))
                before = jnp.where(lane == 0, side_p, roll(p[x], 1))
                after = jnp.where(lane == 127, side_p, roll(p[x], -1))
                v = vb[r, c, x + 2, zr] - 0.5 * (after - before)
                side_v = roll(near_side, -(8 * g + 3))
                before = jnp.where(lane == 0, side_v, roll(v, 1))
                after = jnp.where(lane == 127, side_v, roll(v, -1))
                new_p = p[x] - speed * ((u[x + 1] - u[x - 1]) + (after - before))
                if x < 0:
                    new_p = jnp.where(gx == 0, 0.0, new_p)
                if x >= BX:
                    new_p = jnp.where(gx == GX - 1, 0.0, new_p)
                if final:
                    for f, value in enumerate((new_p, u[x], v)):
                        out_ref[pl.ds(f * NZ * BX + (c * ZC + 8 * t) * BX + x, 8, stride=BX), :] = value
                else:
                    pb[r + 1, c, x + 4, zr] = new_p
                    if 0 <= x < BX:
                        vb[r + 1, c, x + 2, zr] = v
                    if packs:
                        pack = jnp.where(group == x, roll(new_p, 8 * x + 2), pack)
            if packs:
                ok[r + 1, c, zr] = pack

        for t in range(TILES):
            tile(t)

    corner_at = (0, 48, 88) if s > 0 else (0, 40, 72)
    early, late = ((-2, 12), (10, 6)) if s > 0 else ((6, 12), (0, 6))

    def begin(c, carry):
        @pl.when(at_x & (c == CHUNKS // 2))
        def _():
            for k, far in enumerate((2, 1)):
                remote(RS + k, rsp, rsr.at[k], here(-far * s, 0)).wait_recv()
            for k in range(3):
                rsum[k] = rsp[k] + rsr[0, k] + rsr[1, k]
            start(strip_messages())

        arrive(inside(0, -s), FIRST + 5 * c + 3, lp.at[c], here(0, -s))
        arrive(inside(s, -s), FIRST + 5 * c + 4, cr.at[c], here(s, -s))

        @pl.when(jnp.logical_not(at_y))
        def _():
            for f in range(3):
                corner, side, at = cr[c], lp[c, f], corner_at[f]
                if s > 0:
                    qm[c, f] = jnp.where(lane_c < 96, roll(side, -32), roll(corner, 96 - at))
                    qe[c, f] = jnp.where(
                        lane_c < 16, roll(side, -16), jnp.where(lane_c < 32, roll(corner, -16 - at), roll(side, 32))
                    )
                else:
                    qm[c, f] = jnp.where(lane_c < 32, roll(corner, -16 - at), roll(side, 32))
                    qe[c, f] = jnp.where(lane_c < 16, roll(corner, -at), roll(side, -80))

        for f in range(3):
            mine = yp[c, f]
            bm[c, f] = roll(mine, -32 * s)
            be[c, f] = roll(mine, -16 if s > 0 else -80)
        assemble(c, True)

        @pl.when(gx == GX - 1 - ex)
        def _():
            pb[0, c, pl.ds(0 if s > 0 else 20, 4)] = jnp.zeros((4, ZC, 128), F32)

        lw, rw = windows(c)
        for dest, k in ((sd, 0), (sx, 1)):
            (pl_, vl_), (pr_, vr_) = [(w[0][k], w[2][k]) for w in (lw, rw)]
            pl_, pr_ = jnp.where(ends_l, 0.0, pl_), jnp.where(ends_r, 0.0, pr_)
            put_sides(dest, c, pl_, pr_, new_v(pl_, vl_, ends_l), new_v(pr_, vr_, ends_r))
        step(0, c, *early)
        start(near_messages(c))

        @pl.when(c == 0)
        def _():
            start(first_x(2))

        @pl.when(c == 2)
        def _():
            start(first_x(3))

        return carry

    lax.fori_loop(0, CHUNKS, begin, 0)

    @pl.when(at_x)
    def _():
        base = 28 if s > 0 else 30
        other = jnp.where(gy <= last, gy + 1, gy - 1)

        def weights(block, f, j):
            lower = base + 32 * gy + ((2 * j - 3) >> 3)
            frac = ((2 * j - 3) & 7).astype(F32) * 0.125
            valid = (kk >= PCOLS * f) & (kk < PCOLS * f + PCOLS)
            return jnp.where(valid, bilinear(PCOLS * block + kk - PCOLS * f, lower, frac), 0.0)

        ne = nn & 7
        for b, block in enumerate((gy, other)):
            kr = slice(128 * b, 128 * b + 128)
            for f in range(3):
                wr[f, kr] = weights(block, f, nn).astype(jnp.bfloat16)
                wr[3 + f, kr] = weights(block, f, ne - 4).astype(jnp.bfloat16)
                wr[6 + f, kr] = weights(block, f, ne + 124).astype(jnp.bfloat16)

    @pl.when(at_x)
    def _():
        @pl.when(gy <= last)
        def _():
            remote(NB, rsum, rnb, here(0, 1)).wait_recv()

        @pl.when(gy > last)
        def _():
            remote(NB + 1, rsum, rnb, here(0, -1)).wait_recv()

        group_z = iota((NZ, 128), 1) >> 3
        rows = jnp.concatenate([jnp.concatenate([rsum[k], rnb[k]], axis=1) for k in range(3)], axis=0)
        for n in range(9):
            total = split_dot(rows, wr[n])
            slots = [total[NZ * k : NZ * k + NZ] for k in range(3)]
            strips = [sum(w * x for w, x in zip(SLOTS[r], slots) if w) for r in range(4)]
            if n < 3:
                for r in range(4):
                    for c in range(CHUNKS):
                        fr[c, n, r] = strips[r][c * ZC : (c + 1) * ZC]
            else:
                total = jnp.zeros((NZ, 128), F32)
                for r in range(4):
                    total = jnp.where(group_z == strip + r, strips[r], total)
                for c in range(CHUNKS):
                    hfr[c, n - 3] = total[c * ZC : (c + 1) * ZC]

    def complete(c, carry):
        arrive(inside(s, 0), FIRST + 5 * c, hx.at[c], here(s, 0))
        assemble(c, False)
        late_columns(c)

        @pl.when(at_x)
        def _():
            for r in range(4):
                for f, (dest, base, _, _) in enumerate(spans):
                    dest[0, c, base + strip + r] = fr[c, f, r]
            pb[0, c, pl.ds(20 if s > 0 else 2, 2)] = jnp.zeros((2, ZC, 128), F32)
            strip_rows = (group_c >= strip) & (group_c < strip + 4)
            for f in range(3):
                for dest, region in ((qm, 0 if s > 0 else 1), (bm, 1 if s > 0 else 0)):
                    dest[c, f] = jnp.where(strip_rows, hfr[c, 3 * region + f], dest[c, f])

        lw, rw = windows(c)
        speed = window_speed(c)
        lw = [(jnp.where(ends_l, 0.0, m), jnp.where(ends_l, 0.0, x)) for m, x in lw]
        rw = [(jnp.where(ends_r, 0.0, m), jnp.where(ends_r, 0.0, x)) for m, x in rw]
        pl1, vl1 = window_step(lw, ends_l, speed)
        pr1, vr1 = window_step(rw, ends_r, speed)
        put_sides(sd, c, lw[0][0], rw[0][0], vl1, vr1)
        step(0, c, *late)
        arrive(inside(s, 0), round_slot(1, c), p_rows(1, c, far_side), here(s, 0))
        vl2, vr2 = new_v(pl1, vl1, ends_l), new_v(pr1, vr1, ends_r)
        put_sides(sd, c, pl1, pr1, vl2, vr2)
        wv[c] = jnp.where(e_c < 5, roll(vl2, 1), roll(vr2, 1))
        step(1, c, 0, 2)
        step(1, c, BX - 2, 2)
        start(round_messages(2, c)[:2])
        step(1, c, 2, BX - 4)
        start(round_messages(2, c)[2:])
        return carry

    def window_speed(c):
        return sp[pl.ds(pl.multiple_of(c * ZC, ZC), ZC), :]

    lax.fori_loop(0, CHUNKS, complete, 0)

    def gather(r, c):
        receive(r, c)
        mine = ok[r, c]
        halo = jnp.where(e_c < 2, lr[r, c, 0], jnp.where(e_c < 4, lr[r, c, 1], wv[c]))
        halo = jnp.where(ends_y, 0.0, halo)
        slope = jnp.where(e_c == 4, roll(mine, 2) - roll(halo, 4), roll(halo, 2) - roll(mine, 4))
        wind = jnp.where(ends_y, 0.0, halo - 0.5 * slope)
        wv[c] = wind
        sd[c] = jnp.where(
            e_c == 0,
            roll(halo, -2),
            jnp.where(e_c == 1, halo, jnp.where(e_c == 2, roll(wind, -3), roll(wind, -1))),
        )

    def middle(c, carry):
        gather(2, c)
        step(2, c, 0, 2)
        step(2, c, BX - 2, 2)
        start(round_messages(3, c)[:2])
        step(2, c, 2, BX - 4)
        start(round_messages(3, c)[2:])
        return carry

    lax.fori_loop(0, CHUNKS, middle, 0)

    def finish(c, carry):
        gather(3, c)
        step(3, c, 0, BX)
        return carry

    lax.fori_loop(0, CHUNKS, finish, 0)

    sent(column_messages())
    sent(row_messages())
    sent(strip_messages())

    def settle(c, carry):
        sent(first_x(c))
        sent(first_y(c))
        sent(near_messages(c))
        for r in range(2, 4):
            sent(round_messages(r, c))
        return carry

    lax.fori_loop(0, CHUNKS, settle, 0)


def move(s, state, parent, stiffness, offsets):
    vmem = lambda *shape: pltpu.VMEM(shape, F32)
    sems = 14 + CHUNKS * 5 + 3 * CHUNKS * 4
    scratch = [
        vmem(3, NZ * BX, 128),
        vmem(3 * PROWS, PCOLS, NZ),
        vmem(NZ, 128),
        vmem(CHUNKS, 3, BX, ZC, 128),
        vmem(CHUNKS, 15, ZC, 128),
        vmem(CHUNKS, 15, ZC, 128),
        vmem(CHUNKS, 3, ZC, 128),
        vmem(CHUNKS, 3, ZC, 128),
        vmem(CHUNKS, ZC, 128),
        vmem(CHUNKS, ZC, 128),
        vmem(CHUNKS, 3, ZC, 128),
        vmem(CHUNKS, 3, ZC, 128),
        vmem(4, CHUNKS, 24, ZC, 128),
        vmem(4, CHUNKS, 22, ZC, 128),
        vmem(4, CHUNKS, 20, ZC, 128),
        vmem(4, CHUNKS, ZC, 128),
        vmem(4, CHUNKS, 2, ZC, 128),
        vmem(CHUNKS, 3, ZC, 128),
        vmem(CHUNKS, 3, ZC, 128),
        vmem(CHUNKS, ZC, 128),
        vmem(CHUNKS, ZC, 128),
        vmem(CHUNKS, ZC, 128),
        vmem(4, 128, 128),
        vmem(3, NZ, 128),
        vmem(2, 3, NZ, 128),
        vmem(3, NZ, 128),
        vmem(3, NZ, 128),
        pltpu.VMEM((9, 256, 128), jnp.bfloat16),
        vmem(CHUNKS, 3, 4, ZC, 128),
        vmem(CHUNKS, 6, ZC, 128),
        vmem(32, 128),
        vmem(4, 32, 128),
        pltpu.VMEM((3, 2, 512, 128), jnp.bfloat16),
        pltpu.SMEM((4,), jnp.int32),
        pltpu.SMEM((NZ,), F32),
        pltpu.SemaphoreType.DMA((CHUNKS,)),
        pltpu.SemaphoreType.DMA,
        pltpu.SemaphoreType.DMA((2,)),
        pltpu.SemaphoreType.DMA((sems,)),
        pltpu.SemaphoreType.DMA((sems,)),
    ]
    hbm = pl.BlockSpec(memory_space=pltpu.HBM)
    return pl.pallas_call(
        functools.partial(kernel, s),
        out_shape=jax.ShapeDtypeStruct((3 * NZ * BX, BY), F32),
        in_specs=[hbm, hbm, hbm, hbm],
        out_specs=pl.BlockSpec(memory_space=pltpu.VMEM),
        scratch_shapes=scratch,
        compiler_params=pltpu.CompilerParams(
            collective_id=0 if s > 0 else 1, has_side_effects=True, vmem_limit_bytes=48 * 2**20
        ),
    )(offsets, stiffness, state, parent)


def per_device(state, parent, stiffness, offsets):
    flat = state.reshape(3, NZ * BX, BY)
    cells = parent.transpose(0, 2, 3, 1).reshape(3 * PROWS, PCOLS, NZ)
    out = lax.cond(
        offsets[2] > 0, functools.partial(move, 1), functools.partial(move, -1), flat, cells, stiffness, offsets
    )
    return out.reshape(3, NZ, BX, BY)


def solution(mesh):
    return jax.shard_map(
        per_device,
        mesh=mesh,
        in_specs=(P(None, None, "gx", "gy"), P(None, None, "gx", "gy"), P(), P()),
        out_specs=P(None, None, "gx", "gy"),
        check_vma=False,
    )
```
